256 devices in a mesh: diag: 32 (over x, z_hi, core), off: 8 (over y, z_lo).
Axes of the slice: x: 4, y: 4, z: 8 (z_hi: 4, z_lo: 2; z = z_hi * 2 + z_lo), core: 2. Of those that a mesh axis runs over, the one named last changes fastest.
Arguments:
- bin_embed: bfloat16 [32, 4096], P(None, 'diag'), may hold values from -4.1875 to 4.1875
- weights: bfloat16 [2, 9, 32, 32], replicated, may hold values from -0.375 to 0.375
- biases: float32 [2, 32], replicated, may hold values from -1.8 to 1.8
- dilations: int32 [2], replicated, may hold values from 1 to 8, as said below
- cotangent: bfloat16 [32, 4096, 1024], P(None, 'diag', 'off'), may hold values from -0.29882812 to 0.29882812
Outputs:
- section_out: bfloat16 [32, 4096, 1024], P(None, 'diag', 'off')
- grad_weights: float32 [2, 9, 32, 32], replicated
- grad_biases: float32 [2, 32], replicated
- grad_embed: float32 [32, 4096], P(None, 'diag')
The draws below stay inside these ranges and needn't reach their ends.
Inputs may be any that keep to these rules, and one draw needn't show every extreme that they name: `dilations`: some layer has dilation exactly 8.
All inputs are finite; a program needn't handle non-finite values.
Results may differ from the reference program's by a relative error of at most 0.0055.
The reference program's roundings to bfloat16 on the way count: a program that leaves them out, or rounds other values in their place, can miss the bound.
Values may be sent and summed in bfloat16 or wider, within the bound.
A program may use at most 256 MiB of HBM per device.

```python
import jax
import jax.numpy as jnp
from jax import lax

CH = 32
TI = 128
DMAX = 8
LAYERS = 2
NB = 4096
KB = 1024


def draw_dilations(key, part):
    key = jax.random.fold_in(key, 7)
    key_values, key_widest = jax.random.split(key)
    values = jax.random.randint(key_values, (LAYERS,), 1, DMAX + 1)
    widest = jax.random.randint(key_widest, (), 0, LAYERS)
    return jnp.where(jnp.arange(LAYERS) == widest, DMAX, values).astype(jnp.int32)


def block_scale(own_key, dims, cuts, smallest, top_value):
    level = 1.0
    for dim, parts in cuts:
        steps = jax.random.uniform(jax.random.fold_in(jax.random.fold_in(own_key, 6), dim), (parts,), jnp.float32, smallest / len(cuts), top_value / len(cuts))
        level = level * jnp.repeat(jnp.exp(steps), dims[dim] // parts).reshape((-1,) + (1,) * (len(dims) - 1 - dim))
    return level


def scatter_about(key, extent, scale, bound, cuts=(), kind=jnp.bfloat16):
    drawn = scale * jax.random.normal(key, extent, jnp.float32)
    if cuts:
        drawn = drawn * block_scale(key, extent, cuts, -0.22, 0.18)
    return jnp.clip(drawn, -bound, bound).astype(kind)


def setup_inputs(seed: int = 0) -> dict:
    keys = jax.random.split(jax.random.key(seed), 6)
    return {
        "bin_embed": scatter_about(keys[0], (CH, NB), 0.7, 4.1875, ((1, 32),)),
        "weights": scatter_about(keys[1], (LAYERS, 9, CH, CH), (9 * CH) ** -0.5, 0.375),
        "biases": scatter_about(keys[2], (LAYERS, CH), 0.3, 1.8, (), jnp.float32),
        "dilations": draw_dilations(jax.random.fold_in(keys[5], 71), 0),
        "cotangent": scatter_about(keys[4], (CH, NB, KB), 0.05, 0.29882812, ((1, 32), (2, 8))),
    }


def band_mask(first_row, first_band, row_count, band_count, total_rows, total_band):
    row_index = first_row + lax.broadcasted_iota(jnp.int32, (row_count, band_count), 0)
    band_index = first_band + lax.broadcasted_iota(jnp.int32, (row_count, band_count), 1)
    inside = (row_index >= 0) & (row_index < total_rows) & (band_index >= 0) & (band_index < total_band)
    return inside & (row_index + band_index < total_rows)


def skew_rows(vector, row_count, band_count):
    length_all = row_count + band_count - 1
    repeated = jnp.tile(vector, (1, row_count + 1))
    flat_view = repeated[:, : row_count * (length_all + 1)]
    return flat_view.reshape(vector.shape[0], row_count, length_all + 1)[:, :, :band_count]


def unskew_sum(pair_grid):
    channels, row_count, band_count = pair_grid.shape
    length_all = row_count + band_count - 1
    padded = jnp.pad(pair_grid, ((0, 0), (0, 0), (0, length_all + 1 - band_count)))
    flat_view = padded.reshape(channels, row_count * (length_all + 1))[:, : row_count * length_all]
    return jnp.sum(flat_view.reshape(channels, row_count, length_all), axis=1, dtype=jnp.float32)


def tap_start(offset_index, direction, dilation):
    vertical = offset_index // 3 - 1
    lateral = offset_index % 3 - 1
    start_row = DMAX + direction * vertical * dilation
    start_band = 2 * DMAX + direction * (lateral - vertical) * dilation
    return start_row, start_band


def tap_sum(padded, matrices, dilation, direction):
    channels = padded.shape[0]
    row_count = padded.shape[1] - 2 * DMAX
    band_count = padded.shape[2] - 4 * DMAX
    anchor = jnp.zeros((), jnp.int32)

    def one_block(block_index):
        window = lax.dynamic_slice_in_dim(padded, block_index * TI, TI + 2 * DMAX, 1)
        summed = jnp.zeros((matrices.shape[1], TI, band_count), jnp.float32)
        for offset_index in range(9):
            start_row, start_band = tap_start(offset_index, direction, dilation)
            shifted = lax.dynamic_slice(window, (anchor, start_row, start_band), (channels, TI, band_count))
            summed = summed + jnp.einsum("oc,chw->ohw", matrices[offset_index].astype(jnp.float32), shifted.astype(jnp.float32))
        return summed

    blocks = lax.map(one_block, jnp.arange(row_count // TI, dtype=jnp.int32))
    return jnp.transpose(blocks, (1, 0, 2, 3)).reshape(blocks.shape[1], row_count, band_count)


def tap_grads(grad_pre, padded_relu, dilation):
    channels, row_count, band_count = grad_pre.shape
    anchor = jnp.zeros((), jnp.int32)

    def one_block(running, block_index):
        rows_grad = lax.dynamic_slice_in_dim(grad_pre, block_index * TI, TI, 1).astype(jnp.float32)
        window = lax.dynamic_slice_in_dim(padded_relu, block_index * TI, TI + 2 * DMAX, 1)
        tap_terms = []
        for offset_index in range(9):
            start_row, start_band = tap_start(offset_index, 1, dilation)
            shifted = lax.dynamic_slice(window, (anchor, start_row, start_band), (channels, TI, band_count))
            tap_terms.append(jnp.einsum("ohw,chw->oc", rows_grad, shifted.astype(jnp.float32)))
        return running + jnp.stack(tap_terms), None

    summed, unused = lax.scan(one_block, jnp.zeros((9, channels, channels), jnp.float32), jnp.arange(row_count // TI, dtype=jnp.int32))
    return summed


def column_sums(grad_pair):
    channels, row_count, band_count = grad_pair.shape

    def one_block(running, block_index):
        first_row = block_index * TI
        rows_grad = lax.dynamic_slice_in_dim(grad_pair, first_row, TI, 1)
        spread = unskew_sum(rows_grad)
        current = lax.dynamic_slice_in_dim(running, first_row, TI + band_count - 1, 1)
        return lax.dynamic_update_slice_in_dim(running, current + spread, first_row, 1), None

    summed, unused = lax.scan(one_block, jnp.zeros((channels, row_count + band_count), jnp.float32), jnp.arange(row_count // TI, dtype=jnp.int32))
    return summed[:, :row_count]


def pair_map(bin_embed, band_count):
    channels, row_count = bin_embed.shape
    padded = jnp.pad(bin_embed, ((0, 0), (0, band_count)))

    def one_block(block_index):
        first_row = block_index * TI
        row_part = lax.dynamic_slice_in_dim(bin_embed, first_row, TI, 1).astype(jnp.float32)
        column_part = skew_rows(lax.dynamic_slice_in_dim(padded, first_row, TI + band_count - 1, 1), TI, band_count).astype(jnp.float32)
        inside = band_mask(first_row, 0, TI, band_count, row_count, band_count)
        return jnp.where(inside, row_part[:, :, None] + column_part, 0.0).astype(jnp.bfloat16)

    blocks = lax.map(one_block, jnp.arange(row_count // TI, dtype=jnp.int32))
    return jnp.transpose(blocks, (1, 0, 2, 3)).reshape(channels, row_count, band_count)


def pad_rim(values):
    return jnp.pad(values, ((0, 0), (DMAX, DMAX), (2 * DMAX, 2 * DMAX)))


def reference(bin_embed, weights, biases, dilations, cotangent):
    channels, total_rows = bin_embed.shape
    total_band = cotangent.shape[2]
    inside_all = band_mask(0, 0, total_rows, total_band, total_rows, total_band)
    current_map = pair_map(bin_embed, total_band)
    saved_maps = []
    for layer_index in range(LAYERS):
        dilation = dilations[layer_index]
        saved_maps.append(current_map)
        conv_out = tap_sum(pad_rim(jnp.maximum(current_map, 0)), weights[layer_index], dilation, 1)
        updated = current_map.astype(jnp.float32) + conv_out + biases[layer_index][:, None, None]
        current_map = jnp.where(inside_all, updated, 0.0).astype(jnp.bfloat16)
    section_out = current_map
    upstream = cotangent
    weight_grads = [None] * LAYERS
    bias_grads = [None] * LAYERS
    for layer_index in reversed(range(LAYERS)):
        dilation = dilations[layer_index]
        grad_pre = jnp.where(inside_all, upstream, jnp.zeros((), jnp.bfloat16))
        stored = saved_maps[layer_index]
        weight_grads[layer_index] = tap_grads(grad_pre, pad_rim(jnp.maximum(stored, 0)), dilation)
        bias_grads[layer_index] = jnp.sum(grad_pre.astype(jnp.float32), axis=(1, 2))
        backward = tap_sum(pad_rim(grad_pre), jnp.transpose(weights[layer_index], (0, 2, 1)), dilation, -1)
        upstream = (grad_pre.astype(jnp.float32) + jnp.where(stored > 0, backward, 0.0)).astype(jnp.bfloat16)
    grad_pair = jnp.where(inside_all, upstream, jnp.zeros((), jnp.bfloat16))
    row_part = jnp.sum(grad_pair.astype(jnp.float32), axis=2)
    grad_embed = row_part + column_sums(grad_pair)
    return section_out, jnp.stack(weight_grads), jnp.stack(bias_grads), grad_embed
```

```python
import jax
import jax.numpy as jnp
from jax import lax
from jax.experimental import pallas as pl
from jax.experimental.pallas import tpu as pltpu
from jax.sharding import PartitionSpec as P

DMAX = 8
CH = 32
TI = 128
TK = 128
H1 = TI + 2 * DMAX
H2 = TI + 4 * DMAX
NBINS = 4096
KBAND = 1024
bf16 = jnp.bfloat16
f32 = jnp.float32
NT = (((1,), (1,)), ((), ()))


def lanes(n=1):
    return lax.broadcasted_iota(jnp.int32, (CH, 128), 1)


def in_range(amount):
    p = lanes() + amount
    return (p >= 0) & (p < 128)


def turned(x, amount):
    return pltpu.roll(x, lax.rem(256 - amount, 128), 1)


def shift_pair(a, b, amount, inside, both=True):
    ra, rb = turned(a, amount), turned(b, amount)
    out_a = jnp.where(inside, ra, rb)
    if not both:
        return out_a
    return out_a, jnp.where(inside, rb, ra)


def row_masks(row0, band0, i):
    p = lanes()
    row = row0 + i
    ka = band0 + p
    kb = band0 + jnp.where(p < 64, p + 128, p - 128)
    live = (row >= 0)
    ma = (ka < NBINS - row) & live
    mb = (kb < NBINS - row) & (kb >= 0) & (kb < KBAND) & live
    return ma, mb


def store_shifts(dst, i, a, b, amounts, insides, both=True):
    for n, s in enumerate((-2, -1, 0, 1, 2)):
        rows = slice(CH * n, CH * (n + 1))
        if s == 0:
            dst[i, rows, 0:128] = a
            if both:
                dst[i, rows, 128:256] = b
        elif both:
            sa, sb = shift_pair(a, b, amounts[n], insides[n])
            dst[i, rows, 0:128] = sa
            dst[i, rows, 128:256] = sb
        else:
            dst[i, rows, 0:128] = shift_pair(a, b, amounts[n], insides[n], False)


def taps(src, i, d, lo=0, hi=256):
    return jnp.concatenate(
        [src[i - d, 64:160, lo:hi], src[i, 32:128, lo:hi], src[i + d, 0:96, lo:hi]], axis=0
    )


def shift_tables(d):
    amounts = [s * d for s in (-2, -1, 0, 1, 2)]
    return amounts, [in_range(t) for t in amounts]


def phase_x0(row0, band0, d, ec, er, x0, s0, unroll=4):
    amounts, insides = shift_tables(d)

    def body(it, _):
        for w in range(unroll):
            j = it * unroll + w
            i = j - 2 * DMAX
            q = lax.div(i + 128, 128) - 1
            t = i - q * 128
            back = lax.rem(128 - t, 128)
            re = [pltpu.roll(ec[q + 1 + n], back, 1) for n in range(4)]
            cut = lanes() < 128 - t
            wm = jnp.where(cut, re[0], re[1])
            w0 = jnp.where(cut, re[1], re[2])
            w1 = jnp.where(cut, re[2], re[3])
            wb = jnp.where(lanes() < 64, w1, wm)
            own = pltpu.roll(er[q + 1], back, 1).astype(f32)[:, 0:1]
            ma, mb = row_masks(row0, band0, i)
            a = jnp.where(ma, own + w0.astype(f32), 0.0).astype(bf16)
            b = jnp.where(mb, own + wb.astype(f32), 0.0).astype(bf16)
            x0[j, :, 0:128] = a
            x0[j, :, 128:256] = b
            store_shifts(s0, j, jnp.maximum(a, 0), jnp.maximum(b, 0), amounts, insides)
        return 0

    lax.fori_loop(0, H2 // unroll, body, 0)


def phase_x1(row0, band0, d, dn, wf, bias, x0, s0, x1, s1, unroll=4):
    amounts, insides = shift_tables(dn)
    bias = jnp.broadcast_to(bias, (CH, 128))

    def body(it, _):
        for w in range(unroll):
            j = it * unroll + w
            jj = j + DMAX
            conv = jnp.dot(wf, taps(s0, jj, d), preferred_element_type=f32)
            ma, mb = row_masks(row0, band0, j - DMAX)
            a = x0[jj, :, 0:128].astype(f32) + conv[:, 0:128] + bias
            b = x0[jj, :, 128:256].astype(f32) + conv[:, 128:256] + bias
            a = jnp.where(ma, a, 0.0).astype(bf16)
            b = jnp.where(mb, b, 0.0).astype(bf16)
            x1[j, :, 0:128] = a
            x1[j, :, 128:256] = b
            store_shifts(s1, j, jnp.maximum(a, 0), jnp.maximum(b, 0), amounts, insides, False)
        return 0

    lax.fori_loop(0, H1 // unroll, body, 0)


def phase_x2(row0, band0, d, wf, bias, x1, s1, out, unroll=16):
    bias = jnp.broadcast_to(bias, (CH, 128))

    def body(it, _):
        rows = []
        for w in range(0, unroll, 2):
            i = it * unroll + w
            j = i + DMAX
            x = jnp.concatenate([taps(s1, j, d, 0, 128), taps(s1, j + 1, d, 0, 128)], axis=1)
            conv = jnp.dot(wf, x, preferred_element_type=f32)
            for z in range(2):
                ma, _mb = row_masks(row0, band0, i + z)
                a = x1[j + z, :, 0:128].astype(f32) + conv[:, 128 * z : 128 * z + 128] + bias
                rows.append(jnp.where(ma, a, 0.0).astype(bf16))
        out[:, pl.ds(pl.multiple_of(it * unroll, unroll), unroll), :] = jnp.swapaxes(jnp.stack(rows), 0, 1)
        return 0

    lax.fori_loop(0, TI // unroll, body, 0)


def phase_gw(h, hoff, s, soff, d, gw, gb, unroll=4):
    def body(it, carry):
        acc, accb = carry
        for w in range(0, unroll, 2):
            i = it * unroll + w
            x = jnp.concatenate(
                [taps(s, i + soff, d, 0, 128), taps(s, i + 1 + soff, d, 0, 128)], axis=1
            )
            ha = h[i + hoff, 64:96, 0:128]
            hb = h[i + hoff + 1, 64:96, 0:128]
            hh = jnp.concatenate([ha, hb], axis=1)
            acc = acc + lax.dot_general(hh, x, NT, preferred_element_type=f32)
            accb = accb + (ha.astype(f32) + hb.astype(f32))
        return acc, accb

    acc, accb = lax.fori_loop(
        0, TI // unroll, body, (jnp.zeros((CH, 9 * CH), f32), jnp.zeros((CH, 128), f32))
    )
    gw[...] = acc
    gb[...] = accb


def phase_h(row0, band0, d, a_rows, rl, rr, t1):
    amounts, insides = shift_tables(d)

    def body(it, _):
        pl_, pr_ = rl[it], rr[it]
        for w in range(4):
            j = it * 4 + w
            ma, mb = row_masks(row0, band0, j - 2 * DMAX)
            right = pltpu.roll(pl_, (128 - 32 * w) % 128, 1) if w else pl_
            left = pltpu.roll(pr_, 32 * (3 - w), 1) if w < 3 else pr_
            b = jnp.where(lanes() < 64, right, left)
            a = jnp.where(ma, a_rows[j], 0)
            b = jnp.where(mb, b, 0)
            store_shifts(t1, j, a, b, amounts, insides)
        return 0

    lax.fori_loop(0, H2 // 4, body, 0)


def phase_g1(d, dn, wb, x1, t1, t0, unroll=4):
    amounts, insides = shift_tables(dn)

    def body(it, _):
        for w in range(unroll):
            j = it * unroll + w
            jj = j + DMAX
            q = jnp.dot(wb, taps(t1, jj, d), preferred_element_type=f32)
            ab = []
            for z in range(2):
                sl = slice(128 * z, 128 * z + 128)
                h = t1[jj, 64:96, sl].astype(f32)
                gate = x1[j, :, sl].astype(f32) > 0
                ab.append((h + jnp.where(gate, q[:, sl], 0.0)).astype(bf16))
            store_shifts(t0, j, ab[0], ab[1], amounts, insides, False)
        return 0

    lax.fori_loop(0, H1 // unroll, body, 0)


def phase_g0(d, wb, x0, t0, unroll=4):
    lane = lanes()

    def body(it, carry):
        rsum, lo, hi = carry
        for w in range(0, unroll, 2):
            i = it * unroll + w
            j = i + DMAX
            x = jnp.concatenate([taps(t0, j, d, 0, 128), taps(t0, j + 1, d, 0, 128)], axis=1)
            q = jnp.dot(wb, x, preferred_element_type=f32)
            for z in range(2):
                g1 = t0[j + z, 64:96, 0:128].astype(f32)
                gate = x0[j + z + DMAX, :, 0:128].astype(f32) > 0
                gp = (g1 + jnp.where(gate, q[:, 128 * z : 128 * z + 128], 0.0)).astype(bf16)
                gf = gp.astype(f32)
                rsum = jnp.where(lane == i + z, jnp.sum(gf, axis=1, keepdims=True), rsum)
                moved = pltpu.roll(gp, i + z, 1).astype(f32)
                low = jnp.where(lane >= i + z, moved, 0.0)
                lo = lo + low
                hi = hi + (moved - low)
        return rsum, lo, hi

    zero = jnp.zeros((CH, 128), f32)
    return lax.fori_loop(0, TI // unroll, body, (zero, zero, zero))
MESH = pl.DeviceIdType.MESH
NR, NO = 32, 8


def place_weights(w, wf, wb):
    row = lax.broadcasted_iota(jnp.int32, (CH, 9 * CH), 0)
    col = lax.broadcasted_iota(jnp.int32, (CH, 9 * CH), 1)
    for layer in range(2):
        fwd = jnp.zeros((CH, 9 * CH), f32)
        bwd = jnp.zeros((CH, 9 * CH), f32)
        for t in range(9):
            spot = jnp.where(col == row + CH * t, 1.0, 0.0).astype(bf16)
            fwd = fwd + jnp.dot(w[layer, t], spot, preferred_element_type=f32)
            bwd = bwd + lax.dot_general(
                w[layer, 8 - t], spot, (((0,), (0,)), ((), ())), preferred_element_type=f32
            )
        wf[layer] = fwd.astype(bf16)
        wb[layer] = bwd.astype(bf16)


def pack_grads(layer, gw, gb, pay):
    third = jnp.concatenate([gw[:, 256:288], jnp.sum(gb[...], axis=1, keepdims=True), jnp.zeros((CH, 95), f32)], axis=1)
    for og in range(4):
        rows = slice(8 * og, 8 * og + 8)
        for lt in range(2):
            pay[layer * 8 + og * 2 + lt, 0] = gw[rows, 128 * lt : 128 * lt + 128]
    return third


def unpack_grads(res, gw_out, gb_out):
    eye = lax.broadcasted_iota(jnp.int32, (CH, CH), 0) == lax.broadcasted_iota(jnp.int32, (CH, CH), 1)
    third = jnp.concatenate([res[og, 1] for og in range(4)], axis=0)
    for layer in range(2):
        for lt in range(2):
            tile = jnp.concatenate([res[layer * 8 + og * 2 + lt, 0] for og in range(4)], axis=0)
            for n in range(4):
                gw_out[layer, 4 * lt + n] = tile[:, CH * n : CH * n + CH]
        gw_out[layer, 8] = third[:, 64 * layer : 64 * layer + CH]
        column = third[:, 64 * layer + CH : 64 * layer + CH + 1]
        gb_out[layer : layer + 1, :] = jnp.sum(jnp.where(eye, column, 0.0), axis=0, keepdims=True)


def remote(src, dst, send, recv, target):
    return pltpu.make_async_remote_copy(
        src_ref=src, dst_ref=dst, send_sem=send, recv_sem=recv, device_id=target, device_id_type=MESH
    )


def wrap(r, o):
    return (lax.rem(r + 2 * NR, NR), lax.rem(o + NO, NO))


def halo_copies(r, o, a, pl_, pr_, rl, rr, send, recv):
    last, first = slice(112, 128), slice(0, 16)
    jobs = [
        (a.at[16 + 112 : 16 + 128], a.at[0:16], 1, 0),
        (a.at[16:32], a.at[144:160], -1, 0),
        (pl_, rl.at[4:36], 0, -1),
        (pr_, rr.at[4:36], 0, 1),
        (pl_.at[28:32], rl.at[0:4], 1, -1),
        (pl_.at[0:4], rl.at[36:40], -1, -1),
        (pr_.at[28:32], rr.at[0:4], 1, 1),
        (pr_.at[0:4], rr.at[36:40], -1, 1),
    ]
    return [
        remote(src, dst, send.at[n], recv.at[n], wrap(r + dr, o + do))
        for n, (src, dst, dr, do) in enumerate(jobs)
    ]


def embed_copies(r, o, emb, ec, er, send, recv):
    other = o + 1 - 2 * lax.rem(o, 2)
    copies = [
        remote(emb, ec.at[n], send.at[n - 1], recv.at[n - 1], wrap(r - other - (n - 2), other))
        for n in range(1, 5)
    ]
    copies.append(remote(emb, er.at[0], send.at[4], recv.at[4], wrap(r + 1, o)))
    copies.append(remote(emb, er.at[2], send.at[5], recv.at[5], wrap(r - 1, o)))
    return copies


def greet_exchange(r, o, barrier):
    other = o + 1 - 2 * lax.rem(o, 2)
    targets = [wrap(r + o + n - 2, other) for n in range(1, 5)]
    targets += [wrap(r + dr, o + do) for dr in (-1, 0, 1) for do in (-1, 0, 1) if (dr, do) != (0, 0)]
    for target in targets:
        pl.semaphore_signal(barrier, inc=1, device_id=target, device_id_type=MESH)
    return len(targets)


def lay_rows(cot, a, pl_, pr_):
    lane = lanes()

    def body(it, _):
        block = jnp.swapaxes(cot[:, pl.ds(pl.multiple_of(it * 16, 16), 16), :], 0, 1)
        a[pl.ds(16 + it * 16, 16)] = block
        for n in range(4):
            left = block[4 * n]
            right = block[4 * n + 3]
            for w in range(1, 4):
                left = jnp.where(lane < 32 * w, left, pltpu.roll(block[4 * n + w], 32 * w, 1))
            for w in range(2, -1, -1):
                right = jnp.where(lane >= 32 * (w + 1), right, pltpu.roll(block[4 * n + w], 128 - 32 * (3 - w), 1))
            pl_[it * 4 + n] = left
            pr_[it * 4 + n] = right
        return 0

    lax.fori_loop(0, 8, body, 0)


def exchange_kernel(emb, cot, ec, er, a, rl, rr, pl_, pr_, esend, erecv, hsend, hrecv):
    r, o = lax.axis_index("diag"), lax.axis_index("off")
    barrier = pltpu.get_barrier_semaphore()
    count = greet_exchange(r, o, barrier)
    ec[0] = jnp.zeros((CH, 128), bf16)
    ec[5] = jnp.zeros((CH, 128), bf16)
    er[1] = emb[...]
    pl.semaphore_wait(barrier, count)
    ecopies = embed_copies(r, o, emb, ec, er, esend, erecv)
    for c in ecopies:
        c.start()
    lay_rows(cot, a, pl_, pr_)
    hcopies = halo_copies(r, o, a, pl_, pr_, rl, rr, hsend, hrecv)
    for c in hcopies:
        c.start()
    for c in ecopies + hcopies:
        c.wait()


def compute_kernel(
    dil, ec, er, a_rows, rl, rr, w, bias, out, pay, emb, x0, x1, s0, t1, s1, t0, wf, wb, gw, gb
):
    r, o = lax.axis_index("diag"), lax.axis_index("off")
    d0, d1 = dil[0], dil[1]
    row0, band0 = r * TI, o * TK
    place_weights(w, wf, wb)
    eye = lax.broadcasted_iota(jnp.int32, (CH, CH), 0) == lax.broadcasted_iota(jnp.int32, (CH, CH), 1)

    def column(layer):
        return jnp.sum(jnp.where(eye, bias[layer : layer + 1, :], 0.0), axis=1, keepdims=True)

    phase_x0(row0, band0, d0, ec, er, x0, s0, 8)
    phase_x1(row0, band0, d0, d1, wf[0], column(0), x0, s0, x1, s1, 16)
    phase_x2(row0, band0, d1, wf[1], column(1), x1, s1, out, 32)
    phase_h(row0, band0, d1, a_rows, rl, rr, t1)
    phase_gw(t1, 16, s1, 8, d1, gw, gb, 16)
    third1 = pack_grads(1, gw, gb, pay)
    phase_g1(d1, d0, wb[1], x1, t1, t0, 16)
    phase_gw(t0, 8, s0, 16, d0, gw, gb, 16)
    third0 = pack_grads(0, gw, gb, pay)
    third = third0 + pltpu.roll(third1, 64, 1)
    for n in range(16):
        pay[n, 1] = third[8 * n : 8 * n + 8] if n < 4 else jnp.zeros((8, 128), f32)
    rsum, lo, hi = phase_g0(d0, wb[0], x0, t0, 16)
    emb[0] = rsum
    emb[1] = lo
    emb[2] = hi


def reduce_kernel(
    pay, emb, gw_out, gb_out, emb_out, wr1, w2, wr2, res, er, s1, r1, s2, r2, s3, r3, es, erc, ls
):
    r, o = lax.axis_index("diag"), lax.axis_index("off")
    core, b = lax.rem(r, 2), lax.div(r, 2)
    me = o * 2 + core
    barrier = pltpu.get_barrier_semaphore()

    def peer_a(n):
        other = lax.rem(me + n, 16)
        return other, (2 * b + lax.rem(other, 2), lax.div(other, 2))

    def peer_b(n):
        other = lax.rem(b + n, 16)
        return other, (2 * other + core, o)

    def greet(target):
        pl.semaphore_signal(barrier, inc=1, device_id=target, device_id_type=MESH)

    for n in range(1, 16):
        greet(peer_a(n)[1])
        greet(peer_b(n)[1])
    for n in range(1, 8):
        oo = lax.rem(o + n, 8)
        greet(wrap(r, oo))
        greet(wrap(r - oo, oo))
        greet(wrap(r - oo - 1, oo))
    greet(wrap(r - o - 1, o))

    @pl.when(o > 0)
    def _():
        greet(wrap(r - o, o))

    pl.semaphore_wait(barrier, 30 + 21 + 1 + jnp.minimum(o, 1))

    first = [remote(pay.at[other], wr1.at[me], s1.at[n], r1.at[me], target)
             for n in range(1, 16) for other, target in [peer_a(n)]]
    for c in first:
        c.start()
    eout = []
    for n in range(0, 8):
        oo = lax.rem(o + n, 8)
        for kind, dr in ((0, 0), (1, o), (2, o + 1)):
            if n == 0 and kind < 2:
                continue
            eout.append(remote(emb.at[kind], er.at[kind * 8 + o], es.at[kind * 8 + n], erc.at[kind * 8 + o], wrap(r + dr, oo)))
    for c in eout:
        c.start()
    own = remote(emb.at[1], er.at[8 + o], es.at[8], erc.at[8 + o], wrap(r + o, o))

    @pl.when(o > 0)
    def _():
        own.start()

    local = pltpu.make_async_copy(emb.at[1], er.at[8 + o], ls)

    @pl.when(o == 0)
    def _():
        local.start()

    er[o] = emb[0]
    wr1[me] = pay[me]

    def arrived(dst, sem):
        pltpu.make_async_copy(dst, dst, sem).wait()

    def total(buf):
        acc = buf[0]
        for n in range(1, 16):
            acc = acc + buf[n]
        return acc

    for n in range(1, 16):
        other, _t = peer_a(n)
        arrived(wr1.at[other], r1.at[other])
    w2[...] = total(wr1)
    second = [remote(w2, wr2.at[b], s2.at[n], r2.at[b], target)
              for n in range(1, 16) for other, target in [peer_b(n)]]
    for c in second:
        c.start()
    wr2[b] = w2[...]
    for n in range(1, 16):
        other, _t = peer_b(n)
        arrived(wr2.at[other], r2.at[other])
    res[me] = total(wr2)
    third = [remote(res.at[me], res.at[me], s3.at[n], r3.at[me], target)
             for n in range(1, 16) for other, target in [peer_a(n)]]
    for c in third:
        c.start()

    for kind in range(3):
        for n in range(8):
            if kind == 0 and n == 0:
                continue
            oo = lax.rem(o + n, 8)
            slot = kind * 8 + oo
            if kind == 1 and n == 0:
                @pl.when(o > 0)
                def _():
                    arrived(er.at[slot], erc.at[slot])
            else:
                arrived(er.at[slot], erc.at[slot])

    @pl.when(o == 0)
    def _():
        local.wait()

    acc = er[0]
    for n in range(1, 24):
        acc = acc + er[n]
    emb_out[...] = acc
    for n in range(1, 16):
        other, _t = peer_a(n)
        arrived(res.at[other], r3.at[other])
    unpack_grads(res, gw_out, gb_out)
    for c in first + second + third + eout:
        c.wait_send()

    @pl.when(o > 0)
    def _():
        own.wait_send()


def per_device(bin_embed, weights, biases, dilations, cotangent):
    vmem = pl.BlockSpec(memory_space=pltpu.VMEM)
    smem = pl.BlockSpec(memory_space=pltpu.SMEM)
    shape = jax.ShapeDtypeStruct
    dma = pltpu.SemaphoreType.DMA
    ec, er, a, rl, rr = pl.pallas_call(
        exchange_kernel,
        out_shape=[shape((6, CH, 128), bf16), shape((3, CH, 128), bf16), shape((H2, CH, 128), bf16),
                   shape((40, CH, 128), bf16), shape((40, CH, 128), bf16)],
        in_specs=[vmem] * 2,
        out_specs=[vmem] * 5,
        scratch_shapes=[pltpu.VMEM((32, CH, 128), bf16), pltpu.VMEM((32, CH, 128), bf16),
                        dma((6,)), dma((6,)), dma((8,)), dma((8,))],
        compiler_params=pltpu.CompilerParams(collective_id=0, has_side_effects=True, vmem_limit_bytes=32 << 20),
        name="exchange",
    )(bin_embed, cotangent)
    out, pay, emb = pl.pallas_call(
        compute_kernel,
        out_shape=[shape((CH, TI, TK), bf16), shape((16, 2, 8, 128), f32), shape((3, CH, 128), f32)],
        in_specs=[smem] + [vmem] * 7,
        out_specs=[vmem] * 3,
        scratch_shapes=[pltpu.VMEM((H2, CH, 256), bf16), pltpu.VMEM((H1, CH, 256), bf16),
                        pltpu.VMEM((H2, 5 * CH, 256), bf16), pltpu.VMEM((H2, 5 * CH, 256), bf16),
                        pltpu.VMEM((H1, 5 * CH, 128), bf16), pltpu.VMEM((H1, 5 * CH, 128), bf16),
                        pltpu.VMEM((2, CH, 9 * CH), bf16), pltpu.VMEM((2, CH, 9 * CH), bf16),
                        pltpu.VMEM((CH, 9 * CH), f32), pltpu.VMEM((CH, 128), f32)],
        compiler_params=pltpu.CompilerParams(vmem_limit_bytes=63 << 20),
        name="compute",
    )(dilations, ec, er, a, rl, rr, weights, biases)
    gw, gb, ge = pl.pallas_call(
        reduce_kernel,
        out_shape=[shape((2, 9, CH, CH), f32), shape((2, CH), f32), shape((CH, TI), f32)],
        in_specs=[vmem] * 2,
        out_specs=[vmem] * 3,
        scratch_shapes=[pltpu.VMEM((16, 2, 8, 128), f32), pltpu.VMEM((2, 8, 128), f32),
                        pltpu.VMEM((16, 2, 8, 128), f32), pltpu.VMEM((16, 2, 8, 128), f32),
                        pltpu.VMEM((24, CH, 128), f32),
                        dma((16,)), dma((16,)), dma((16,)), dma((16,)), dma((16,)), dma((16,)),
                        dma((24,)), dma((24,)), dma],
        compiler_params=pltpu.CompilerParams(collective_id=1, has_side_effects=True, vmem_limit_bytes=32 << 20),
        name="reduce",
    )(pay, emb)
    return out, gw, gb, ge


def solution(mesh):
    placed = (P(None, "diag"), P(), P(), P(), P(None, "diag", "off"))
    return jax.shard_map(
        per_device,
        mesh=mesh,
        in_specs=placed,
        out_specs=(P(None, "diag", "off"), P(), P(), P(None, "diag")),
        check_vma=False,
    )
```

```python
import jax
import jax.numpy as jnp
from jax import lax
from jax.experimental import pallas as pl
from jax.experimental.pallas import tpu as pltpu
from jax.sharding import PartitionSpec as P

DMAX = 8
CH = 32
TI = 128
TK = 128
H1 = TI + 2 * DMAX
H2 = TI + 4 * DMAX
NBINS = 4096
KBAND = 1024
bf16 = jnp.bfloat16
f32 = jnp.float32
NT = (((1,), (1,)), ((), ()))


def lanes(n=1):
    return lax.broadcasted_iota(jnp.int32, (CH, 128), 1)


def in_range(amount):
    p = lanes() + amount
    return (p >= 0) & (p < 128)


def turned(x, amount):
    return pltpu.roll(x, lax.rem(256 - amount, 128), 1)


def shift_pair(a, b, amount, inside, both=True):
    ra, rb = turned(a, amount), turned(b, amount)
    out_a = jnp.where(inside, ra, rb)
    if not both:
        return out_a
    return out_a, jnp.where(inside, rb, ra)


def row_masks(row0, band0, i):
    p = lanes()
    row = row0 + i
    ka = band0 + p
    kb = band0 + jnp.where(p < 64, p + 128, p - 128)
    live = (row >= 0)
    ma = (ka < NBINS - row) & live
    mb = (kb < NBINS - row) & (kb >= 0) & (kb < KBAND) & live
    return ma, mb


def store_shifts(dst, i, a, b, amounts, insides, both=True):
    for n, s in enumerate((-2, -1, 0, 1, 2)):
        rows = slice(CH * n, CH * (n + 1))
        if s == 0:
            dst[i, rows, 0:128] = a
            if both:
                dst[i, rows, 128:256] = b
        elif both:
            sa, sb = shift_pair(a, b, amounts[n], insides[n])
            dst[i, rows, 0:128] = sa
            dst[i, rows, 128:256] = sb
        else:
            dst[i, rows, 0:128] = shift_pair(a, b, amounts[n], insides[n], False)


def taps(src, i, d, lo=0, hi=256):
    return jnp.concatenate(
        [src[i - d, 64:160, lo:hi], src[i, 32:128, lo:hi], src[i + d, 0:96, lo:hi]], axis=0
    )


def shift_tables(d):
    amounts = [s * d for s in (-2, -1, 0, 1, 2)]
    return amounts, [in_range(t) for t in amounts]


def phase_x0(row0, band0, d, ec, er, x0, s0, unroll=4):
    amounts, insides = shift_tables(d)

    def body(it, _):
        for w in range(unroll):
            j = it * unroll + w
            i = j - 2 * DMAX
            q = lax.div(i + 128, 128) - 1
            t = i - q * 128
            back = lax.rem(128 - t, 128)
            re = [pltpu.roll(ec[q + 1 + n], back, 1) for n in range(4)]
            cut = lanes() < 128 - t
            wm = jnp.where(cut, re[0], re[1])
            w0 = jnp.where(cut, re[1], re[2])
            w1 = jnp.where(cut, re[2], re[3])
            wb = jnp.where(lanes() < 64, w1, wm)
            own = pltpu.roll(er[q + 1], back, 1).astype(f32)[:, 0:1]
            ma, mb = row_masks(row0, band0, i)
            a = jnp.where(ma, own + w0.astype(f32), 0.0).astype(bf16)
            b = jnp.where(mb, own + wb.astype(f32), 0.0).astype(bf16)
            x0[j, :, 0:128] = a
            x0[j, :, 128:256] = b
            store_shifts(s0, j, jnp.maximum(a, 0), jnp.maximum(b, 0), amounts, insides)
        return 0

    lax.fori_loop(0, H2 // unroll, body, 0)


def phase_x1(row0, band0, d, dn, wf, bias, x0, s0, x1, s1, unroll=4):
    amounts, insides = shift_tables(dn)
    bias = jnp.broadcast_to(bias, (CH, 128))

    def body(it, _):
        for w in range(unroll):
            j = it * unroll + w
            jj = j + DMAX
            conv = jnp.dot(wf, taps(s0, jj, d), preferred_element_type=f32)
            ma, mb = row_masks(row0, band0, j - DMAX)
            a = x0[jj, :, 0:128].astype(f32) + conv[:, 0:128] + bias
            b = x0[jj, :, 128:256].astype(f32) + conv[:, 128:256] + bias
            a = jnp.where(ma, a, 0.0).astype(bf16)
            b = jnp.where(mb, b, 0.0).astype(bf16)
            x1[j, :, 0:128] = a
            x1[j, :, 128:256] = b
            store_shifts(s1, j, jnp.maximum(a, 0), jnp.maximum(b, 0), amounts, insides, False)
        return 0

    lax.fori_loop(0, H1 // unroll, body, 0)


def phase_x2(row0, band0, d, wf, bias, x1, s1, out, unroll=16):
    bias = jnp.broadcast_to(bias, (CH, 128))

    def body(it, _):
        rows = []
        for w in range(0, unroll, 2):
            i = it * unroll + w
            j = i + DMAX
            x = jnp.concatenate([taps(s1, j, d, 0, 128), taps(s1, j + 1, d, 0, 128)], axis=1)
            conv = jnp.dot(wf, x, preferred_element_type=f32)
            for z in range(2):
                ma, _mb = row_masks(row0, band0, i + z)
                a = x1[j + z, :, 0:128].astype(f32) + conv[:, 128 * z : 128 * z + 128] + bias
                rows.append(jnp.where(ma, a, 0.0).astype(bf16))
        out[:, pl.ds(pl.multiple_of(it * unroll, unroll), unroll), :] = jnp.swapaxes(jnp.stack(rows), 0, 1)
        return 0

    lax.fori_loop(0, TI // unroll, body, 0)


def phase_gw(h, hoff, s, soff, d, gw, gb, unroll=4):
    def body(it, carry):
        acc, accb = carry
        for w in range(0, unroll, 2):
            i = it * unroll + w
            x = jnp.concatenate(
                [taps(s, i + soff, d, 0, 128), taps(s, i + 1 + soff, d, 0, 128)], axis=1
            )
            ha = h[i + hoff, 64:96, 0:128]
            hb = h[i + hoff + 1, 64:96, 0:128]
            hh = jnp.concatenate([ha, hb], axis=1)
            acc = acc + lax.dot_general(hh, x, NT, preferred_element_type=f32)
            accb = accb + (ha.astype(f32) + hb.astype(f32))
        return acc, accb

    acc, accb = lax.fori_loop(
        0, TI // unroll, body, (jnp.zeros((CH, 9 * CH), f32), jnp.zeros((CH, 128), f32))
    )
    gw[...] = acc
    gb[...] = accb


def phase_h(row0, band0, d, a_rows, rl, rr, t1):
    amounts, insides = shift_tables(d)

    def body(it, _):
        pl_, pr_ = rl[it], rr[it]
        for w in range(4):
            j = it * 4 + w
            ma, mb = row_masks(row0, band0, j - 2 * DMAX)
            right = pltpu.roll(pl_, (128 - 32 * w) % 128, 1) if w else pl_
            left = pltpu.roll(pr_, 32 * (3 - w), 1) if w < 3 else pr_
            b = jnp.where(lanes() < 64, right, left)
            a = jnp.where(ma, a_rows[j], 0)
            b = jnp.where(mb, b, 0)
            store_shifts(t1, j, a, b, amounts, insides)
        return 0

    lax.fori_loop(0, H2 // 4, body, 0)


def phase_g1(d, dn, wb, x1, t1, t0, unroll=4):
    amounts, insides = shift_tables(dn)

    def body(it, _):
        for w in range(unroll):
            j = it * unroll + w
            jj = j + DMAX
            q = jnp.dot(wb, taps(t1, jj, d), preferred_element_type=f32)
            ab = []
            for z in range(2):
                sl = slice(128 * z, 128 * z + 128)
                h = t1[jj, 64:96, sl].astype(f32)
                gate = x1[j, :, sl].astype(f32) > 0
                ab.append((h + jnp.where(gate, q[:, sl], 0.0)).astype(bf16))
            store_shifts(t0, j, ab[0], ab[1], amounts, insides, False)
        return 0

    lax.fori_loop(0, H1 // unroll, body, 0)


def phase_g0(d, wb, x0, t0, unroll=4):
    lane = lanes()

    def body(it, carry):
        rsum, lo, hi = carry
        for w in range(0, unroll, 2):
            i = it * unroll + w
            j = i + DMAX
            x = jnp.concatenate([taps(t0, j, d, 0, 128), taps(t0, j + 1, d, 0, 128)], axis=1)
            q = jnp.dot(wb, x, preferred_element_type=f32)
            for z in range(2):
                g1 = t0[j + z, 64:96, 0:128].astype(f32)
                gate = x0[j + z + DMAX, :, 0:128].astype(f32) > 0
                gp = (g1 + jnp.where(gate, q[:, 128 * z : 128 * z + 128], 0.0)).astype(bf16)
                gf = gp.astype(f32)
                rsum = jnp.where(lane == i + z, jnp.sum(gf, axis=1, keepdims=True), rsum)
                moved = pltpu.roll(gp, i + z, 1).astype(f32)
                low = jnp.where(lane >= i + z, moved, 0.0)
                lo = lo + low
                hi = hi + (moved - low)
        return rsum, lo, hi

    zero = jnp.zeros((CH, 128), f32)
    return lax.fori_loop(0, TI // unroll, body, (zero, zero, zero))
MESH = pl.DeviceIdType.MESH
NR, NO = 32, 8


def place_weights(w, wf, wb):
    row = lax.broadcasted_iota(jnp.int32, (CH, 9 * CH), 0)
    col = lax.broadcasted_iota(jnp.int32, (CH, 9 * CH), 1)
    for layer in range(2):
        fwd = jnp.zeros((CH, 9 * CH), f32)
        bwd = jnp.zeros((CH, 9 * CH), f32)
        for t in range(9):
            spot = jnp.where(col == row + CH * t, 1.0, 0.0).astype(bf16)
            fwd = fwd + jnp.dot(w[layer, t], spot, preferred_element_type=f32)
            bwd = bwd + lax.dot_general(
                w[layer, 8 - t], spot, (((0,), (0,)), ((), ())), preferred_element_type=f32
            )
        wf[layer] = fwd.astype(bf16)
        wb[layer] = bwd.astype(bf16)


def pack_grads(layer, gw, gb, pay):
    third = jnp.concatenate([gw[:, 256:288], jnp.sum(gb[...], axis=1, keepdims=True), jnp.zeros((CH, 95), f32)], axis=1)
    for og in range(4):
        rows = slice(8 * og, 8 * og + 8)
        for lt in range(2):
            pay[layer * 8 + og * 2 + lt, 0] = gw[rows, 128 * lt : 128 * lt + 128]
    return third


def unpack_grads(res, gw_out, gb_out):
    eye = lax.broadcasted_iota(jnp.int32, (CH, CH), 0) == lax.broadcasted_iota(jnp.int32, (CH, CH), 1)
    third = jnp.concatenate([res[og, 1] for og in range(4)], axis=0)
    for layer in range(2):
        for lt in range(2):
            tile = jnp.concatenate([res[layer * 8 + og * 2 + lt, 0] for og in range(4)], axis=0)
            for n in range(4):
                gw_out[layer, 4 * lt + n] = tile[:, CH * n : CH * n + CH]
        gw_out[layer, 8] = third[:, 64 * layer : 64 * layer + CH]
        column = third[:, 64 * layer + CH : 64 * layer + CH + 1]
        gb_out[layer : layer + 1, :] = jnp.sum(jnp.where(eye, column, 0.0), axis=0, keepdims=True)


def remote(src, dst, send, recv, target):
    return pltpu.make_async_remote_copy(
        src_ref=src, dst_ref=dst, send_sem=send, recv_sem=recv, device_id=target, device_id_type=MESH
    )


def wrap(r, o):
    return (lax.rem(r + 2 * NR, NR), lax.rem(o + NO, NO))


def halo_copies(r, o, a, pl_, pr_, rl, rr, send, recv):
    last, first = slice(112, 128), slice(0, 16)
    jobs = [
        (a.at[16 + 112 : 16 + 128], a.at[0:16], 1, 0),
        (a.at[16:32], a.at[144:160], -1, 0),
        (pl_, rl.at[4:36], 0, -1),
        (pr_, rr.at[4:36], 0, 1),
        (pl_.at[28:32], rl.at[0:4], 1, -1),
        (pl_.at[0:4], rl.at[36:40], -1, -1),
        (pr_.at[28:32], rr.at[0:4], 1, 1),
        (pr_.at[0:4], rr.at[36:40], -1, 1),
    ]
    return [
        remote(src, dst, send.at[n], recv.at[n], wrap(r + dr, o + do))
        for n, (src, dst, dr, do) in enumerate(jobs)
    ]


def embed_copies(r, o, emb, ec, er, send, recv):
    other = o + 1 - 2 * lax.rem(o, 2)
    copies = [
        remote(emb, ec.at[n], send.at[n - 1], recv.at[n - 1], wrap(r - other - (n - 2), other))
        for n in range(1, 5)
    ]
    copies.append(remote(emb, er.at[0], send.at[4], recv.at[4], wrap(r + 1, o)))
    copies.append(remote(emb, er.at[2], send.at[5], recv.at[5], wrap(r - 1, o)))
    return copies


def greet_exchange(r, o, barrier):
    other = o + 1 - 2 * lax.rem(o, 2)
    targets = [wrap(r + o + n - 2, other) for n in range(1, 5)]
    targets += [wrap(r + dr, o + do) for dr in (-1, 0, 1) for do in (-1, 0, 1) if (dr, do) != (0, 0)]
    for target in targets:
        pl.semaphore_signal(barrier, inc=1, device_id=target, device_id_type=MESH)
    return len(targets)


def lay_rows(cot, a, pl_, pr_):
    lane = lanes()

    def body(it, _):
        block = jnp.swapaxes(cot[:, pl.ds(pl.multiple_of(it * 16, 16), 16), :], 0, 1)
        a[pl.ds(16 + it * 16, 16)] = block
        for n in range(4):
            left = block[4 * n]
            right = block[4 * n + 3]
            for w in range(1, 4):
                left = jnp.where(lane < 32 * w, left, pltpu.roll(block[4 * n + w], 32 * w, 1))
            for w in range(2, -1, -1):
                right = jnp.where(lane >= 32 * (w + 1), right, pltpu.roll(block[4 * n + w], 128 - 32 * (3 - w), 1))
            pl_[it * 4 + n] = left
            pr_[it * 4 + n] = right
        return 0

    lax.fori_loop(0, 8, body, 0)


def kernel(
    dil, emb, w, bias, cot_hbm, out_hbm, gw_out, gb_out, ge_out,
    cot, out, ec, er, a, rl, rr, pl_, pr_, x0, x1, s0, t1, s1, t0, wf, wb, gw, gb,
    pay, terms, wr1, w2, wr2, res, inbox,
    io, esend, erecv, hsend, hrecv, sa, ra, sb, rb, sc, rc, st, rt, local_sem,
):
    r, o = lax.axis_index("diag"), lax.axis_index("off")
    core, b = lax.rem(r, 2), lax.div(r, 2)
    me = o * 2 + core
    row0, band0 = r * TI, o * TK
    fetch = pltpu.make_async_copy(cot_hbm, cot, io.at[0])
    fetch.start()

    def peer_a(n):
        other = lax.rem(me + n, 16)
        return other, (2 * b + lax.rem(other, 2), lax.div(other, 2))

    def peer_b(n):
        other = lax.rem(b + n, 16)
        return other, (2 * other + core, o)

    barrier = pltpu.get_barrier_semaphore()

    def greet(target):
        pl.semaphore_signal(barrier, inc=1, device_id=target, device_id_type=MESH)

    count = greet_exchange(r, o, barrier)
    for n in range(1, 16):
        greet(peer_a(n)[1])
        greet(peer_b(n)[1])
    for n in range(1, 8):
        oo = lax.rem(o + n, 8)
        greet(wrap(r - oo, oo))
        greet(wrap(r - oo - 1, oo))
    greet(wrap(r - o - 1, o))

    @pl.when(o > 0)
    def _():
        greet(wrap(r - o, o))

    count = count + 30 + 14 + 1 + jnp.minimum(o, 1)
    ec[0] = jnp.zeros((CH, 128), bf16)
    ec[5] = jnp.zeros((CH, 128), bf16)
    er[1] = emb[...]
    place_weights(w, wf, wb)
    fetch.wait()
    lay_rows(cot, a, pl_, pr_)
    pl.semaphore_wait(barrier, count)
    ecopies = embed_copies(r, o, emb, ec, er, esend, erecv)
    hcopies = halo_copies(r, o, a, pl_, pr_, rl, rr, hsend, hrecv)
    for c in ecopies + hcopies:
        c.start()

    eye = lax.broadcasted_iota(jnp.int32, (CH, CH), 0) == lax.broadcasted_iota(jnp.int32, (CH, CH), 1)

    def column(layer):
        return jnp.sum(jnp.where(eye, bias[layer : layer + 1, :], 0.0), axis=1, keepdims=True)

    d0, d1 = dil[0], dil[1]
    for c in ecopies:
        c.wait_recv()
    phase_x0(row0, band0, d0, ec, er, x0, s0, 8)
    phase_x1(row0, band0, d0, d1, wf[0], column(0), x0, s0, x1, s1, 16)
    for c in hcopies:
        c.wait_recv()
    phase_h(row0, band0, d1, a, rl, rr, t1)
    phase_g1(d1, d0, wb[1], x1, t1, t0, 16)
    phase_gw(t1, 16, s1, 8, d1, gw, gb, 16)
    third1 = pack_grads(1, gw, gb, pay)
    phase_gw(t0, 8, s0, 16, d0, gw, gb, 16)
    third0 = pack_grads(0, gw, gb, pay)
    rest = third0 + pltpu.roll(third1, 64, 1)
    for n in range(16):
        pay[n, 1] = rest[8 * n : 8 * n + 8] if n < 4 else jnp.zeros((8, 128), f32)

    first = [remote(pay.at[other], wr1.at[me], sa.at[n], ra.at[me], target)
             for n in range(1, 16) for other, target in [peer_a(n)]]
    for c in first:
        c.start()

    rsum, lo, hi = phase_g0(d0, wb[0], x0, t0, 16)
    terms[0] = rsum
    terms[1] = lo
    terms[2] = hi
    eout = []
    for n in range(0, 8):
        oo = lax.rem(o + n, 8)
        for kind, dr in ((0, 0), (1, o), (2, o + 1)):
            if n == 0 and kind < 2:
                continue
            eout.append(remote(terms.at[kind], inbox.at[kind * 8 + o], st.at[kind * 8 + n], rt.at[kind * 8 + o], wrap(r + dr, oo)))
    for c in eout:
        c.start()
    own = remote(terms.at[1], inbox.at[8 + o], st.at[8], rt.at[8 + o], wrap(r + o, o))

    @pl.when(o > 0)
    def _():
        own.start()

    local = pltpu.make_async_copy(terms.at[1], inbox.at[8 + o], local_sem)

    @pl.when(o == 0)
    def _():
        local.start()

    inbox[o] = terms[0]

    def arrived(dst, sem):
        pltpu.make_async_copy(dst, dst, sem).wait()

    def total(buf):
        acc = buf[0]
        for n in range(1, 16):
            acc = acc + buf[n]
        return acc

    wr1[me] = pay[me]
    for n in range(1, 16):
        other, _t = peer_a(n)
        arrived(wr1.at[other], ra.at[other])
    w2[...] = total(wr1)
    second = [remote(w2, wr2.at[b], sb.at[n], rb.at[b], target)
              for n in range(1, 16) for other, target in [peer_b(n)]]
    for c in second:
        c.start()

    phase_x2(row0, band0, d1, wf[1], column(1), x1, s1, out, 32)
    write = pltpu.make_async_copy(out, out_hbm, io.at[1])
    write.start()

    wr2[b] = w2[...]
    for n in range(1, 16):
        other, _t = peer_b(n)
        arrived(wr2.at[other], rb.at[other])
    res[me] = total(wr2)
    third = [remote(res.at[me], res.at[me], sc.at[n], rc.at[me], target)
             for n in range(1, 16) for other, target in [peer_a(n)]]
    for c in third:
        c.start()

    for kind in range(3):
        for n in range(8):
            if kind == 0 and n == 0:
                continue
            oo = lax.rem(o + n, 8)
            slot = kind * 8 + oo
            if kind == 1 and n == 0:
                @pl.when(o > 0)
                def _():
                    arrived(inbox.at[slot], rt.at[slot])
            else:
                arrived(inbox.at[slot], rt.at[slot])

    @pl.when(o == 0)
    def _():
        local.wait()

    acc = inbox[0]
    for n in range(1, 24):
        acc = acc + inbox[n]
    ge_out[...] = acc
    for n in range(1, 16):
        other, _t = peer_a(n)
        arrived(res.at[other], rc.at[other])
    unpack_grads(res, gw_out, gb_out)
    for c in first + second + third + eout + ecopies + hcopies:
        c.wait_send()

    @pl.when(o > 0)
    def _():
        own.wait_send()

    write.wait()


def per_device(bin_embed, weights, biases, dilations, cotangent):
    vmem = pl.BlockSpec(memory_space=pltpu.VMEM)
    smem = pl.BlockSpec(memory_space=pltpu.SMEM)
    hbm = pl.BlockSpec(memory_space=pl.ANY)
    shape = jax.ShapeDtypeStruct
    dma = pltpu.SemaphoreType.DMA
    mem = pltpu.VMEM
    return pl.pallas_call(
        kernel,
        out_shape=[shape((CH, TI, TK), bf16), shape((2, 9, CH, CH), f32), shape((2, CH), f32), shape((CH, TI), f32)],
        in_specs=[smem, vmem, vmem, vmem, hbm],
        out_specs=[hbm, vmem, vmem, vmem],
        scratch_shapes=[
            mem((CH, TI, TK), bf16), mem((CH, TI, TK), bf16),
            mem((6, CH, 128), bf16), mem((3, CH, 128), bf16), mem((H2, CH, 128), bf16),
            mem((40, CH, 128), bf16), mem((40, CH, 128), bf16),
            mem((32, CH, 128), bf16), mem((32, CH, 128), bf16),
            mem((H2, CH, 256), bf16), mem((H1, CH, 256), bf16),
            mem((H2, 5 * CH, 256), bf16), mem((H2, 5 * CH, 256), bf16),
            mem((H1, 5 * CH, 128), bf16), mem((H1, 5 * CH, 128), bf16),
            mem((2, CH, 9 * CH), bf16), mem((2, CH, 9 * CH), bf16),
            mem((CH, 9 * CH), f32), mem((CH, 128), f32),
            mem((16, 2, 8, 128), f32), mem((3, CH, 128), f32),
            mem((16, 2, 8, 128), f32), mem((2, 8, 128), f32),
            mem((16, 2, 8, 128), f32), mem((16, 2, 8, 128), f32), mem((24, CH, 128), f32),
            dma((2,)), dma((6,)), dma((6,)), dma((8,)), dma((8,)),
            dma((16,)), dma((16,)), dma((16,)), dma((16,)), dma((16,)), dma((16,)),
            dma((24,)), dma((24,)), dma,
        ],
        compiler_params=pltpu.CompilerParams(collective_id=0, has_side_effects=True, vmem_limit_bytes=63 << 20),
        name="section",
    )(dilations, bin_embed, weights, biases, cotangent)


def solution(mesh):
    placed = (P(None, "diag"), P(), P(), P(), P(None, "diag", "off"))
    return jax.shard_map(
        per_device,
        mesh=mesh,
        in_specs=placed,
        out_specs=(P(None, "diag", "off"), P(), P(), P(None, "diag")),
        check_vma=False,
    )
```

```python
import jax
import jax.numpy as jnp
from jax import lax
from jax.experimental import pallas as pl
from jax.experimental.pallas import tpu as pltpu
from jax.sharding import PartitionSpec as P

DMAX = 8
CH = 32
TI = 128
TK = 128
H1 = TI + 2 * DMAX
H2 = TI + 4 * DMAX
NBINS = 4096
KBAND = 1024
bf16 = jnp.bfloat16
f32 = jnp.float32
NT = (((1,), (1,)), ((), ()))


def lanes(n=1):
    return lax.broadcasted_iota(jnp.int32, (CH, 128), 1)


def in_range(amount):
    p = lanes() + amount
    return (p >= 0) & (p < 128)


def turned(x, amount):
    return pltpu.roll(x, lax.rem(256 - amount, 128), 1)


def shift_pair(a, b, amount, inside, both=True):
    ra, rb = turned(a, amount), turned(b, amount)
    out_a = jnp.where(inside, ra, rb)
    if not both:
        return out_a
    return out_a, jnp.where(inside, rb, ra)


def row_masks(row0, band0, i):
    p = lanes()
    row = row0 + i
    ka = band0 + p
    kb = band0 + jnp.where(p < 64, p + 128, p - 128)
    live = (row >= 0)
    ma = (ka < NBINS - row) & live
    mb = (kb < NBINS - row) & (kb >= 0) & (kb < KBAND) & live
    return ma, mb


def store_shifts(dst, i, a, b, amounts, insides, both=True):
    for n, s in enumerate((-2, -1, 0, 1, 2)):
        rows = slice(CH * n, CH * (n + 1))
        if s == 0:
            dst[i, rows, 0:128] = a
            if both:
                dst[i, rows, 128:256] = b
        elif both:
            sa, sb = shift_pair(a, b, amounts[n], insides[n])
            dst[i, rows, 0:128] = sa
            dst[i, rows, 128:256] = sb
        else:
            dst[i, rows, 0:128] = shift_pair(a, b, amounts[n], insides[n], False)


def taps(src, i, d, lo=0, hi=256):
    return jnp.concatenate(
        [src[i - d, 64:160, lo:hi], src[i, 32:128, lo:hi], src[i + d, 0:96, lo:hi]], axis=0
    )


def shift_tables(d):
    amounts = [s * d for s in (-2, -1, 0, 1, 2)]
    return amounts, [in_range(t) for t in amounts]


def phase_x0(row0, band0, d, ec, er, x0, s0, unroll=4):
    amounts, insides = shift_tables(d)

    def body(it, _):
        for w in range(unroll):
            j = it * unroll + w
            i = j - 2 * DMAX
            q = lax.div(i + 128, 128) - 1
            t = i - q * 128
            back = lax.rem(128 - t, 128)
            re = [pltpu.roll(ec[q + 1 + n], back, 1) for n in range(4)]
            cut = lanes() < 128 - t
            wm = jnp.where(cut, re[0], re[1])
            w0 = jnp.where(cut, re[1], re[2])
            w1 = jnp.where(cut, re[2], re[3])
            wb = jnp.where(lanes() < 64, w1, wm)
            own = pltpu.roll(er[q + 1], back, 1).astype(f32)[:, 0:1]
            ma, mb = row_masks(row0, band0, i)
            a = jnp.where(ma, own + w0.astype(f32), 0.0).astype(bf16)
            b = jnp.where(mb, own + wb.astype(f32), 0.0).astype(bf16)
            x0[j, :, 0:128] = a
            x0[j, :, 128:256] = b
            store_shifts(s0, j, jnp.maximum(a, 0), jnp.maximum(b, 0), amounts, insides)
        return 0

    lax.fori_loop(0, H2 // unroll, body, 0)


def phase_x1(row0, band0, d, dn, wf, bias, x0, s0, x1, s1, unroll=4):
    amounts, insides = shift_tables(dn)
    bias = jnp.broadcast_to(bias, (CH, 128))

    def body(it, _):
        for w in range(unroll):
            j = it * unroll + w
            jj = j + DMAX
            conv = jnp.dot(wf, taps(s0, jj, d), preferred_element_type=f32)
            ma, mb = row_masks(row0, band0, j - DMAX)
            a = x0[jj, :, 0:128].astype(f32) + conv[:, 0:128] + bias
            b = x0[jj, :, 128:256].astype(f32) + conv[:, 128:256] + bias
            a = jnp.where(ma, a, 0.0).astype(bf16)
            b = jnp.where(mb, b, 0.0).astype(bf16)
            x1[j, :, 0:128] = a
            x1[j, :, 128:256] = b
            store_shifts(s1, j, jnp.maximum(a, 0), jnp.maximum(b, 0), amounts, insides, False)
        return 0

    lax.fori_loop(0, H1 // unroll, body, 0)


def phase_x2(row0, band0, d, wf, bias, x1, s1, out, unroll=16):
    bias = jnp.broadcast_to(bias, (CH, 128))

    def body(it, _):
        rows = []
        for w in range(0, unroll, 2):
            i = it * unroll + w
            j = i + DMAX
            x = jnp.concatenate([taps(s1, j, d, 0, 128), taps(s1, j + 1, d, 0, 128)], axis=1)
            conv = jnp.dot(wf, x, preferred_element_type=f32)
            for z in range(2):
                ma, _mb = row_masks(row0, band0, i + z)
                a = x1[j + z, :, 0:128].astype(f32) + conv[:, 128 * z : 128 * z + 128] + bias
                rows.append(jnp.where(ma, a, 0.0).astype(bf16))
        out[:, pl.ds(pl.multiple_of(it * unroll, unroll), unroll), :] = jnp.swapaxes(jnp.stack(rows), 0, 1)
        return 0

    lax.fori_loop(0, TI // unroll, body, 0)


def phase_gw(h, s, soff, d, gw, gb, unroll=16):
    def body(it, carry):
        acc, accb = carry
        for w in range(0, unroll, 2):
            i = it * unroll + w
            x = jnp.concatenate(
                [taps(s, i + soff, d, 0, 128), taps(s, i + 1 + soff, d, 0, 128)], axis=1
            )
            ha, hb = h(i), h(i + 1)
            hh = jnp.concatenate([ha, hb], axis=1)
            acc = acc + lax.dot_general(hh, x, NT, preferred_element_type=f32)
            accb = accb + (ha.astype(f32) + hb.astype(f32))
        return acc, accb

    acc, accb = lax.fori_loop(
        0, TI // unroll, body, (jnp.zeros((CH, 9 * CH), f32), jnp.zeros((CH, 128), f32))
    )
    gw[...] = acc
    gb[...] = accb


def packed(rows):
    lane = lanes()
    left, right = rows[0], rows[7]
    for w in range(1, 8):
        left = jnp.where(lane < 16 * w, left, pltpu.roll(rows[w], 16 * w, 1))
    for w in range(6, -1, -1):
        right = jnp.where(lane >= 16 * (w + 1), right, pltpu.roll(rows[w], 16 * w + 16, 1))
    return left, right


def phase_shift(row0, band0, d, rows, rl, rr, dst, unroll=2):
    lane = lanes()
    insides = [in_range(s * d) for s in (-2, -1, 1, 2)]

    def body(it, _):
        for g in range(unroll):
            group = it * unroll + g
            first = row0 + group * 8 - DMAX
            row = first + lax.div(lane, 16)
            kr = band0 + 128 + lax.rem(lane, 16)
            kl = band0 - 16 + lax.rem(lane, 16)
            right = jnp.where((row >= 0) & (kr < KBAND) & (kr < NBINS - row), rl[group], 0)
            left = jnp.where((row >= 0) & (kl >= 0) & (kl < NBINS - row), rr[group], 0)
            for w in range(8):
                j = group * 8 + w
                live = (first + w >= 0) & (band0 + lane < NBINS - (first + w))
                a = jnp.where(live, rows[j], 0)
                dst[j, 64:96, :] = a
                for n, s in enumerate((-2, -1, 1, 2)):
                    if s > 0:
                        side = pltpu.roll(right, lax.rem(256 - 16 * w - s * d, 128), 1)
                    else:
                        side = pltpu.roll(left, lax.rem(256 + 16 * (7 - w) - s * d, 128), 1)
                    m = n if s < 0 else n + 1
                    dst[j, CH * m : CH * m + CH, :] = jnp.where(
                        insides[n], pltpu.roll(a, lax.rem(256 - s * d, 128), 1), side
                    )
        return 0

    lax.fori_loop(0, H1 // 8 // unroll, body, 0)


def phase_g1(d, wb, x1, t1, ga, gpl, gpr, unroll=16):
    def body(it, _):
        rows = []
        for w in range(0, unroll, 2):
            j = it * unroll + w + DMAX
            x = jnp.concatenate([taps(t1, j, d, 0, 128), taps(t1, j + 1, d, 0, 128)], axis=1)
            q = jnp.dot(wb, x, preferred_element_type=f32)
            for z in range(2):
                h = t1[j + z, 64:96, :].astype(f32)
                gate = x1[j + z, :, 0:128].astype(f32) > 0
                g = (h + jnp.where(gate, q[:, 128 * z : 128 * z + 128], 0.0)).astype(bf16)
                ga[j + z] = g
                rows.append(g)
        for n in range(unroll // 8):
            left, right = packed(rows[8 * n : 8 * n + 8])
            gpl[it * (unroll // 8) + n] = left
            gpr[it * (unroll // 8) + n] = right
        return 0

    lax.fori_loop(0, TI // unroll, body, 0)


def phase_g0(d, wb, x0, t0, unroll=4):
    lane = lanes()

    def body(it, carry):
        rsum, lo, hi = carry
        for w in range(0, unroll, 2):
            i = it * unroll + w
            j = i + DMAX
            x = jnp.concatenate([taps(t0, j, d, 0, 128), taps(t0, j + 1, d, 0, 128)], axis=1)
            q = jnp.dot(wb, x, preferred_element_type=f32)
            for z in range(2):
                g1 = t0[j + z, 64:96, 0:128].astype(f32)
                gate = x0[j + z + DMAX, :, 0:128].astype(f32) > 0
                gp = (g1 + jnp.where(gate, q[:, 128 * z : 128 * z + 128], 0.0)).astype(bf16)
                gf = gp.astype(f32)
                rsum = jnp.where(lane == i + z, jnp.sum(gf, axis=1, keepdims=True), rsum)
                moved = pltpu.roll(gp, i + z, 1).astype(f32)
                low = jnp.where(lane >= i + z, moved, 0.0)
                lo = lo + low
                hi = hi + (moved - low)
        return rsum, lo, hi

    zero = jnp.zeros((CH, 128), f32)
    return lax.fori_loop(0, TI // unroll, body, (zero, zero, zero))
MESH = pl.DeviceIdType.MESH
NR, NO = 32, 8


def place_weights(w, wf, wb):
    row = lax.broadcasted_iota(jnp.int32, (CH, 9 * CH), 0)
    col = lax.broadcasted_iota(jnp.int32, (CH, 9 * CH), 1)
    for layer in range(2):
        fwd = jnp.zeros((CH, 9 * CH), f32)
        bwd = jnp.zeros((CH, 9 * CH), f32)
        for t in range(9):
            spot = jnp.where(col == row + CH * t, 1.0, 0.0).astype(bf16)
            fwd = fwd + jnp.dot(w[layer, t], spot, preferred_element_type=f32)
            bwd = bwd + lax.dot_general(
                w[layer, 8 - t], spot, (((0,), (0,)), ((), ())), preferred_element_type=f32
            )
        wf[layer] = fwd.astype(bf16)
        wb[layer] = bwd.astype(bf16)


def pack_grads(layer, gw, gb, pay):
    third = jnp.concatenate([gw[:, 256:288], jnp.sum(gb[...], axis=1, keepdims=True), jnp.zeros((CH, 95), f32)], axis=1)
    for og in range(4):
        rows = slice(8 * og, 8 * og + 8)
        for lt in range(2):
            pay[layer * 8 + og * 2 + lt, 0] = gw[rows, 128 * lt : 128 * lt + 128]
    return third


def unpack_grads(res, gw_out, gb_out):
    eye = lax.broadcasted_iota(jnp.int32, (CH, CH), 0) == lax.broadcasted_iota(jnp.int32, (CH, CH), 1)
    third = jnp.concatenate([res[og, 1] for og in range(4)], axis=0)
    for layer in range(2):
        for lt in range(2):
            tile = jnp.concatenate([res[layer * 8 + og * 2 + lt, 0] for og in range(4)], axis=0)
            for n in range(4):
                gw_out[layer, 4 * lt + n] = tile[:, CH * n : CH * n + CH]
        gw_out[layer, 8] = third[:, 64 * layer : 64 * layer + CH]
        column = third[:, 64 * layer + CH : 64 * layer + CH + 1]
        gb_out[layer : layer + 1, :] = jnp.sum(jnp.where(eye, column, 0.0), axis=0, keepdims=True)


def remote(src, dst, send, recv, target):
    return pltpu.make_async_remote_copy(
        src_ref=src, dst_ref=dst, send_sem=send, recv_sem=recv, device_id=target, device_id_type=MESH
    )


def wrap(r, o):
    return (lax.rem(r + 2 * NR, NR), lax.rem(o + NO, NO))


def halo_copies(r, o, a, pl_, pr_, rl, rr, send, recv):
    jobs = [
        (pl_, rl.at[1:17], 0, -1),
        (pr_, rr.at[1:17], 0, 1),
        (a.at[128:136], a.at[0:8], 1, 0),
        (a.at[8:16], a.at[136:144], -1, 0),
        (pl_.at[15:16], rl.at[0:1], 1, -1),
        (pl_.at[0:1], rl.at[17:18], -1, -1),
        (pr_.at[15:16], rr.at[0:1], 1, 1),
        (pr_.at[0:1], rr.at[17:18], -1, 1),
    ]
    return [
        remote(src, dst, send.at[n], recv.at[n], wrap(r + dr, o + do))
        for n, (src, dst, dr, do) in enumerate(jobs)
    ]


def embed_copies(r, o, emb, ec, er, send, recv):
    other = o + 1 - 2 * lax.rem(o, 2)
    copies = [
        remote(emb, ec.at[n], send.at[n - 1], recv.at[n - 1], wrap(r - other - (n - 2), other))
        for n in range(1, 5)
    ]
    copies.append(remote(emb, er.at[0], send.at[4], recv.at[4], wrap(r + 1, o)))
    copies.append(remote(emb, er.at[2], send.at[5], recv.at[5], wrap(r - 1, o)))
    return copies


def greet_exchange(r, o, barrier):
    other = o + 1 - 2 * lax.rem(o, 2)
    targets = [wrap(r + o + n - 2, other) for n in range(1, 5)]
    targets += [wrap(r + dr, o + do) for dr in (-1, 0, 1) for do in (-1, 0, 1) if (dr, do) != (0, 0)]
    for target in targets:
        pl.semaphore_signal(barrier, inc=1, device_id=target, device_id_type=MESH)
    return len(targets)


def lay_rows(cot, a, pl_, pr_):
    def body(it, _):
        block = jnp.swapaxes(cot[:, pl.ds(pl.multiple_of(it * 16, 16), 16), :], 0, 1)
        a[pl.ds(DMAX + it * 16, 16)] = block
        for n in range(2):
            left, right = packed([block[8 * n + w] for w in range(8)])
            pl_[it * 2 + n] = left
            pr_[it * 2 + n] = right
        return 0

    lax.fori_loop(0, 8, body, 0)


def kernel(
    dil, emb, w, bias, cot_hbm, out_hbm, res, ge,
    cot, out, ec, er, a, rl, rr, pl_, pr_, ga, grl, grr, gpl, gpr, x0, x1, s0, t1, s1, t0, wf, wb, gw, gb,
    pay, terms, wr1, w2, wr2, inbox,
    io, esend, erecv, hsend, hrecv, gsend, grecv, sa, ra, sb, rb, sc, rc, st, rt, su, ru, local_sem,
):
    r, o = lax.axis_index("diag"), lax.axis_index("off")
    core, b = lax.rem(r, 2), lax.div(r, 2)
    me = o * 2 + core
    row0, band0 = r * TI, o * TK
    fetch = pltpu.make_async_copy(cot_hbm, cot, io.at[0])
    fetch.start()

    def peer_a(n):
        other = lax.rem(me + n, 16)
        return other, (2 * b + lax.rem(other, 2), lax.div(other, 2))

    def peer_b(n):
        other = lax.rem(b + n, 16)
        return other, (2 * other + core, o)

    barrier = pltpu.get_barrier_semaphore()

    def greet(target):
        pl.semaphore_signal(barrier, inc=1, device_id=target, device_id_type=MESH)

    count = greet_exchange(r, o, barrier)
    for n in range(1, 16):
        greet(peer_a(n)[1])
        greet(peer_b(n)[1])
    for n in range(1, 8):
        oo = lax.rem(o + n, 8)
        greet(wrap(r - oo, oo))
        greet(wrap(r - oo - 1, oo))
    greet(wrap(r - o - 1, o))

    @pl.when(o > 0)
    def _():
        greet(wrap(r - o, o))

    count = count + 30 + 14 + 1 + jnp.minimum(o, 1)
    ec[0] = jnp.zeros((CH, 128), bf16)
    ec[5] = jnp.zeros((CH, 128), bf16)
    er[1] = emb[...]
    place_weights(w, wf, wb)
    fetch.wait()
    lay_rows(cot, a, pl_, pr_)
    pl.semaphore_wait(barrier, count)
    ecopies = embed_copies(r, o, emb, ec, er, esend, erecv)
    hcopies = halo_copies(r, o, a, pl_, pr_, rl, rr, hsend, hrecv)
    for c in ecopies + hcopies:
        c.start()

    eye = lax.broadcasted_iota(jnp.int32, (CH, CH), 0) == lax.broadcasted_iota(jnp.int32, (CH, CH), 1)

    def column(layer):
        return jnp.sum(jnp.where(eye, bias[layer : layer + 1, :], 0.0), axis=1, keepdims=True)

    d0, d1 = dil[0], dil[1]
    for c in ecopies:
        c.wait_recv()
    phase_x0(row0, band0, d0, ec, er, x0, s0, 8)
    phase_x1(row0, band0, d0, d1, wf[0], column(0), x0, s0, x1, s1, 16)
    for c in hcopies:
        c.wait_recv()
    phase_shift(row0, band0, d1, a, rl, rr, t1)
    phase_g1(d1, wb[1], x1, t1, ga, gpl, gpr)
    gcopies = halo_copies(r, o, ga, gpl, gpr, grl, grr, gsend, grecv)
    for c in gcopies:
        c.start()
    phase_gw(lambda i: t1[i + DMAX, 64:96, :], s1, DMAX, d1, gw, gb)
    third1 = pack_grads(1, gw, gb, pay)
    phase_gw(lambda i: ga[i + DMAX], s0, 2 * DMAX, d0, gw, gb)
    third0 = pack_grads(0, gw, gb, pay)
    rest = third0 + pltpu.roll(third1, 64, 1)
    for n in range(16):
        pay[n, 1] = rest[8 * n : 8 * n + 8] if n < 4 else jnp.zeros((8, 128), f32)

    first = [remote(pay.at[other], wr1.at[me], sa.at[n], ra.at[me], target)
             for n in range(1, 16) for other, target in [peer_a(n)]]
    for c in first:
        c.start()

    for c in gcopies:
        c.wait_recv()
    phase_shift(row0, band0, d0, ga, grl, grr, t0)
    rsum, lo, hi = phase_g0(d0, wb[0], x0, t0, 16)
    for n in range(8):
        rows = slice(4 * n, 4 * n + 4)
        terms[0, n] = rsum[rows]
        terms[1, n] = lo[rows]
        terms[2, n] = hi[rows]
    eout = []
    for n in range(0, 8):
        oo = lax.rem(o + n, 8)
        for kind, dr in ((0, 0), (1, o), (2, o + 1)):
            if n == 0 and kind < 2:
                continue
            eout.append(remote(terms.at[kind, oo], inbox.at[kind * 8 + o], st.at[kind * 8 + n], rt.at[kind * 8 + o], wrap(r + dr, oo)))
    for c in eout:
        c.start()
    own = remote(terms.at[1, o], inbox.at[8 + o], st.at[8], rt.at[8 + o], wrap(r + o, o))

    @pl.when(o > 0)
    def _():
        own.start()

    local = pltpu.make_async_copy(terms.at[1, o], inbox.at[8 + o], local_sem)

    @pl.when(o == 0)
    def _():
        local.start()

    inbox[o] = terms[0, o]

    def arrived(dst, sem):
        pltpu.make_async_copy(dst, dst, sem).wait()

    def total(buf):
        acc = buf[0]
        for n in range(1, 16):
            acc = acc + buf[n]
        return acc

    wr1[me] = pay[me]
    for n in range(1, 16):
        other, _t = peer_a(n)
        arrived(wr1.at[other], ra.at[other])
    w2[...] = total(wr1)
    second = [remote(w2, wr2.at[b], sb.at[n], rb.at[b], target)
              for n in range(1, 16) for other, target in [peer_b(n)]]
    for c in second:
        c.start()

    phase_x2(row0, band0, d1, wf[1], column(1), x1, s1, out, 32)
    write = pltpu.make_async_copy(out, out_hbm, io.at[1])
    write.start()

    for kind in range(3):
        for n in range(8):
            if kind == 0 and n == 0:
                continue
            oo = lax.rem(o + n, 8)
            slot = kind * 8 + oo
            if kind == 1 and n == 0:
                @pl.when(o > 0)
                def _():
                    arrived(inbox.at[slot], rt.at[slot])
            else:
                arrived(inbox.at[slot], rt.at[slot])

    @pl.when(o == 0)
    def _():
        local.wait()

    acc = inbox[0]
    for n in range(1, 24):
        acc = acc + inbox[n]
    ge[o] = acc
    eall = [remote(ge.at[o], ge.at[o], su.at[n], ru.at[o], wrap(r, o + n)) for n in range(1, 8)]
    for c in eall:
        c.start()

    wr2[b] = w2[...]
    for n in range(1, 16):
        other, _t = peer_b(n)
        arrived(wr2.at[other], rb.at[other])
    res[me] = total(wr2)
    third = [remote(res.at[me], res.at[me], sc.at[n], rc.at[me], target)
             for n in range(1, 16) for other, target in [peer_a(n)]]
    for c in third:
        c.start()
    for n in range(1, 8):
        oo = lax.rem(o + n, 8)
        arrived(ge.at[oo], ru.at[oo])
    for n in range(1, 16):
        other, _t = peer_a(n)
        arrived(res.at[other], rc.at[other])
    for c in first + second + third + eout + eall + ecopies + hcopies + gcopies:
        c.wait_send()

    @pl.when(o > 0)
    def _():
        own.wait_send()

    write.wait()


def finish(section, res, ge, out, gw_out, gb_out, ge_out, sem):
    move = pltpu.make_async_copy(section, out, sem)
    move.start()
    unpack_grads(res, gw_out, gb_out)
    for n in range(8):
        ge_out[4 * n : 4 * n + 4, :] = ge[n]
    move.wait()


def per_device(bin_embed, weights, biases, dilations, cotangent):
    vmem = pl.BlockSpec(memory_space=pltpu.VMEM)
    smem = pl.BlockSpec(memory_space=pltpu.SMEM)
    hbm = pl.BlockSpec(memory_space=pl.ANY)
    shape = jax.ShapeDtypeStruct
    dma = pltpu.SemaphoreType.DMA
    mem = pltpu.VMEM
    halo = [mem((H1, CH, 128), bf16), mem((18, CH, 128), bf16), mem((18, CH, 128), bf16),
            mem((16, CH, 128), bf16), mem((16, CH, 128), bf16)]
    section, res, ge = pl.pallas_call(
        kernel,
        out_shape=[shape((CH, TI, TK), bf16), shape((16, 2, 8, 128), f32), shape((8, 4, 128), f32)],
        in_specs=[smem, vmem, vmem, vmem, hbm],
        out_specs=[hbm, vmem, vmem],
        scratch_shapes=[
            mem((CH, TI, TK), bf16), mem((CH, TI, TK), bf16),
            mem((6, CH, 128), bf16), mem((3, CH, 128), bf16), *halo, *halo,
            mem((H2, CH, 256), bf16), mem((H1, CH, 256), bf16),
            mem((H2, 5 * CH, 256), bf16), mem((H1, 5 * CH, 128), bf16),
            mem((H1, 5 * CH, 128), bf16), mem((H1, 5 * CH, 128), bf16),
            mem((2, CH, 9 * CH), bf16), mem((2, CH, 9 * CH), bf16),
            mem((CH, 9 * CH), f32), mem((CH, 128), f32),
            mem((16, 2, 8, 128), f32), mem((3, 8, 4, 128), f32),
            mem((16, 2, 8, 128), f32), mem((2, 8, 128), f32),
            mem((16, 2, 8, 128), f32), mem((24, 4, 128), f32),
            dma((2,)), dma((6,)), dma((6,)), dma((8,)), dma((8,)), dma((8,)), dma((8,)),
            dma((16,)), dma((16,)), dma((16,)), dma((16,)), dma((16,)), dma((16,)),
            dma((24,)), dma((24,)), dma((8,)), dma((8,)), dma,
        ],
        compiler_params=pltpu.CompilerParams(collective_id=0, has_side_effects=True, vmem_limit_bytes=60 << 20),
        name="section",
    )(dilations, bin_embed, weights, biases, cotangent)
    return pl.pallas_call(
        finish,
        out_shape=[shape((CH, TI, TK), bf16), shape((2, 9, CH, CH), f32), shape((2, CH), f32), shape((CH, TI), f32)],
        in_specs=[hbm, vmem, vmem],
        out_specs=[hbm, vmem, vmem, vmem],
        scratch_shapes=[dma],
        name="finish",
    )(section, res, ge)


def solution(mesh):
    placed = (P(None, "diag"), P(), P(), P(), P(None, "diag", "off"))
    return jax.shard_map(
        per_device,
        mesh=mesh,
        in_specs=placed,
        out_specs=(P(None, "diag", "off"), P(), P(), P(None, "diag")),
        check_vma=False,
    )
```

```python
import jax
import jax.numpy as jnp
from jax import lax
from jax.experimental import pallas as pl
from jax.experimental.pallas import tpu as pltpu
from jax.sharding import PartitionSpec as P

DMAX = 8
CH = 32
TI = 128
TK = 128
H1 = TI + 2 * DMAX
H2 = TI + 4 * DMAX
NBINS = 4096
KBAND = 1024
bf16 = jnp.bfloat16
f32 = jnp.float32
NT = (((1,), (1,)), ((), ()))


def lanes(n=1):
    return lax.broadcasted_iota(jnp.int32, (CH, 128), 1)


def level(value):
    return jnp.full((CH, 128), value.astype(f32)).astype(bf16)


def in_range(s, d):
    p = lanes().astype(bf16)
    return p < level(128 - s * d) if s > 0 else p >= level(-s * d)


def turned(x, amount):
    return pltpu.roll(x, lax.rem(256 - amount, 128), 1)


def shift_pair(a, b, amount, inside, both=True):
    ra, rb = turned(a, amount), turned(b, amount)
    out_a = jnp.where(inside, ra, rb)
    if not both:
        return out_a
    return out_a, jnp.where(inside, rb, ra)


def row_masks(row0, band0, i):
    p = lanes()
    row = row0 + i
    ka = band0 + p
    kb = band0 + jnp.where(p < 64, p + 128, p - 128)
    live = (row >= 0)
    ma = (ka < NBINS - row) & live
    mb = (kb < NBINS - row) & (kb >= 0) & (kb < KBAND) & live
    return ma, mb


def store_shifts(dst, i, a, b, amounts, insides, both=True):
    for n, s in enumerate((-2, -1, 0, 1, 2)):
        rows = slice(CH * n, CH * (n + 1))
        if s == 0:
            dst[i, rows, 0:128] = a
            if both:
                dst[i, rows, 128:256] = b
        elif both:
            sa, sb = shift_pair(a, b, amounts[n], insides[n])
            dst[i, rows, 0:128] = sa
            dst[i, rows, 128:256] = sb
        else:
            dst[i, rows, 0:128] = shift_pair(a, b, amounts[n], insides[n], False)


def taps(src, i, d, lo=0, hi=256):
    return jnp.concatenate(
        [src[i - d, 64:160, lo:hi], src[i, 32:128, lo:hi], src[i + d, 0:96, lo:hi]], axis=0
    )


def shift_tables(d):
    amounts = [s * d for s in (-2, -1, 0, 1, 2)]
    return amounts, [in_range(s, d) for s in (-2, -1, 0, 1, 2)]


LOW = -1e38


def bounded_blocks(r, o, ec, er):
    for n in range(1, 5):
        ec[n] = jnp.where(r + o + n - 2 < NBINS // TI, ec[n], LOW)
    for n in (0, 2):
        ec_row = r + n - 1
        er[n] = jnp.where((ec_row >= 0) & (ec_row < NBINS // TI), er[n], LOW)


def lane_caps(band0, d, caps):
    p = lanes()
    for n, s in enumerate((-2, -1, 0, 1, 2)):
        for half in range(2):
            k = band0 + s * d + (jnp.where(p < 64, p + 128, p - 128) if half else p)
            caps[2 * n + half] = jnp.where((k >= 0) & (k < KBAND), 3e38, 0.0).astype(bf16)


def phase_windows(ec, win, unroll=32):
    u = lanes()
    ub = u.astype(bf16)

    def body(it, _):
        m0 = it * unroll - 4 * DMAX
        q = lax.div(m0 + 128, 128) - 1
        t0 = m0 - 128 * q
        prev, here, after, later = (ec[q + 1 + n] for n in range(4))
        high = jnp.where((u >= 64) & (t0 < 32), prev, after)
        low = jnp.where((u < 64) & (t0 >= 96), later, here)
        for w in range(unroll):
            t = t0 + w
            beyond = ub >= level(t)
            back = lax.rem(128 - t, 128)
            win[it * unroll + w, :, 0:128] = pltpu.roll(jnp.where(beyond, here, after), back, 1)
            win[it * unroll + w, :, 128:256] = pltpu.roll(jnp.where(beyond, high, low), back, 1)
        return 0

    lax.fori_loop(0, (H2 + 4 * DMAX) // unroll, body, 0)


def phase_x0(d, er, win, caps, x0, s0, unroll=16):
    def body(it, _):
        i0 = it * unroll - 2 * DMAX
        q = lax.div(i0 + 128, 128) - 1
        block = pltpu.roll(er[q + 1], lax.rem(256 - (i0 - 128 * q), 128), 1)
        for w in range(unroll):
            j = it * unroll + w
            own = jnp.broadcast_to(block[:, w : w + 1], (CH, 128))
            for n, s in enumerate((-2, -1, 0, 1, 2)):
                for half in range(2):
                    at = slice(128 * half, 128 * half + 128)
                    v = own + win[j + 2 * DMAX + s * d, :, at]
                    if s == 0:
                        x0[j, :, at] = v
                    s0[j, CH * n : CH * n + CH, at] = jnp.minimum(jnp.maximum(v, 0), caps[2 * n + half])
        return 0

    lax.fori_loop(0, H2 // unroll, body, 0)


def phase_x1(row0, band0, d, dn, wf, bias, x0, s0, x1, s1, unroll=4):
    amounts, insides = shift_tables(dn)
    bias = jnp.broadcast_to(bias, (CH, 128))

    def body(it, _):
        for w in range(unroll):
            j = it * unroll + w
            jj = j + DMAX
            conv = jnp.dot(wf, taps(s0, jj, d), preferred_element_type=f32)
            ma, mb = row_masks(row0, band0, j - DMAX)
            a = x0[jj, :, 0:128].astype(f32) + conv[:, 0:128] + bias
            b = x0[jj, :, 128:256].astype(f32) + conv[:, 128:256] + bias
            a = jnp.where(ma, a, 0.0).astype(bf16)
            b = jnp.where(mb, b, 0.0).astype(bf16)
            x1[j, :, 0:128] = a
            x1[j, :, 128:256] = b
            store_shifts(s1, j, jnp.maximum(a, 0), jnp.maximum(b, 0), amounts, insides, False)
        return 0

    lax.fori_loop(0, H1 // unroll, body, 0)


def phase_x2(row0, band0, d, wf, bias, x1, s1, out, unroll=16):
    bias = jnp.broadcast_to(bias, (CH, 128))

    def body(it, _):
        rows = []
        for w in range(0, unroll, 2):
            i = it * unroll + w
            j = i + DMAX
            x = jnp.concatenate([taps(s1, j, d, 0, 128), taps(s1, j + 1, d, 0, 128)], axis=1)
            conv = jnp.dot(wf, x, preferred_element_type=f32)
            for z in range(2):
                ma, _mb = row_masks(row0, band0, i + z)
                a = x1[j + z, :, 0:128].astype(f32) + conv[:, 128 * z : 128 * z + 128] + bias
                rows.append(jnp.where(ma, a, 0.0).astype(bf16))
        out[:, pl.ds(pl.multiple_of(it * unroll, unroll), unroll), :] = jnp.swapaxes(jnp.stack(rows), 0, 1)
        return 0

    lax.fori_loop(0, TI // unroll, body, 0)


def phase_gw(h, s, soff, d, gw, gb, unroll=64):
    def body(it, carry):
        acc, accb = carry
        for w in range(0, unroll, 2):
            i = it * unroll + w
            x = jnp.concatenate(
                [taps(s, i + soff, d, 0, 128), taps(s, i + 1 + soff, d, 0, 128)], axis=1
            )
            ha, hb = h(i), h(i + 1)
            hh = jnp.concatenate([ha, hb], axis=1)
            acc = acc + lax.dot_general(hh, x, NT, preferred_element_type=f32)
            accb = accb + (ha.astype(f32) + hb.astype(f32))
        return acc, accb

    acc, accb = lax.fori_loop(
        0, TI // unroll, body, (jnp.zeros((CH, 9 * CH), f32), jnp.zeros((CH, 128), f32))
    )
    gw[...] = acc
    gb[...] = accb


def packed(rows):
    lane = lanes()
    left, right = rows[0], rows[7]
    for w in range(1, 8):
        left = jnp.where(lane < 16 * w, left, pltpu.roll(rows[w], 16 * w, 1))
    for w in range(6, -1, -1):
        right = jnp.where(lane >= 16 * (w + 1), right, pltpu.roll(rows[w], 16 * w + 16, 1))
    return left, right


def phase_shift(row0, band0, d, rows, rl, rr, dst, unroll=3):
    lane = lanes()
    insides = [in_range(s, d) for s in (-2, -1, 1, 2)]

    def body(it, _):
        for g in range(unroll):
            group = it * unroll + g
            first = row0 + group * 8 - DMAX
            row = first + lax.div(lane, 16)
            kr = band0 + 128 + lax.rem(lane, 16)
            kl = band0 - 16 + lax.rem(lane, 16)
            right = jnp.where((row >= 0) & (kr < KBAND) & (kr < NBINS - row), rl[group], 0)
            left = jnp.where((row >= 0) & (kl >= 0) & (kl < NBINS - row), rr[group], 0)
            for w in range(8):
                j = group * 8 + w
                live = (first + w >= 0) & (band0 + lane < NBINS - (first + w))
                a = jnp.where(live, rows[j], 0)
                dst[j, 64:96, :] = a
                for n, s in enumerate((-2, -1, 1, 2)):
                    if s > 0:
                        side = pltpu.roll(right, lax.rem(256 - 16 * w - s * d, 128), 1)
                    else:
                        side = pltpu.roll(left, lax.rem(256 + 16 * (7 - w) - s * d, 128), 1)
                    m = n if s < 0 else n + 1
                    dst[j, CH * m : CH * m + CH, :] = jnp.where(
                        insides[n], pltpu.roll(a, lax.rem(256 - s * d, 128), 1), side
                    )
        return 0

    lax.fori_loop(0, H1 // 8 // unroll, body, 0)


def phase_g1(d, wb, x1, t1, ga, gpl, gpr, unroll=64):
    def body(it, _):
        rows = []
        for w in range(0, unroll, 2):
            j = it * unroll + w + DMAX
            x = jnp.concatenate([taps(t1, j, d, 0, 128), taps(t1, j + 1, d, 0, 128)], axis=1)
            q = jnp.dot(wb, x, preferred_element_type=f32)
            for z in range(2):
                h = t1[j + z, 64:96, :].astype(f32)
                gate = x1[j + z, :, 0:128].astype(f32) > 0
                g = (h + jnp.where(gate, q[:, 128 * z : 128 * z + 128], 0.0)).astype(bf16)
                ga[j + z] = g
                rows.append(g)
        for n in range(unroll // 8):
            left, right = packed(rows[8 * n : 8 * n + 8])
            gpl[it * (unroll // 8) + n] = left
            gpr[it * (unroll // 8) + n] = right
        return 0

    lax.fori_loop(0, TI // unroll, body, 0)


def phase_g0(d, wb, s0, t0, unroll=32):
    lane = lanes()
    ones = jnp.ones((128, 128), bf16)

    def body(it, carry):
        rsum, lo, hi = carry
        rows = []
        for w in range(0, unroll, 2):
            i = it * unroll + w
            j = i + DMAX
            x = jnp.concatenate([taps(t0, j, d, 0, 128), taps(t0, j + 1, d, 0, 128)], axis=1)
            q = jnp.dot(wb, x, preferred_element_type=f32)
            for z in range(2):
                g1 = t0[j + z, 64:96, 0:128].astype(f32)
                gate = s0[j + z + DMAX, 64:96, 0:128].astype(f32) > 0
                gp = (g1 + jnp.where(gate, q[:, 128 * z : 128 * z + 128], 0.0)).astype(bf16)
                rows.append(gp)
                moved = pltpu.roll(gp, i + z, 1).astype(f32)
                low = jnp.where(lane >= i + z, moved, 0.0)
                lo = lo + low
                hi = hi + (moved - low)
        sums = jnp.dot(jnp.concatenate(rows, axis=0), ones, preferred_element_type=f32)
        for w in range(unroll):
            rsum = jnp.where(lane == it * unroll + w, sums[CH * w : CH * w + CH], rsum)
        return rsum, lo, hi

    zero = jnp.zeros((CH, 128), f32)
    return lax.fori_loop(0, TI // unroll, body, (zero, zero, zero))
MESH = pl.DeviceIdType.MESH
NR, NO = 32, 8


def place_weights(w, wf, wb):
    row = lax.broadcasted_iota(jnp.int32, (CH, 9 * CH), 0)
    col = lax.broadcasted_iota(jnp.int32, (CH, 9 * CH), 1)
    for layer in range(2):
        fwd = jnp.zeros((CH, 9 * CH), f32)
        bwd = jnp.zeros((CH, 9 * CH), f32)
        for t in range(9):
            spot = jnp.where(col == row + CH * t, 1.0, 0.0).astype(bf16)
            fwd = fwd + jnp.dot(w[layer, t], spot, preferred_element_type=f32)
            bwd = bwd + lax.dot_general(
                w[layer, 8 - t], spot, (((0,), (0,)), ((), ())), preferred_element_type=f32
            )
        wf[layer] = fwd.astype(bf16)
        wb[layer] = bwd.astype(bf16)


def pack_grads(layer, gw, gb, pay):
    third = jnp.concatenate([gw[:, 256:288], jnp.sum(gb[...], axis=1, keepdims=True), jnp.zeros((CH, 95), f32)], axis=1)
    for og in range(4):
        rows = slice(8 * og, 8 * og + 8)
        for lt in range(2):
            pay[layer * 8 + og * 2 + lt, 0] = gw[rows, 128 * lt : 128 * lt + 128]
    return third


def unpack_grads(res, gw_out, gb_out):
    eye = lax.broadcasted_iota(jnp.int32, (CH, CH), 0) == lax.broadcasted_iota(jnp.int32, (CH, CH), 1)
    third = jnp.concatenate([res[og, 1] for og in range(4)], axis=0)
    for layer in range(2):
        for lt in range(2):
            tile = jnp.concatenate([res[layer * 8 + og * 2 + lt, 0] for og in range(4)], axis=0)
            for n in range(4):
                gw_out[layer, 4 * lt + n] = tile[:, CH * n : CH * n + CH]
        gw_out[layer, 8] = third[:, 64 * layer : 64 * layer + CH]
        column = third[:, 64 * layer + CH : 64 * layer + CH + 1]
        gb_out[layer : layer + 1, :] = jnp.sum(jnp.where(eye, column, 0.0), axis=0, keepdims=True)


def remote(src, dst, send, recv, target):
    return pltpu.make_async_remote_copy(
        src_ref=src, dst_ref=dst, send_sem=send, recv_sem=recv, device_id=target, device_id_type=MESH
    )


def wrap(r, o):
    return (lax.rem(r + 2 * NR, NR), lax.rem(o + NO, NO))


def halo_copies(r, o, a, pl_, pr_, rl, rr, send, recv):
    jobs = [
        (pl_, rl.at[1:17], 0, -1),
        (pr_, rr.at[1:17], 0, 1),
        (a.at[128:136], a.at[0:8], 1, 0),
        (a.at[8:16], a.at[136:144], -1, 0),
        (pl_.at[15:16], rl.at[0:1], 1, -1),
        (pl_.at[0:1], rl.at[17:18], -1, -1),
        (pr_.at[15:16], rr.at[0:1], 1, 1),
        (pr_.at[0:1], rr.at[17:18], -1, 1),
    ]
    return [
        remote(src, dst, send.at[n], recv.at[n], wrap(r + dr, o + do))
        for n, (src, dst, dr, do) in enumerate(jobs)
    ]


def embed_copies(r, o, emb, ec, er, send, recv):
    other = o + 1 - 2 * lax.rem(o, 2)
    copies = [
        remote(emb, ec.at[n], send.at[n - 1], recv.at[n - 1], wrap(r - other - (n - 2), other))
        for n in range(1, 5)
    ]
    copies.append(remote(emb, er.at[0], send.at[4], recv.at[4], wrap(r + 1, o)))
    copies.append(remote(emb, er.at[2], send.at[5], recv.at[5], wrap(r - 1, o)))
    return copies


def greet_exchange(r, o, barrier):
    other = o + 1 - 2 * lax.rem(o, 2)
    targets = [wrap(r + o + n - 2, other) for n in range(1, 5)]
    targets += [wrap(r + dr, o + do) for dr in (-1, 0, 1) for do in (-1, 0, 1) if (dr, do) != (0, 0)]
    for target in targets:
        pl.semaphore_signal(barrier, inc=1, device_id=target, device_id_type=MESH)
    return len(targets)


def lay_rows(cot, a, pl_, pr_):
    def body(it, _):
        block = jnp.swapaxes(cot[:, pl.ds(pl.multiple_of(it * 16, 16), 16), :], 0, 1)
        a[pl.ds(DMAX + it * 16, 16)] = block
        for n in range(2):
            left, right = packed([block[8 * n + w] for w in range(8)])
            pl_[it * 2 + n] = left
            pr_[it * 2 + n] = right
        return 0

    lax.fori_loop(0, 8, body, 0)


def kernel(
    dil, emb, w, bias, cot_hbm, out_hbm, res, ge,
    cot, out, ec, er, a, rl, rr, pl_, pr_, ga, grl, grr, gpl, gpr, x0, x1, s0, t1, s1, t0, wf, wb, gw, gb,
    pay, terms, wr1, w2, wr2, inbox, win, caps,
    io, esend, erecv, hsend, hrecv, gsend, grecv, sa, ra, sb, rb, sc, rc, st, rt, su, ru, local_sem,
):
    r, o = lax.axis_index("diag"), lax.axis_index("off")
    core, b = lax.rem(r, 2), lax.div(r, 2)
    me = o * 2 + core
    row0, band0 = r * TI, o * TK
    fetch = pltpu.make_async_copy(cot_hbm, cot, io.at[0])
    fetch.start()

    def peer_a(n):
        other = lax.rem(me + n, 16)
        return other, (2 * b + lax.rem(other, 2), lax.div(other, 2))

    def peer_b(n):
        other = lax.rem(b + n, 16)
        return other, (2 * other + core, o)

    barrier = pltpu.get_barrier_semaphore()

    def greet(target):
        pl.semaphore_signal(barrier, inc=1, device_id=target, device_id_type=MESH)

    count = greet_exchange(r, o, barrier)
    for n in range(1, 16):
        greet(peer_a(n)[1])
        greet(peer_b(n)[1])
    for n in range(1, 8):
        oo = lax.rem(o + n, 8)
        greet(wrap(r - oo, oo))
        greet(wrap(r - oo - 1, oo))
    greet(wrap(r - o - 1, o))

    @pl.when(o > 0)
    def _():
        greet(wrap(r - o, o))

    count = count + 30 + 14 + 1 + jnp.minimum(o, 1)
    ec[0] = jnp.zeros((CH, 128), bf16)
    ec[5] = jnp.zeros((CH, 128), bf16)
    er[1] = emb[...]
    d0, d1 = dil[0], dil[1]
    place_weights(w, wf, wb)
    lane_caps(band0, d0, caps)
    fetch.wait()
    lay_rows(cot, a, pl_, pr_)
    pl.semaphore_wait(barrier, count)
    ecopies = embed_copies(r, o, emb, ec, er, esend, erecv)
    hcopies = halo_copies(r, o, a, pl_, pr_, rl, rr, hsend, hrecv)
    for c in ecopies + hcopies:
        c.start()

    eye = lax.broadcasted_iota(jnp.int32, (CH, CH), 0) == lax.broadcasted_iota(jnp.int32, (CH, CH), 1)

    def column(layer):
        return jnp.sum(jnp.where(eye, bias[layer : layer + 1, :], 0.0), axis=1, keepdims=True)

    for c in ecopies:
        c.wait_recv()
    bounded_blocks(r, o, ec, er)
    phase_windows(ec, win)
    phase_x0(d0, er, win, caps, x0, s0)
    phase_x1(row0, band0, d0, d1, wf[0], column(0), x0, s0, x1, s1, 48)
    for c in hcopies:
        c.wait_recv()
    phase_shift(row0, band0, d1, a, rl, rr, t1)
    phase_g1(d1, wb[1], x1, t1, ga, gpl, gpr)
    gcopies = halo_copies(r, o, ga, gpl, gpr, grl, grr, gsend, grecv)
    for c in gcopies:
        c.start()
    phase_gw(lambda i: t1[i + DMAX, 64:96, :], s1, DMAX, d1, gw, gb)
    third1 = pack_grads(1, gw, gb, pay)
    phase_gw(lambda i: ga[i + DMAX], s0, 2 * DMAX, d0, gw, gb)
    third0 = pack_grads(0, gw, gb, pay)
    rest = third0 + pltpu.roll(third1, 64, 1)
    for n in range(16):
        pay[n, 1] = rest[8 * n : 8 * n + 8] if n < 4 else jnp.zeros((8, 128), f32)

    first = [remote(pay.at[other], wr1.at[me], sa.at[n], ra.at[me], target)
             for n in range(1, 16) for other, target in [peer_a(n)]]
    for c in first:
        c.start()

    for c in gcopies:
        c.wait_recv()
    phase_shift(row0, band0, d0, ga, grl, grr, t0)
    rsum, lo, hi = phase_g0(d0, wb[0], s0, t0)
    for n in range(8):
        rows = slice(4 * n, 4 * n + 4)
        terms[0, n] = rsum[rows]
        terms[1, n] = lo[rows]
        terms[2, n] = hi[rows]
    eout = []
    for n in range(0, 8):
        oo = lax.rem(o + n, 8)
        for kind, dr in ((0, 0), (1, o), (2, o + 1)):
            if n == 0 and kind < 2:
                continue
            eout.append(remote(terms.at[kind, oo], inbox.at[kind * 8 + o], st.at[kind * 8 + n], rt.at[kind * 8 + o], wrap(r + dr, oo)))
    for c in eout:
        c.start()
    own = remote(terms.at[1, o], inbox.at[8 + o], st.at[8], rt.at[8 + o], wrap(r + o, o))

    @pl.when(o > 0)
    def _():
        own.start()

    local = pltpu.make_async_copy(terms.at[1, o], inbox.at[8 + o], local_sem)

    @pl.when(o == 0)
    def _():
        local.start()

    inbox[o] = terms[0, o]

    def arrived(dst, sem):
        pltpu.make_async_copy(dst, dst, sem).wait()

    def total(buf):
        acc = buf[0]
        for n in range(1, 16):
            acc = acc + buf[n]
        return acc

    wr1[me] = pay[me]
    for n in range(1, 16):
        other, _t = peer_a(n)
        arrived(wr1.at[other], ra.at[other])
    w2[...] = total(wr1)
    second = [remote(w2, wr2.at[b], sb.at[n], rb.at[b], target)
              for n in range(1, 16) for other, target in [peer_b(n)]]
    for c in second:
        c.start()

    phase_x2(row0, band0, d1, wf[1], column(1), x1, s1, out, 64)
    write = pltpu.make_async_copy(out, out_hbm, io.at[1])
    write.start()

    for kind in range(3):
        for n in range(8):
            if kind == 0 and n == 0:
                continue
            oo = lax.rem(o + n, 8)
            slot = kind * 8 + oo
            if kind == 1 and n == 0:
                @pl.when(o > 0)
                def _():
                    arrived(inbox.at[slot], rt.at[slot])
            else:
                arrived(inbox.at[slot], rt.at[slot])

    @pl.when(o == 0)
    def _():
        local.wait()

    acc = inbox[0]
    for n in range(1, 24):
        acc = acc + inbox[n]
    ge[o] = acc
    eall = [remote(ge.at[o], ge.at[o], su.at[n], ru.at[o], wrap(r, o + n)) for n in range(1, 8)]
    for c in eall:
        c.start()

    wr2[b] = w2[...]
    for n in range(1, 16):
        other, _t = peer_b(n)
        arrived(wr2.at[other], rb.at[other])
    res[me] = total(wr2)
    third = [remote(res.at[me], res.at[me], sc.at[n], rc.at[me], target)
             for n in range(1, 16) for other, target in [peer_a(n)]]
    for c in third:
        c.start()
    for n in range(1, 8):
        oo = lax.rem(o + n, 8)
        arrived(ge.at[oo], ru.at[oo])
    for n in range(1, 16):
        other, _t = peer_a(n)
        arrived(res.at[other], rc.at[other])
    for c in first + second + third + eout + eall + ecopies + hcopies + gcopies:
        c.wait_send()

    @pl.when(o > 0)
    def _():
        own.wait_send()

    write.wait()


def finish(section, res, ge, out, gw_out, gb_out, ge_out):
    out[...] = section[...]

    @pl.when(pl.program_id(0) == 0)
    def _():
        unpack_grads(res, gw_out, gb_out)
        for n in range(8):
            ge_out[4 * n : 4 * n + 4, :] = ge[n]


def per_device(bin_embed, weights, biases, dilations, cotangent):
    vmem = pl.BlockSpec(memory_space=pltpu.VMEM)
    smem = pl.BlockSpec(memory_space=pltpu.SMEM)
    hbm = pl.BlockSpec(memory_space=pl.ANY)
    shape = jax.ShapeDtypeStruct
    dma = pltpu.SemaphoreType.DMA
    mem = pltpu.VMEM
    halo = [mem((H1, CH, 128), bf16), mem((18, CH, 128), bf16), mem((18, CH, 128), bf16),
            mem((16, CH, 128), bf16), mem((16, CH, 128), bf16)]
    section, res, ge = pl.pallas_call(
        kernel,
        out_shape=[shape((CH, TI, TK), bf16), shape((16, 2, 8, 128), f32), shape((8, 4, 128), f32)],
        in_specs=[smem, vmem, vmem, vmem, hbm],
        out_specs=[hbm, vmem, vmem],
        scratch_shapes=[
            mem((CH, TI, TK), bf16), mem((CH, TI, TK), bf16),
            mem((6, CH, 128), bf16), mem((3, CH, 128), bf16), *halo, *halo,
            mem((H2, CH, 256), bf16), mem((H1, CH, 256), bf16),
            mem((H2, 5 * CH, 256), bf16), mem((H1, 5 * CH, 128), bf16),
            mem((H1, 5 * CH, 128), bf16), mem((H1, 5 * CH, 128), bf16),
            mem((2, CH, 9 * CH), bf16), mem((2, CH, 9 * CH), bf16),
            mem((CH, 9 * CH), f32), mem((CH, 128), f32),
            mem((16, 2, 8, 128), f32), mem((3, 8, 4, 128), f32),
            mem((16, 2, 8, 128), f32), mem((2, 8, 128), f32),
            mem((16, 2, 8, 128), f32), mem((24, 4, 128), f32),
            mem((H2 + 4 * DMAX, CH, 256), bf16), mem((10, CH, 128), bf16),
            dma((2,)), dma((6,)), dma((6,)), dma((8,)), dma((8,)), dma((8,)), dma((8,)),
            dma((16,)), dma((16,)), dma((16,)), dma((16,)), dma((16,)), dma((16,)),
            dma((24,)), dma((24,)), dma((8,)), dma((8,)), dma,
        ],
        compiler_params=pltpu.CompilerParams(collective_id=0, has_side_effects=True, vmem_limit_bytes=60 << 20),
        name="section",
    )(dilations, bin_embed, weights, biases, cotangent)
    part = pl.BlockSpec((8, TI, TK), lambda n: (n, 0, 0))
    return pl.pallas_call(
        finish,
        grid=(CH // 8,),
        out_shape=[shape((CH, TI, TK), bf16), shape((2, 9, CH, CH), f32), shape((2, CH), f32), shape((CH, TI), f32)],
        in_specs=[part, vmem, vmem],
        out_specs=[part, vmem, vmem, vmem],
        name="finish",
    )(section, res, ge)


def solution(mesh):
    placed = (P(None, "diag"), P(), P(), P(), P(None, "diag", "off"))
    return jax.shard_map(
        per_device,
        mesh=mesh,
        in_specs=placed,
        out_specs=(P(None, "diag", "off"), P(), P(), P(None, "diag")),
        check_vma=False,
    )
```

```python
import jax
import jax.numpy as jnp
from jax import lax
from jax.experimental import pallas as pl
from jax.experimental.pallas import tpu as pltpu
from jax.sharding import PartitionSpec as P

DMAX = 8
CH = 32
TI = 128
TK = 128
H1 = TI + 2 * DMAX
H2 = TI + 4 * DMAX
NBINS = 4096
KBAND = 1024
bf16 = jnp.bfloat16
f32 = jnp.float32
NT = (((1,), (1,)), ((), ()))


def lanes(n=1):
    return lax.broadcasted_iota(jnp.int32, (CH, 128), 1)


def level(value):
    return jnp.full((CH, 128), value.astype(f32)).astype(bf16)


def in_range(s, d):
    p = lanes().astype(bf16)
    return p < level(128 - s * d) if s > 0 else p >= level(-s * d)


def turned(x, amount):
    return pltpu.roll(x, lax.rem(256 - amount, 128), 1)


def shift_pair(a, b, amount, inside, both=True):
    ra, rb = turned(a, amount), turned(b, amount)
    out_a = jnp.where(inside, ra, rb)
    if not both:
        return out_a
    return out_a, jnp.where(inside, rb, ra)


def row_masks(row0, band0, i):
    p = lanes()
    row = row0 + i
    ka = band0 + p
    kb = band0 + jnp.where(p < 64, p + 128, p - 128)
    live = (row >= 0)
    ma = (ka < NBINS - row) & live
    mb = (kb < NBINS - row) & (kb >= 0) & (kb < KBAND) & live
    return ma, mb


def store_shifts(dst, i, a, b, amounts, insides, both=True):
    for n, s in enumerate((-2, -1, 0, 1, 2)):
        rows = slice(CH * n, CH * (n + 1))
        if s == 0:
            dst[i, rows, 0:128] = a
            if both:
                dst[i, rows, 128:256] = b
        elif both:
            sa, sb = shift_pair(a, b, amounts[n], insides[n])
            dst[i, rows, 0:128] = sa
            dst[i, rows, 128:256] = sb
        else:
            dst[i, rows, 0:128] = shift_pair(a, b, amounts[n], insides[n], False)


def taps(src, i, d, lo=0, hi=256):
    return jnp.concatenate(
        [src[i - d, 64:160, lo:hi], src[i, 32:128, lo:hi], src[i + d, 0:96, lo:hi]], axis=0
    )


def shift_tables(d):
    amounts = [s * d for s in (-2, -1, 0, 1, 2)]
    return amounts, [in_range(s, d) for s in (-2, -1, 0, 1, 2)]


LOW = -1e38


def bounded_blocks(r, o, ec, er):
    for n in range(1, 5):
        ec[n] = jnp.where(r + o + n - 2 < NBINS // TI, ec[n], LOW)
    for n in (0, 2):
        ec_row = r + n - 1
        er[n] = jnp.where((ec_row >= 0) & (ec_row < NBINS // TI), er[n], LOW)


def lane_caps(band0, d, caps):
    p = lanes()
    for n, s in enumerate((-2, -1, 0, 1, 2)):
        for half in range(2):
            k = band0 + s * d + (jnp.where(p < 64, p + 128, p - 128) if half else p)
            caps[2 * n + half] = jnp.where((k >= 0) & (k < KBAND), 3e38, 0.0).astype(bf16)


def phase_windows(ec, win, unroll=32):
    u = lanes()
    ub = u.astype(bf16)

    def body(it, _):
        m0 = it * unroll - 4 * DMAX
        q = lax.div(m0 + 128, 128) - 1
        t0 = m0 - 128 * q
        prev, here, after, later = (ec[q + 1 + n] for n in range(4))
        high = jnp.where((u >= 64) & (t0 < 32), prev, after)
        low = jnp.where((u < 64) & (t0 >= 96), later, here)
        for w in range(unroll):
            t = t0 + w
            beyond = ub >= level(t)
            back = lax.rem(128 - t, 128)
            win[it * unroll + w, :, 0:128] = pltpu.roll(jnp.where(beyond, here, after), back, 1)
            win[it * unroll + w, :, 128:256] = pltpu.roll(jnp.where(beyond, high, low), back, 1)
        return 0

    lax.fori_loop(0, (H2 + 4 * DMAX) // unroll, body, 0)


def phase_x0(d, er, win, caps, x0, s0, unroll=16):
    def body(it, _):
        i0 = it * unroll - 2 * DMAX
        q = lax.div(i0 + 128, 128) - 1
        block = pltpu.roll(er[q + 1], lax.rem(256 - (i0 - 128 * q), 128), 1)
        for w in range(unroll):
            j = it * unroll + w
            own = jnp.broadcast_to(block[:, w : w + 1], (CH, 128))
            for n, s in enumerate((-2, -1, 0, 1, 2)):
                for half in range(2):
                    at = slice(128 * half, 128 * half + 128)
                    v = own + win[j + 2 * DMAX + s * d, :, at]
                    if s == 0:
                        x0[j, :, at] = v
                    s0[j, CH * n : CH * n + CH, at] = jnp.minimum(jnp.maximum(v, 0), caps[2 * n + half])
        return 0

    lax.fori_loop(0, H2 // unroll, body, 0)


def phase_x1(row0, band0, d, dn, wf, bias, x0, s0, x1, s1, unroll=4):
    amounts, insides = shift_tables(dn)
    bias = jnp.broadcast_to(bias, (CH, 128))

    def body(it, _):
        for w in range(unroll):
            j = it * unroll + w
            jj = j + DMAX
            conv = jnp.dot(wf, taps(s0, jj, d), preferred_element_type=f32)
            ma, mb = row_masks(row0, band0, j - DMAX)
            a = x0[jj, :, 0:128].astype(f32) + conv[:, 0:128] + bias
            b = x0[jj, :, 128:256].astype(f32) + conv[:, 128:256] + bias
            a = jnp.where(ma, a, 0.0).astype(bf16)
            b = jnp.where(mb, b, 0.0).astype(bf16)
            x1[j, :, 0:128] = a
            x1[j, :, 128:256] = b
            store_shifts(s1, j, jnp.maximum(a, 0), jnp.maximum(b, 0), amounts, insides, False)
        return 0

    lax.fori_loop(0, H1 // unroll, body, 0)


def phase_x2(row0, band0, d, wf, bias, x1, s1, out, unroll=16):
    bias = jnp.broadcast_to(bias, (CH, 128))

    def body(it, _):
        rows = []
        for w in range(0, unroll, 2):
            i = it * unroll + w
            j = i + DMAX
            x = jnp.concatenate([taps(s1, j, d, 0, 128), taps(s1, j + 1, d, 0, 128)], axis=1)
            conv = jnp.dot(wf, x, preferred_element_type=f32)
            for z in range(2):
                ma, _mb = row_masks(row0, band0, i + z)
                a = x1[j + z, :, 0:128].astype(f32) + conv[:, 128 * z : 128 * z + 128] + bias
                rows.append(jnp.where(ma, a, 0.0).astype(bf16))
        out[:, pl.ds(pl.multiple_of(it * unroll, unroll), unroll), :] = jnp.swapaxes(jnp.stack(rows), 0, 1)
        return 0

    lax.fori_loop(0, TI // unroll, body, 0)


def phase_gw(h, s, soff, d, gw, gb, unroll=64):
    def body(it, carry):
        acc, accb = carry
        for w in range(0, unroll, 2):
            i = it * unroll + w
            x = jnp.concatenate(
                [taps(s, i + soff, d, 0, 128), taps(s, i + 1 + soff, d, 0, 128)], axis=1
            )
            ha, hb = h(i), h(i + 1)
            hh = jnp.concatenate([ha, hb], axis=1)
            acc = acc + lax.dot_general(hh, x, NT, preferred_element_type=f32)
            accb = accb + (ha.astype(f32) + hb.astype(f32))
        return acc, accb

    acc, accb = lax.fori_loop(
        0, TI // unroll, body, (jnp.zeros((CH, 9 * CH), f32), jnp.zeros((CH, 128), f32))
    )
    gw[...] = acc
    gb[...] = accb


def packed(rows):
    lane = lanes()
    left, right = rows[0], rows[7]
    for w in range(1, 8):
        left = jnp.where(lane < 16 * w, left, pltpu.roll(rows[w], 16 * w, 1))
    for w in range(6, -1, -1):
        right = jnp.where(lane >= 16 * (w + 1), right, pltpu.roll(rows[w], 16 * w + 16, 1))
    return left, right


def phase_shift(row0, band0, d, depth, rows, rl, rr, dst, unroll):
    lane = lanes()
    insides = [in_range(s, d) for s in (-2, -1, 1, 2)]

    def body(it, _):
        for g in range(unroll):
            group = it * unroll + g
            first = row0 + group * 8 - depth
            row = first + lax.div(lane, 16)
            kr = band0 + 128 + lax.rem(lane, 16)
            kl = band0 - 16 + lax.rem(lane, 16)
            right = jnp.where((row >= 0) & (kr < KBAND) & (kr < NBINS - row), rl[group], 0)
            left = jnp.where((row >= 0) & (kl >= 0) & (kl < NBINS - row), rr[group], 0)
            for w in range(8):
                j = group * 8 + w
                live = (first + w >= 0) & (band0 + lane < NBINS - (first + w))
                a = jnp.where(live, rows[j], 0)
                dst[j, 64:96, :] = a
                for n, s in enumerate((-2, -1, 1, 2)):
                    if s > 0:
                        side = pltpu.roll(right, lax.rem(256 - 16 * w - s * d, 128), 1)
                    else:
                        side = pltpu.roll(left, lax.rem(256 + 16 * (7 - w) - s * d, 128), 1)
                    m = n if s < 0 else n + 1
                    dst[j, CH * m : CH * m + CH, :] = jnp.where(
                        insides[n], pltpu.roll(a, lax.rem(256 - s * d, 128), 1), side
                    )
        return 0

    lax.fori_loop(0, (TI + 2 * depth) // 8 // unroll, body, 0)


def phase_g1(d, wb, x1, t1, ga, gpl, gpr, unroll=48):
    def body(it, _):
        rows = []
        for w in range(0, unroll, 2):
            j = it * unroll + w
            x = jnp.concatenate([taps(t1, j + DMAX, d, 0, 128), taps(t1, j + DMAX + 1, d, 0, 128)], axis=1)
            q = jnp.dot(wb, x, preferred_element_type=f32)
            for z in range(2):
                h = t1[j + DMAX + z, 64:96, :].astype(f32)
                gate = x1[j + z, :, 0:128].astype(f32) > 0
                g = (h + jnp.where(gate, q[:, 128 * z : 128 * z + 128], 0.0)).astype(bf16)
                ga[j + z] = g
                rows.append(g)
        for n in range(unroll // 8):
            left, right = packed(rows[8 * n : 8 * n + 8])
            gpl[it * (unroll // 8) + n] = left
            gpr[it * (unroll // 8) + n] = right
        return 0

    lax.fori_loop(0, H1 // unroll, body, 0)


def phase_g0(d, wb, s0, t0, begin, end, carry, unroll=32):
    lane = lanes()
    ones = jnp.ones((128, 128), bf16)

    def body(it, carry):
        rsum, lo, hi = carry
        rows = []
        for w in range(0, unroll, 2):
            i = it * unroll + w
            j = i + DMAX
            x = jnp.concatenate([taps(t0, j, d, 0, 128), taps(t0, j + 1, d, 0, 128)], axis=1)
            q = jnp.dot(wb, x, preferred_element_type=f32)
            for z in range(2):
                g1 = t0[j + z, 64:96, 0:128].astype(f32)
                gate = s0[j + z + DMAX, 64:96, 0:128].astype(f32) > 0
                gp = (g1 + jnp.where(gate, q[:, 128 * z : 128 * z + 128], 0.0)).astype(bf16)
                rows.append(gp)
                moved = pltpu.roll(gp, i + z, 1).astype(f32)
                low = jnp.where(lane >= i + z, moved, 0.0)
                lo = lo + low
                hi = hi + (moved - low)
        sums = jnp.dot(jnp.concatenate(rows, axis=0), ones, preferred_element_type=f32)
        for w in range(unroll):
            rsum = jnp.where(lane == it * unroll + w, sums[CH * w : CH * w + CH], rsum)
        return rsum, lo, hi

    return lax.fori_loop(begin // unroll, end // unroll, body, carry)
MESH = pl.DeviceIdType.MESH
NR, NO = 32, 8


def place_weights(w, wf, wb):
    row = lax.broadcasted_iota(jnp.int32, (CH, 9 * CH), 0)
    col = lax.broadcasted_iota(jnp.int32, (CH, 9 * CH), 1)
    for layer in range(2):
        fwd = jnp.zeros((CH, 9 * CH), f32)
        bwd = jnp.zeros((CH, 9 * CH), f32)
        for t in range(9):
            spot = jnp.where(col == row + CH * t, 1.0, 0.0).astype(bf16)
            fwd = fwd + jnp.dot(w[layer, t], spot, preferred_element_type=f32)
            bwd = bwd + lax.dot_general(
                w[layer, 8 - t], spot, (((0,), (0,)), ((), ())), preferred_element_type=f32
            )
        wf[layer] = fwd.astype(bf16)
        wb[layer] = bwd.astype(bf16)


def pack_grads(layer, gw, gb, pay):
    third = jnp.concatenate([gw[:, 256:288], jnp.sum(gb[...], axis=1, keepdims=True), jnp.zeros((CH, 95), f32)], axis=1)
    for og in range(4):
        rows = slice(8 * og, 8 * og + 8)
        for lt in range(2):
            pay[layer * 8 + og * 2 + lt, 0] = gw[rows, 128 * lt : 128 * lt + 128]
    return third


def unpack_grads(res, gw_out, gb_out):
    eye = lax.broadcasted_iota(jnp.int32, (CH, CH), 0) == lax.broadcasted_iota(jnp.int32, (CH, CH), 1)
    third = jnp.concatenate([res[og, 1] for og in range(4)], axis=0)
    for layer in range(2):
        for lt in range(2):
            tile = jnp.concatenate([res[layer * 8 + og * 2 + lt, 0] for og in range(4)], axis=0)
            for n in range(4):
                gw_out[layer, 4 * lt + n] = tile[:, CH * n : CH * n + CH]
        gw_out[layer, 8] = third[:, 64 * layer : 64 * layer + CH]
        column = third[:, 64 * layer + CH : 64 * layer + CH + 1]
        gb_out[layer : layer + 1, :] = jnp.sum(jnp.where(eye, column, 0.0), axis=0, keepdims=True)


def remote(src, dst, send, recv, target):
    return pltpu.make_async_remote_copy(
        src_ref=src, dst_ref=dst, send_sem=send, recv_sem=recv, device_id=target, device_id_type=MESH
    )


def wrap(r, o):
    return (lax.rem(r + 2 * NR, NR), lax.rem(o + NO, NO))


def halo_copies(r, o, a, pl_, pr_, rl, rr, send, recv):
    jobs = [
        (pl_, rl.at[2:18], 0, -1),
        (pr_, rr.at[2:18], 0, 1),
        (a.at[128:144], a.at[0:16], 1, 0),
        (a.at[16:32], a.at[144:160], -1, 0),
        (pl_.at[14:16], rl.at[0:2], 1, -1),
        (pl_.at[0:2], rl.at[18:20], -1, -1),
        (pr_.at[14:16], rr.at[0:2], 1, 1),
        (pr_.at[0:2], rr.at[18:20], -1, 1),
    ]
    return [
        remote(src, dst, send.at[n], recv.at[n], wrap(r + dr, o + do))
        for n, (src, dst, dr, do) in enumerate(jobs)
    ]


def embed_copies(r, o, emb, ec, er, send, recv):
    other = o + 1 - 2 * lax.rem(o, 2)
    copies = [
        remote(emb, ec.at[n], send.at[n - 1], recv.at[n - 1], wrap(r - other - (n - 2), other))
        for n in range(1, 5)
    ]
    copies.append(remote(emb, er.at[0], send.at[4], recv.at[4], wrap(r + 1, o)))
    copies.append(remote(emb, er.at[2], send.at[5], recv.at[5], wrap(r - 1, o)))
    return copies


def greet_exchange(r, o, barrier):
    other = o + 1 - 2 * lax.rem(o, 2)
    targets = [wrap(r + o + n - 2, other) for n in range(1, 5)]
    targets += [wrap(r + dr, o + do) for dr in (-1, 0, 1) for do in (-1, 0, 1) if (dr, do) != (0, 0)]
    for target in targets:
        pl.semaphore_signal(barrier, inc=1, device_id=target, device_id_type=MESH)
    return len(targets)


def lay_rows(cot, a, pl_, pr_):
    def body(it, _):
        block = jnp.swapaxes(cot[:, pl.ds(pl.multiple_of(it * 16, 16), 16), :], 0, 1)
        a[pl.ds(2 * DMAX + it * 16, 16)] = block
        for n in range(2):
            left, right = packed([block[8 * n + w] for w in range(8)])
            pl_[it * 2 + n] = left
            pr_[it * 2 + n] = right
        return 0

    lax.fori_loop(0, 8, body, 0)


def kernel(
    dil, emb_hbm, w_hbm, bias_hbm, cot_hbm, out_hbm, res, ge,
    emb, w, bias, cot, out, ec, er, a, rl, rr, pl_, pr_, ga, grl, grr, gpl, gpr, x0, x1, s0, t1, s1, t0, wf, wb, gw, gb,
    pay, terms, wr1, w2, wr2, inbox, shares, win, caps,
    io, esend, erecv, hsend, hrecv, gsend, grecv, sa, ra, sb, rb, sc, rc, st, rt, su, ru, local_sem,
):
    r, o = lax.axis_index("diag"), lax.axis_index("off")
    core, b = lax.rem(r, 2), lax.div(r, 2)
    me = o * 2 + core
    row0, band0 = r * TI, o * TK
    fetches = [
        pltpu.make_async_copy(src, dst, io.at[n])
        for n, (src, dst) in enumerate(((emb_hbm, emb), (w_hbm, w), (bias_hbm, bias), (cot_hbm, cot)))
    ]
    for c in fetches:
        c.start()

    def peer_a(n):
        other = lax.rem(me + n, 16)
        return other, (2 * b + lax.rem(other, 2), lax.div(other, 2))

    def peer_b(n):
        other = lax.rem(b + n, 16)
        return other, (2 * other + core, o)

    barrier = pltpu.get_barrier_semaphore()

    def greet(target):
        pl.semaphore_signal(barrier, inc=1, device_id=target, device_id_type=MESH)

    count = greet_exchange(r, o, barrier)
    for n in range(1, 16):
        greet(peer_a(n)[1])
        greet(peer_b(n)[1])
    greet(wrap(r - o - 1, o))

    @pl.when(o > 0)
    def _():
        greet(wrap(r - o, o))

    count = count + 30 + 1 + jnp.minimum(o, 1)
    ec[0] = jnp.zeros((CH, 128), bf16)
    ec[5] = jnp.zeros((CH, 128), bf16)
    d0, d1 = dil[0], dil[1]
    lane_caps(band0, d0, caps)
    for c in fetches:
        c.wait()
    er[1] = emb[...]
    place_weights(w, wf, wb)
    lay_rows(cot, a, pl_, pr_)
    pl.semaphore_wait(barrier, count)
    ecopies = embed_copies(r, o, emb, ec, er, esend, erecv)
    hcopies = halo_copies(r, o, a, pl_, pr_, rl, rr, hsend, hrecv)
    for c in ecopies + hcopies:
        c.start()

    eye = lax.broadcasted_iota(jnp.int32, (CH, CH), 0) == lax.broadcasted_iota(jnp.int32, (CH, CH), 1)

    def column(layer):
        return jnp.sum(jnp.where(eye, bias[layer : layer + 1, :], 0.0), axis=1, keepdims=True)

    for c in ecopies:
        c.wait_recv()
    bounded_blocks(r, o, ec, er)
    phase_windows(ec, win)
    phase_x0(d0, er, win, caps, x0, s0)
    phase_x1(row0, band0, d0, d1, wf[0], column(0), x0, s0, x1, s1, 48)
    for c in hcopies:
        c.wait_recv()
    phase_shift(row0, band0, d1, 2 * DMAX, a, rl, rr, t1, 4)
    phase_g1(d1, wb[1], x1, t1, ga, gpl, gpr)
    gcopies = [
        remote(gpl, grl, gsend.at[0], grecv.at[0], wrap(r, o - 1)),
        remote(gpr, grr, gsend.at[1], grecv.at[1], wrap(r, o + 1)),
    ]
    for c in gcopies:
        c.start()
    phase_gw(lambda i: t1[i + 2 * DMAX, 64:96, :], s1, DMAX, d1, gw, gb)
    third1 = pack_grads(1, gw, gb, pay)
    phase_gw(lambda i: ga[i + DMAX], s0, 2 * DMAX, d0, gw, gb)
    third0 = pack_grads(0, gw, gb, pay)
    rest = third0 + pltpu.roll(third1, 64, 1)
    for n in range(16):
        pay[n, 1] = rest[8 * n : 8 * n + 8] if n < 4 else jnp.zeros((8, 128), f32)

    first = [remote(pay.at[other], wr1.at[me], sa.at[n], ra.at[me], target)
             for n in range(1, 16) for other, target in [peer_a(n)]]
    for c in first:
        c.start()

    for c in gcopies:
        c.wait_recv()
    phase_shift(row0, band0, d0, DMAX, ga, grl, grr, t0, 3)
    def arrived(dst, sem):
        pltpu.make_async_copy(dst, dst, sem).wait()

    def total(buf):
        acc = buf[0]
        for n in range(1, 16):
            acc = acc + buf[n]
        return acc

    zero = jnp.zeros((CH, TI), f32)
    sums = phase_g0(d0, wb[0], s0, t0, 0, 64, (zero, zero, zero))
    wr1[me] = pay[me]
    for n in range(1, 16):
        other, _t = peer_a(n)
        arrived(wr1.at[other], ra.at[other])
    w2[...] = total(wr1)
    second = [remote(w2, wr2.at[b], sb.at[n], rb.at[b], target)
              for n in range(1, 16) for other, target in [peer_b(n)]]
    for c in second:
        c.start()

    rsum, lo, hi = phase_g0(d0, wb[0], s0, t0, 64, 128, sums)
    terms[0] = lo
    terms[1] = hi
    low = remote(terms.at[0], inbox.at[0], st.at[0], rt.at[0], wrap(r + o, o))
    high = remote(terms.at[1], inbox.at[1], st.at[1], rt.at[1], wrap(r + o + 1, o))
    high.start()
    local = pltpu.make_async_copy(terms.at[0], inbox.at[0], local_sem)

    @pl.when(o > 0)
    def _():
        low.start()

    @pl.when(o == 0)
    def _():
        local.start()

    phase_x2(row0, band0, d1, wf[1], column(1), x1, s1, out, 64)
    write = pltpu.make_async_copy(out, out_hbm, io.at[4])
    write.start()

    @pl.when(o > 0)
    def _():
        low.wait_recv()

    @pl.when(o == 0)
    def _():
        local.wait()

    high.wait_recv()
    shares[o] = rsum + inbox[0] + inbox[1]
    eall = [remote(shares.at[o], shares.at[o], su.at[n], ru.at[o], wrap(r, o + n)) for n in range(1, 8)]
    for c in eall:
        c.start()

    wr2[b] = w2[...]
    for n in range(1, 16):
        other, _t = peer_b(n)
        arrived(wr2.at[other], rb.at[other])
    res[me] = total(wr2)
    third = [remote(res.at[me], res.at[me], sc.at[n], rc.at[me], target)
             for n in range(1, 16) for other, target in [peer_a(n)]]
    for c in third:
        c.start()
    for n in range(1, 8):
        oo = lax.rem(o + n, 8)
        arrived(shares.at[oo], ru.at[oo])
    acc = shares[0]
    for n in range(1, 8):
        acc = acc + shares[n]
    ge[...] = acc
    for n in range(1, 16):
        other, _t = peer_a(n)
        arrived(res.at[other], rc.at[other])
    for c in first + second + third + [high] + eall + ecopies + hcopies + gcopies:
        c.wait_send()

    @pl.when(o > 0)
    def _():
        low.wait_send()

    write.wait()


def finish(section, res, ge, out, gw_out, gb_out, ge_out, held, come, go):
    size = CH // 4
    parts = [slice(n * size, n * size + size) for n in range(4)]
    ins = [pltpu.make_async_copy(section.at[p], held.at[p], come.at[n]) for n, p in enumerate(parts)]
    outs = [pltpu.make_async_copy(held.at[p], out.at[p], go.at[n]) for n, p in enumerate(parts)]
    for c in ins:
        c.start()
    for n in range(4):
        ins[n].wait()
        outs[n].start()
    unpack_grads(res, gw_out, gb_out)
    ge_out[...] = ge[...]
    for c in outs:
        c.wait()


def per_device(bin_embed, weights, biases, dilations, cotangent):
    vmem = pl.BlockSpec(memory_space=pltpu.VMEM)
    smem = pl.BlockSpec(memory_space=pltpu.SMEM)
    hbm = pl.BlockSpec(memory_space=pl.ANY)
    shape = jax.ShapeDtypeStruct
    dma = pltpu.SemaphoreType.DMA
    mem = pltpu.VMEM
    halo = [mem((H2, CH, 128), bf16), mem((20, CH, 128), bf16), mem((20, CH, 128), bf16),
            mem((16, CH, 128), bf16), mem((16, CH, 128), bf16)]
    edge = [mem((H1, CH, 128), bf16)] + [mem((18, CH, 128), bf16)] * 4
    section, res, ge = pl.pallas_call(
        kernel,
        out_shape=[shape((CH, TI, TK), bf16), shape((16, 2, 8, 128), f32), shape((CH, TI), f32)],
        in_specs=[smem, hbm, hbm, hbm, hbm],
        out_specs=[hbm, vmem, vmem],
        scratch_shapes=[
            mem((CH, TI), bf16), mem((2, 9, CH, CH), bf16), mem((2, CH), f32),
            mem((CH, TI, TK), bf16), mem((CH, TI, TK), bf16),
            mem((6, CH, 128), bf16), mem((3, CH, 128), bf16), *halo, *edge,
            mem((H2, CH, 256), bf16), mem((H1, CH, 256), bf16),
            mem((H2, 5 * CH, 256), bf16), mem((H2, 5 * CH, 128), bf16),
            mem((H1, 5 * CH, 128), bf16), mem((H1, 5 * CH, 128), bf16),
            mem((2, CH, 9 * CH), bf16), mem((2, CH, 9 * CH), bf16),
            mem((CH, 9 * CH), f32), mem((CH, 128), f32),
            mem((16, 2, 8, 128), f32), mem((2, CH, TI), f32),
            mem((16, 2, 8, 128), f32), mem((2, 8, 128), f32),
            mem((16, 2, 8, 128), f32), mem((2, CH, TI), f32), mem((8, CH, TI), f32),
            mem((H2 + 4 * DMAX, CH, 256), bf16), mem((10, CH, 128), bf16),
            dma((5,)), dma((6,)), dma((6,)), dma((8,)), dma((8,)), dma((2,)), dma((2,)),
            dma((16,)), dma((16,)), dma((16,)), dma((16,)), dma((16,)), dma((16,)),
            dma((2,)), dma((2,)), dma((8,)), dma((8,)), dma,
        ],
        compiler_params=pltpu.CompilerParams(collective_id=0, has_side_effects=True, vmem_limit_bytes=60 << 20),
        name="section",
    )(dilations, bin_embed, weights, biases, cotangent)
    out, gw, gb, ge_out = pl.pallas_call(
        finish,
        out_shape=[shape((CH, TI, TK), bf16), shape((2, 9, CH, CH), f32), shape((2, CH), f32), shape((CH, TI), f32)],
        in_specs=[hbm, vmem, vmem],
        out_specs=[hbm, vmem, vmem, vmem],
        scratch_shapes=[mem((CH, TI, TK), bf16), dma((4,)), dma((4,))],
        name="finish",
    )(section, res, ge)
    return out, gw, gb, ge_out


def solution(mesh):
    placed = (P(None, "diag"), P(), P(), P(), P(None, "diag", "off"))
    return jax.shard_map(
        per_device,
        mesh=mesh,
        in_specs=placed,
        out_specs=(P(None, "diag", "off"), P(), P(), P(None, "diag")),
        check_vma=False,
    )
```

```python
import jax
import jax.numpy as jnp
from jax import lax
from jax.experimental import pallas as pl
from jax.experimental.pallas import tpu as pltpu
from jax.sharding import PartitionSpec as P

DMAX = 8
CH = 32
TI = 128
TK = 128
H1 = TI + 2 * DMAX
H2 = TI + 4 * DMAX
NBINS = 4096
KBAND = 1024
bf16 = jnp.bfloat16
f32 = jnp.float32
NT = (((1,), (1,)), ((), ()))


def lanes(n=1):
    return lax.broadcasted_iota(jnp.int32, (CH, 128), 1)


def level(value):
    return jnp.full((CH, 128), value.astype(f32)).astype(bf16)


def in_range(s, d):
    p = lanes().astype(bf16)
    return p < level(128 - s * d) if s > 0 else p >= level(-s * d)


def turned(x, amount):
    return pltpu.roll(x, lax.rem(256 - amount, 128), 1)


def shift_pair(a, b, amount, inside, both=True):
    ra, rb = turned(a, amount), turned(b, amount)
    out_a = jnp.where(inside, ra, rb)
    if not both:
        return out_a
    return out_a, jnp.where(inside, rb, ra)


def row_masks(row0, band0, i):
    p = lanes()
    row = row0 + i
    ka = band0 + p
    kb = band0 + jnp.where(p < 64, p + 128, p - 128)
    live = (row >= 0)
    ma = (ka < NBINS - row) & live
    mb = (kb < NBINS - row) & (kb >= 0) & (kb < KBAND) & live
    return ma, mb


def store_shifts(dst, i, a, b, amounts, insides, both=True):
    for n, s in enumerate((-2, -1, 0, 1, 2)):
        rows = slice(CH * n, CH * (n + 1))
        if s == 0:
            dst[i, rows, 0:128] = a
            if both:
                dst[i, rows, 128:256] = b
        elif both:
            sa, sb = shift_pair(a, b, amounts[n], insides[n])
            dst[i, rows, 0:128] = sa
            dst[i, rows, 128:256] = sb
        else:
            dst[i, rows, 0:128] = shift_pair(a, b, amounts[n], insides[n], False)


def taps(src, i, d, lo=0, hi=256):
    return jnp.concatenate(
        [src[i - d, 64:160, lo:hi], src[i, 32:128, lo:hi], src[i + d, 0:96, lo:hi]], axis=0
    )


def shift_tables(d):
    amounts = [s * d for s in (-2, -1, 0, 1, 2)]
    return amounts, [in_range(s, d) for s in (-2, -1, 0, 1, 2)]


LOW = -1e38


def bounded_blocks(r, o, ec, er):
    for n in range(1, 5):
        ec[n] = jnp.where(r + o + n - 2 < NBINS // TI, ec[n], LOW)
    for n in (0, 2):
        ec_row = r + n - 1
        er[n] = jnp.where((ec_row >= 0) & (ec_row < NBINS // TI), er[n], LOW)


def lane_caps(band0, d, caps):
    p = lanes()
    for n, s in enumerate((-2, -1, 0, 1, 2)):
        for half in range(2):
            k = band0 + s * d + (jnp.where(p < 64, p + 128, p - 128) if half else p)
            caps[2 * n + half] = jnp.where((k >= 0) & (k < KBAND), 3e38, 0.0).astype(bf16)


def phase_windows(ec, win, unroll=32):
    u = lanes()
    ub = u.astype(bf16)

    def body(it, _):
        m0 = it * unroll - 4 * DMAX
        q = lax.div(m0 + 128, 128) - 1
        t0 = m0 - 128 * q
        prev, here, after, later = (ec[q + 1 + n] for n in range(4))
        high = jnp.where((u >= 64) & (t0 < 32), prev, after)
        low = jnp.where((u < 64) & (t0 >= 96), later, here)
        for w in range(unroll):
            t = t0 + w
            beyond = ub >= level(t)
            back = lax.rem(128 - t, 128)
            win[it * unroll + w, :, 0:128] = pltpu.roll(jnp.where(beyond, here, after), back, 1)
            win[it * unroll + w, :, 128:256] = pltpu.roll(jnp.where(beyond, high, low), back, 1)
        return 0

    lax.fori_loop(0, (H2 + 4 * DMAX) // unroll, body, 0)


def phase_x0(d, er, win, caps, x0, s0, unroll=16):
    def body(it, _):
        i0 = it * unroll - 2 * DMAX
        q = lax.div(i0 + 128, 128) - 1
        block = pltpu.roll(er[q + 1], lax.rem(256 - (i0 - 128 * q), 128), 1)
        for w in range(unroll):
            j = it * unroll + w
            own = jnp.broadcast_to(block[:, w : w + 1], (CH, 128))
            for n, s in enumerate((-2, -1, 0, 1, 2)):
                for half in range(2):
                    at = slice(128 * half, 128 * half + 128)
                    v = own + win[j + 2 * DMAX + s * d, :, at]
                    if s == 0:
                        x0[j, :, at] = v
                    s0[j, CH * n : CH * n + CH, at] = jnp.minimum(jnp.maximum(v, 0), caps[2 * n + half])
        return 0

    lax.fori_loop(0, H2 // unroll, body, 0)


def phase_x1(row0, band0, d, dn, wf, bias, x0, s0, x1, s1, unroll=4):
    amounts, insides = shift_tables(dn)
    bias = jnp.broadcast_to(bias, (CH, 128))

    def body(it, _):
        for w in range(unroll):
            j = it * unroll + w
            jj = j + DMAX
            conv = jnp.dot(wf, taps(s0, jj, d), preferred_element_type=f32)
            ma, mb = row_masks(row0, band0, j - DMAX)
            a = x0[jj, :, 0:128].astype(f32) + conv[:, 0:128] + bias
            b = x0[jj, :, 128:256].astype(f32) + conv[:, 128:256] + bias
            a = jnp.where(ma, a, 0.0).astype(bf16)
            b = jnp.where(mb, b, 0.0).astype(bf16)
            x1[j, :, 0:128] = a
            x1[j, :, 128:256] = b
            store_shifts(s1, j, jnp.maximum(a, 0), jnp.maximum(b, 0), amounts, insides, False)
        return 0

    lax.fori_loop(0, H1 // unroll, body, 0)


def phase_x2(row0, band0, d, wf, bias, x1, s1, out, unroll=16):
    bias = jnp.broadcast_to(bias, (CH, 128))

    def body(it, _):
        rows = []
        for w in range(0, unroll, 2):
            i = it * unroll + w
            j = i + DMAX
            x = jnp.concatenate([taps(s1, j, d, 0, 128), taps(s1, j + 1, d, 0, 128)], axis=1)
            conv = jnp.dot(wf, x, preferred_element_type=f32)
            for z in range(2):
                ma, _mb = row_masks(row0, band0, i + z)
                a = x1[j + z, :, 0:128].astype(f32) + conv[:, 128 * z : 128 * z + 128] + bias
                rows.append(jnp.where(ma, a, 0.0).astype(bf16))
        out[:, pl.ds(pl.multiple_of(it * unroll, unroll), unroll), :] = jnp.swapaxes(jnp.stack(rows), 0, 1)
        return 0

    lax.fori_loop(0, TI // unroll, body, 0)


def phase_gw(h, s, soff, d, gw, gb, unroll=64):
    def body(it, carry):
        acc, accb = carry
        for w in range(0, unroll, 2):
            i = it * unroll + w
            x = jnp.concatenate(
                [taps(s, i + soff, d, 0, 128), taps(s, i + 1 + soff, d, 0, 128)], axis=1
            )
            ha, hb = h(i), h(i + 1)
            hh = jnp.concatenate([ha, hb], axis=1)
            acc = acc + lax.dot_general(hh, x, NT, preferred_element_type=f32)
            accb = accb + (ha.astype(f32) + hb.astype(f32))
        return acc, accb

    acc, accb = lax.fori_loop(
        0, TI // unroll, body, (jnp.zeros((CH, 9 * CH), f32), jnp.zeros((CH, 128), f32))
    )
    gw[...] = acc
    gb[...] = accb


def packed(rows):
    lane = lanes()
    left, right = rows[0], rows[7]
    for w in range(1, 8):
        left = jnp.where(lane < 16 * w, left, pltpu.roll(rows[w], 16 * w, 1))
    for w in range(6, -1, -1):
        right = jnp.where(lane >= 16 * (w + 1), right, pltpu.roll(rows[w], 16 * w + 16, 1))
    return left, right


SHIFTS = ((0, -2), (1, -1), (3, 1), (4, 2))


def block_of(n):
    return slice(CH * n, CH * n + CH)


def rolled(x, s, d):
    return pltpu.roll(x, lax.rem(256 - s * d, 128), 1)


def halo_sides(row0, band0, depth, group, rl, rr):
    lane = lanes()
    row = row0 + group * 8 - depth + lax.div(lane, 16)
    kr = band0 + 128 + lax.rem(lane, 16)
    kl = band0 - 16 + lax.rem(lane, 16)
    right = jnp.where((row >= 0) & (kr < KBAND) & (kr < NBINS - row), rl[group], 0)
    left = jnp.where((row >= 0) & (kl >= 0) & (kl < NBINS - row), rr[group], 0)
    return right, left


def side_of(right, left, w, s, d):
    if s > 0:
        return pltpu.roll(right, lax.rem(256 - 16 * w - s * d, 128), 1)
    return pltpu.roll(left, lax.rem(256 + 16 * (7 - w) - s * d, 128), 1)


def put_row(row0, band0, d, depth, j, a, dst):
    row = row0 + j - depth
    live = (row >= 0) & (band0 + lanes() < NBINS - row)
    a = jnp.where(live, a, 0)
    dst[j, block_of(2), :] = a
    for m, s in SHIFTS:
        dst[j, block_of(m), :] = rolled(a, s, d)


def patch_group(row0, band0, d, depth, group, insides, rl, rr, dst):
    right, left = halo_sides(row0, band0, depth, group, rl, rr)
    for w in range(8):
        j = group * 8 + w
        for n, (m, s) in enumerate(SHIFTS):
            dst[j, block_of(m), :] = jnp.where(
                insides[n], dst[j, block_of(m), :], side_of(right, left, w, s, d)
            )


def inside_masks(d):
    return [in_range(s, d) for _m, s in SHIFTS]


def phase_patch(row0, band0, d, depth, groups, rl, rr, dst, unroll):
    insides = inside_masks(d)

    def body(it, _):
        for g in range(unroll):
            patch_group(row0, band0, d, depth, it * unroll + g, insides, rl, rr, dst)
        return 0

    lax.fori_loop(0, groups // unroll, body, 0)


def phase_own_shifts(row0, band0, d, a, dst, unroll=32):
    def body(it, _):
        for w in range(unroll):
            j = 2 * DMAX + it * unroll + w
            put_row(row0, band0, d, 2 * DMAX, j, a[j], dst)
        return 0

    lax.fori_loop(0, TI // unroll, body, 0)


def phase_rim_shifts(row0, band0, d, a, dst):
    def body(it, _):
        for w in range(16):
            j = it * 144 + w
            put_row(row0, band0, d, 2 * DMAX, j, a[j], dst)
        return 0

    lax.fori_loop(0, 2, body, 0)


def phase_g1(d, dn, wb, x1, t1, t0, gpl, gpr, send_chunk, unroll=48):
    def body(it, _):
        rows = []
        for w in range(0, unroll, 2):
            j = it * unroll + w
            x = jnp.concatenate([taps(t1, j + DMAX, d, 0, 128), taps(t1, j + DMAX + 1, d, 0, 128)], axis=1)
            q = jnp.dot(wb, x, preferred_element_type=f32)
            for z in range(2):
                h = t1[j + DMAX + z, 64:96, :].astype(f32)
                gate = x1[j + z, :, 0:128].astype(f32) > 0
                g = (h + jnp.where(gate, q[:, 128 * z : 128 * z + 128], 0.0)).astype(bf16)
                rows.append(g)
        for n in range(unroll // 8):
            left, right = packed(rows[8 * n : 8 * n + 8])
            gpl[it * (unroll // 8) + n] = left
            gpr[it * (unroll // 8) + n] = right
        send_chunk(it)
        for w, g in enumerate(rows):
            j = it * unroll + w
            t0[j, block_of(2), :] = g
            for m, s in SHIFTS:
                t0[j, block_of(m), :] = rolled(g, s, dn)
        return 0

    lax.fori_loop(0, H1 // unroll, body, 0)


def phase_g0(d, wb, s0, t0, begin, end, carry, unroll=32):
    lane = lanes()
    ones = jnp.ones((128, 128), bf16)

    def body(it, carry):
        rsum, lo, hi = carry
        rows = []
        for w in range(0, unroll, 2):
            i = it * unroll + w
            j = i + DMAX
            x = jnp.concatenate([taps(t0, j, d, 0, 128), taps(t0, j + 1, d, 0, 128)], axis=1)
            q = jnp.dot(wb, x, preferred_element_type=f32)
            for z in range(2):
                g1 = t0[j + z, 64:96, 0:128].astype(f32)
                gate = s0[j + z + DMAX, 64:96, 0:128].astype(f32) > 0
                gp = (g1 + jnp.where(gate, q[:, 128 * z : 128 * z + 128], 0.0)).astype(bf16)
                rows.append(gp)
                moved = pltpu.roll(gp, i + z, 1).astype(f32)
                low = jnp.where(lane >= i + z, moved, 0.0)
                lo = lo + low
                hi = hi + (moved - low)
        sums = jnp.dot(jnp.concatenate(rows, axis=0), ones, preferred_element_type=f32)
        for w in range(unroll):
            rsum = jnp.where(lane == it * unroll + w, sums[CH * w : CH * w + CH], rsum)
        return rsum, lo, hi

    return lax.fori_loop(begin // unroll, end // unroll, body, carry)
MESH = pl.DeviceIdType.MESH
NR, NO = 32, 8


def place_weights(w, wf, wb):
    row = lax.broadcasted_iota(jnp.int32, (CH, 9 * CH), 0)
    col = lax.broadcasted_iota(jnp.int32, (CH, 9 * CH), 1)
    for layer in range(2):
        fwd = jnp.zeros((CH, 9 * CH), f32)
        bwd = jnp.zeros((CH, 9 * CH), f32)
        for t in range(9):
            spot = jnp.where(col == row + CH * t, 1.0, 0.0).astype(bf16)
            fwd = fwd + jnp.dot(w[layer, t], spot, preferred_element_type=f32)
            bwd = bwd + lax.dot_general(
                w[layer, 8 - t], spot, (((0,), (0,)), ((), ())), preferred_element_type=f32
            )
        wf[layer] = fwd.astype(bf16)
        wb[layer] = bwd.astype(bf16)


def pack_grads(layer, gw, gb, pay):
    third = jnp.concatenate([gw[:, 256:288], jnp.sum(gb[...], axis=1, keepdims=True), jnp.zeros((CH, 95), f32)], axis=1)
    for og in range(4):
        rows = slice(8 * og, 8 * og + 8)
        for lt in range(2):
            pay[layer * 8 + og * 2 + lt, 0] = gw[rows, 128 * lt : 128 * lt + 128]
    return third


def unpack_grads(res, gw_out, gb_out):
    eye = lax.broadcasted_iota(jnp.int32, (CH, CH), 0) == lax.broadcasted_iota(jnp.int32, (CH, CH), 1)
    third = jnp.concatenate([res[og, 1] for og in range(4)], axis=0)
    for layer in range(2):
        for lt in range(2):
            tile = jnp.concatenate([res[layer * 8 + og * 2 + lt, 0] for og in range(4)], axis=0)
            for n in range(4):
                gw_out[layer, 4 * lt + n] = tile[:, CH * n : CH * n + CH]
        gw_out[layer, 8] = third[:, 64 * layer : 64 * layer + CH]
        column = third[:, 64 * layer + CH : 64 * layer + CH + 1]
        gb_out[layer : layer + 1, :] = jnp.sum(jnp.where(eye, column, 0.0), axis=0, keepdims=True)


def remote(src, dst, send, recv, target):
    return pltpu.make_async_remote_copy(
        src_ref=src, dst_ref=dst, send_sem=send, recv_sem=recv, device_id=target, device_id_type=MESH
    )


def wrap(r, o):
    return (lax.rem(r + 2 * NR, NR), lax.rem(o + NO, NO))


def halo_copies(r, o, a, pl_, pr_, rl, rr, send, recv):
    jobs = [
        (pl_, rl.at[2:18], 0, -1),
        (pr_, rr.at[2:18], 0, 1),
        (a.at[128:144], a.at[0:16], 1, 0),
        (a.at[16:32], a.at[144:160], -1, 0),
        (pl_.at[14:16], rl.at[0:2], 1, -1),
        (pl_.at[0:2], rl.at[18:20], -1, -1),
        (pr_.at[14:16], rr.at[0:2], 1, 1),
        (pr_.at[0:2], rr.at[18:20], -1, 1),
    ]
    return [
        remote(src, dst, send.at[n], recv.at[n], wrap(r + dr, o + do))
        for n, (src, dst, dr, do) in enumerate(jobs)
    ]


def embed_copies(r, o, emb, ec, er, send, recv):
    other = o + 1 - 2 * lax.rem(o, 2)
    copies = [
        remote(emb, ec.at[n], send.at[n - 1], recv.at[n - 1], wrap(r - other - (n - 2), other))
        for n in range(1, 5)
    ]
    copies.append(remote(emb, er.at[0], send.at[4], recv.at[4], wrap(r + 1, o)))
    copies.append(remote(emb, er.at[2], send.at[5], recv.at[5], wrap(r - 1, o)))
    return copies


def greet_exchange(r, o, barrier):
    other = o + 1 - 2 * lax.rem(o, 2)
    targets = [wrap(r + o + n - 2, other) for n in range(1, 5)]
    targets += [wrap(r + dr, o + do) for dr in (-1, 0, 1) for do in (-1, 0, 1) if (dr, do) != (0, 0)]
    for target in targets:
        pl.semaphore_signal(barrier, inc=1, device_id=target, device_id_type=MESH)
    return len(targets)


def lay_rows(cot, a, pl_, pr_):
    def body(it, _):
        block = jnp.swapaxes(cot[:, pl.ds(pl.multiple_of(it * 16, 16), 16), :], 0, 1)
        a[pl.ds(2 * DMAX + it * 16, 16)] = block
        for n in range(2):
            left, right = packed([block[8 * n + w] for w in range(8)])
            pl_[it * 2 + n] = left
            pr_[it * 2 + n] = right
        return 0

    lax.fori_loop(0, 8, body, 0)


def kernel(
    dil, emb_hbm, w_hbm, bias_hbm, cot_hbm, out_hbm, res_hbm, ge_hbm,
    res, ge,    emb, w, bias, cot, out, ec, er, a, rl, rr, pl_, pr_, grl, grr, gpl, gpr, x0, x1, s0, t1, s1, t0, wf, wb, gw, gb,
    pay, terms, wr1, w2, wr2, inbox, shares, win, caps,
    io, esend, erecv, hsend, hrecv, gsend, grecv, sa, ra, sb, rb, sc, rc, st, rt, su, ru, local_sem,
):
    r, o = lax.axis_index("diag"), lax.axis_index("off")
    core, b = lax.rem(r, 2), lax.div(r, 2)
    me = o * 2 + core
    row0, band0 = r * TI, o * TK
    fetches = [
        pltpu.make_async_copy(src, dst, io.at[n])
        for n, (src, dst) in enumerate(((emb_hbm, emb), (w_hbm, w), (bias_hbm, bias), (cot_hbm, cot)))
    ]
    for c in fetches:
        c.start()

    def peer_a(n):
        other = lax.rem(me + n, 16)
        return other, (2 * b + lax.rem(other, 2), lax.div(other, 2))

    def peer_b(n):
        other = lax.rem(b + n, 16)
        return other, (2 * other + core, o)

    barrier = pltpu.get_barrier_semaphore()

    def greet(target):
        pl.semaphore_signal(barrier, inc=1, device_id=target, device_id_type=MESH)

    count = greet_exchange(r, o, barrier)
    for n in range(1, 16):
        greet(peer_a(n)[1])
        greet(peer_b(n)[1])
    greet(wrap(r - o - 1, o))

    @pl.when(o > 0)
    def _():
        greet(wrap(r - o, o))

    count = count + 30 + 1 + jnp.minimum(o, 1)
    ec[0] = jnp.zeros((CH, 128), bf16)
    ec[5] = jnp.zeros((CH, 128), bf16)
    d0, d1 = dil[0], dil[1]
    lane_caps(band0, d0, caps)
    for c in fetches:
        c.wait()
    er[1] = emb[...]
    place_weights(w, wf, wb)
    lay_rows(cot, a, pl_, pr_)
    pl.semaphore_wait(barrier, count)
    ecopies = embed_copies(r, o, emb, ec, er, esend, erecv)
    hcopies = halo_copies(r, o, a, pl_, pr_, rl, rr, hsend, hrecv)
    for c in ecopies + hcopies:
        c.start()

    eye = lax.broadcasted_iota(jnp.int32, (CH, CH), 0) == lax.broadcasted_iota(jnp.int32, (CH, CH), 1)

    def column(layer):
        return jnp.sum(jnp.where(eye, bias[layer : layer + 1, :], 0.0), axis=1, keepdims=True)

    phase_own_shifts(row0, band0, d1, a, t1)
    for c in ecopies:
        c.wait_recv()
    bounded_blocks(r, o, ec, er)
    phase_windows(ec, win)
    phase_x0(d0, er, win, caps, x0, s0)
    phase_x1(row0, band0, d0, d1, wf[0], column(0), x0, s0, x1, s1, 48)
    for c in hcopies:
        c.wait_recv()
    phase_rim_shifts(row0, band0, d1, a, t1)
    phase_patch(row0, band0, d1, 2 * DMAX, H2 // 8, rl, rr, t1, 5)

    def edge_copies(it):
        part = pl.ds(it * 6, 6)
        return (
            remote(gpl.at[part], grl.at[part], gsend.at[it], grecv.at[it], wrap(r, o - 1)),
            remote(gpr.at[part], grr.at[part], gsend.at[3 + it], grecv.at[3 + it], wrap(r, o + 1)),
        )

    def send_chunk(it):
        for c in edge_copies(it):
            c.start()

    phase_g1(d1, d0, wb[1], x1, t1, t0, gpl, gpr, send_chunk)
    gcopies = [c for n in range(3) for c in edge_copies(n)]
    phase_gw(lambda i: t1[i + 2 * DMAX, 64:96, :], s1, DMAX, d1, gw, gb)
    third1 = pack_grads(1, gw, gb, pay)
    phase_gw(lambda i: t0[i + DMAX, 64:96, :], s0, 2 * DMAX, d0, gw, gb)
    third0 = pack_grads(0, gw, gb, pay)
    rest = third0 + pltpu.roll(third1, 64, 1)
    for n in range(16):
        pay[n, 1] = rest[8 * n : 8 * n + 8] if n < 4 else jnp.zeros((8, 128), f32)

    first = [remote(pay.at[other], wr1.at[me], sa.at[n], ra.at[me], target)
             for n in range(1, 16) for other, target in [peer_a(n)]]
    for c in first:
        c.start()

    for c in gcopies:
        c.wait_recv()
    phase_patch(row0, band0, d0, DMAX, H1 // 8, grl, grr, t0, 6)

    def arrived(dst, sem):
        pltpu.make_async_copy(dst, dst, sem).wait()

    def total(buf):
        acc = buf[0]
        for n in range(1, 16):
            acc = acc + buf[n]
        return acc

    wr1[me] = pay[me]
    for n in range(1, 16):
        other, _t = peer_a(n)
        arrived(wr1.at[other], ra.at[other])
    w2[...] = total(wr1)
    second = [remote(w2, wr2.at[b], sb.at[n], rb.at[b], target)
              for n in range(1, 16) for other, target in [peer_b(n)]]
    for c in second:
        c.start()

    zero = jnp.zeros((CH, TI), f32)
    rsum, lo, hi = phase_g0(d0, wb[0], s0, t0, 0, 128, (zero, zero, zero))
    terms[0] = lo
    terms[1] = hi
    low = remote(terms.at[0], inbox.at[0], st.at[0], rt.at[0], wrap(r + o, o))
    high = remote(terms.at[1], inbox.at[1], st.at[1], rt.at[1], wrap(r + o + 1, o))
    high.start()
    local = pltpu.make_async_copy(terms.at[0], inbox.at[0], local_sem)

    @pl.when(o > 0)
    def _():
        low.start()

    @pl.when(o == 0)
    def _():
        local.start()

    phase_x2(row0, band0, d1, wf[1], column(1), x1, s1, out, 64)
    write = pltpu.make_async_copy(out, out_hbm, io.at[4])
    write.start()

    @pl.when(o > 0)
    def _():
        low.wait_recv()

    @pl.when(o == 0)
    def _():
        local.wait()

    high.wait_recv()
    shares[o] = rsum + inbox[0] + inbox[1]
    eall = [remote(shares.at[o], shares.at[o], su.at[n], ru.at[o], wrap(r, o + n)) for n in range(1, 8)]
    for c in eall:
        c.start()

    wr2[b] = w2[...]
    for n in range(1, 16):
        other, _t = peer_b(n)
        arrived(wr2.at[other], rb.at[other])
    res[me] = total(wr2)
    third = [remote(res.at[me], res.at[me], sc.at[n], rc.at[me], target)
             for n in range(1, 16) for other, target in [peer_a(n)]]
    for c in third:
        c.start()
    for n in range(1, 8):
        oo = lax.rem(o + n, 8)
        arrived(shares.at[oo], ru.at[oo])
    acc = shares[0]
    for n in range(1, 8):
        acc = acc + shares[n]
    ge[...] = acc
    write_ge = pltpu.make_async_copy(ge, ge_hbm, io.at[5])
    write_ge.start()
    for n in range(1, 16):
        other, _t = peer_a(n)
        arrived(res.at[other], rc.at[other])
    write_res = pltpu.make_async_copy(res, res_hbm, io.at[6])
    write_res.start()
    for c in first + second + third + [high] + eall + ecopies + hcopies + gcopies:
        c.wait_send()

    @pl.when(o > 0)
    def _():
        low.wait_send()

    for c in (write, write_ge, write_res):
        c.wait()


def finish(section, res, ge, out, gw_out, gb_out, ge_out, held, rv, gv, gwv, gbv, come, go):
    size = CH // 4
    parts = [slice(n * size, n * size + size) for n in range(4)]
    ins = [pltpu.make_async_copy(section.at[p], held.at[p], come.at[n]) for n, p in enumerate(parts)]
    outs = [pltpu.make_async_copy(held.at[p], out.at[p], go.at[n]) for n, p in enumerate(parts)]
    res_in = pltpu.make_async_copy(res, rv, come.at[4])
    ge_in = pltpu.make_async_copy(ge, gv, come.at[5])
    for c in [res_in, ge_in] + ins:
        c.start()
    small = [
        pltpu.make_async_copy(src, dst, go.at[4 + n])
        for n, (src, dst) in enumerate(((gwv, gw_out), (gbv, gb_out), (gv, ge_out)))
    ]
    res_in.wait()
    unpack_grads(rv, gwv, gbv)
    ge_in.wait()
    for c in small:
        c.start()
    for n in range(4):
        ins[n].wait()
        outs[n].start()
    for c in outs + small:
        c.wait()


def per_device(bin_embed, weights, biases, dilations, cotangent):
    vmem = pl.BlockSpec(memory_space=pltpu.VMEM)
    smem = pl.BlockSpec(memory_space=pltpu.SMEM)
    hbm = pl.BlockSpec(memory_space=pl.ANY)
    shape = jax.ShapeDtypeStruct
    dma = pltpu.SemaphoreType.DMA
    mem = pltpu.VMEM
    halo = [mem((H2, CH, 128), bf16), mem((20, CH, 128), bf16), mem((20, CH, 128), bf16),
            mem((16, CH, 128), bf16), mem((16, CH, 128), bf16)]
    edge = [mem((18, CH, 128), bf16)] * 4
    section, res, ge = pl.pallas_call(
        kernel,
        out_shape=[shape((CH, TI, TK), bf16), shape((16, 2, 8, 128), f32), shape((CH, TI), f32)],
        in_specs=[smem, hbm, hbm, hbm, hbm],
        out_specs=[hbm, hbm, hbm],
        scratch_shapes=[
            mem((16, 2, 8, 128), f32), mem((CH, TI), f32),
            mem((CH, TI), bf16), mem((2, 9, CH, CH), bf16), mem((2, CH), f32),
            mem((CH, TI, TK), bf16), mem((CH, TI, TK), bf16),
            mem((6, CH, 128), bf16), mem((3, CH, 128), bf16), *halo, *edge,
            mem((H2, CH, 256), bf16), mem((H1, CH, 256), bf16),
            mem((H2, 5 * CH, 256), bf16), mem((H2, 5 * CH, 128), bf16),
            mem((H1, 5 * CH, 128), bf16), mem((H1, 5 * CH, 128), bf16),
            mem((2, CH, 9 * CH), bf16), mem((2, CH, 9 * CH), bf16),
            mem((CH, 9 * CH), f32), mem((CH, 128), f32),
            mem((16, 2, 8, 128), f32), mem((2, CH, TI), f32),
            mem((16, 2, 8, 128), f32), mem((2, 8, 128), f32),
            mem((16, 2, 8, 128), f32), mem((2, CH, TI), f32), mem((8, CH, TI), f32),
            mem((H2 + 4 * DMAX, CH, 256), bf16), mem((10, CH, 128), bf16),
            dma((7,)), dma((6,)), dma((6,)), dma((8,)), dma((8,)), dma((6,)), dma((6,)),
            dma((16,)), dma((16,)), dma((16,)), dma((16,)), dma((16,)), dma((16,)),
            dma((2,)), dma((2,)), dma((8,)), dma((8,)), dma,
        ],
        compiler_params=pltpu.CompilerParams(collective_id=0, has_side_effects=True, vmem_limit_bytes=60 << 20),
        name="section",
    )(dilations, bin_embed, weights, biases, cotangent)
    out, gw, gb, ge_out = pl.pallas_call(
        finish,
        out_shape=[shape((CH, TI, TK), bf16), shape((2, 9, CH, CH), f32), shape((2, CH), f32), shape((CH, TI), f32)],
        in_specs=[hbm] * 3,
        out_specs=[hbm] * 4,
        scratch_shapes=[mem((CH, TI, TK), bf16), mem((16, 2, 8, 128), f32), mem((CH, TI), f32),
                        mem((2, 9, CH, CH), f32), mem((2, CH), f32), dma((6,)), dma((7,))],
        name="finish",
    )(section, res, ge)
    return out, gw, gb, ge_out


def solution(mesh):
    placed = (P(None, "diag"), P(), P(), P(), P(None, "diag", "off"))
    return jax.shard_map(
        per_device,
        mesh=mesh,
        in_specs=placed,
        out_specs=(P(None, "diag", "off"), P(), P(), P(None, "diag")),
        check_vma=False,
    )
```

```python
import jax
import jax.numpy as jnp
from jax import lax
from jax.experimental import pallas as pl
from jax.experimental.pallas import tpu as pltpu
from jax.sharding import PartitionSpec as P

DMAX = 8
CH = 32
TI = 128
TK = 128
H1 = TI + 2 * DMAX
H2 = TI + 4 * DMAX
NBINS = 4096
KBAND = 1024
bf16 = jnp.bfloat16
f32 = jnp.float32
NT = (((1,), (1,)), ((), ()))


def lanes(n=1):
    return lax.broadcasted_iota(jnp.int32, (CH, 128), 1)


def level(value):
    return jnp.full((CH, 128), value.astype(f32)).astype(bf16)


def in_range(s, d):
    p = lanes().astype(bf16)
    return p < level(128 - s * d) if s > 0 else p >= level(-s * d)


def turned(x, amount):
    return pltpu.roll(x, lax.rem(256 - amount, 128), 1)


def shift_pair(a, b, amount, inside, both=True):
    ra, rb = turned(a, amount), turned(b, amount)
    out_a = jnp.where(inside, ra, rb)
    if not both:
        return out_a
    return out_a, jnp.where(inside, rb, ra)


def row_masks(row0, band0, i):
    p = lanes()
    row = row0 + i
    ka = band0 + p
    kb = band0 + jnp.where(p < 64, p + 128, p - 128)
    live = (row >= 0)
    ma = (ka < NBINS - row) & live
    mb = (kb < NBINS - row) & (kb >= 0) & (kb < KBAND) & live
    return ma, mb


def store_shifts(dst, i, a, b, amounts, insides, both=True):
    for n, s in enumerate((-2, -1, 0, 1, 2)):
        rows = slice(CH * n, CH * (n + 1))
        if s == 0:
            dst[i, rows, 0:128] = a
            if both:
                dst[i, rows, 128:256] = b
        elif both:
            sa, sb = shift_pair(a, b, amounts[n], insides[n])
            dst[i, rows, 0:128] = sa
            dst[i, rows, 128:256] = sb
        else:
            dst[i, rows, 0:128] = shift_pair(a, b, amounts[n], insides[n], False)


def taps(src, i, d, lo=0, hi=256):
    return jnp.concatenate(
        [src[i - d, 64:160, lo:hi], src[i, 32:128, lo:hi], src[i + d, 0:96, lo:hi]], axis=0
    )


def shift_tables(d):
    amounts = [s * d for s in (-2, -1, 0, 1, 2)]
    return amounts, [in_range(s, d) for s in (-2, -1, 0, 1, 2)]


LOW = -1e38


def bounded_blocks(r, o, ec, er):
    for n in range(1, 5):
        ec[n] = jnp.where(r + o + n - 2 < NBINS // TI, ec[n], LOW)
    for n in (0, 2):
        ec_row = r + n - 1
        er[n] = jnp.where((ec_row >= 0) & (ec_row < NBINS // TI), er[n], LOW)


def rim_lane():
    t = lax.rem(lanes(), 32)
    return jnp.where(t < 16, t - 16, t + 112)


def lane_caps(band0, d, caps):
    for n, s in enumerate((-2, -1, 0, 1, 2)):
        for rim in range(2):
            k = band0 + s * d + (rim_lane() if rim else lanes())
            caps[2 * n + rim] = jnp.where((k >= 0) & (k < KBAND), 3e38, 0.0).astype(bf16)


def phase_windows(ec, win, unroll=32):
    u = lanes()
    ub = u.astype(bf16)

    def body(it, _):
        m0 = it * unroll - 4 * DMAX
        q = lax.div(m0 + 128, 128) - 1
        t0 = m0 - 128 * q
        prev, here, after, later = (ec[q + 1 + n] for n in range(4))
        high = jnp.where((u >= 64) & (t0 < 32), prev, after)
        low = jnp.where((u < 64) & (t0 >= 96), later, here)
        for w in range(unroll):
            t = t0 + w
            beyond = ub >= level(t)
            back = lax.rem(128 - t, 128)
            win[it * unroll + w, :, 0:128] = pltpu.roll(jnp.where(beyond, here, after), back, 1)
            win[it * unroll + w, :, 128:256] = pltpu.roll(jnp.where(beyond, high, low), back, 1)
        return 0

    lax.fori_loop(0, (H2 + 4 * DMAX) // unroll, body, 0)


def four_groups(rows):
    p = lanes()
    low = jnp.where(p < 32, rows[0], rows[1])
    high = jnp.where(p < 96, rows[2], rows[3])
    return jnp.where(p < 64, low, high)


def phase_rim_windows(win, rwin, unroll=12):
    def body(it, _):
        for w in range(unroll):
            n = it * unroll + w
            rwin[n] = four_groups(
                [pltpu.roll(win[36 * q + n, :, 128:256], (32 * q + 16) % 128, 1) for q in range(4)]
            )
        return 0

    lax.fori_loop(0, 84 // unroll, body, 0)


def phase_x0(d, er, win, caps, x0, s0, owns, unroll=16):
    def body(it, _):
        i0 = it * unroll - 2 * DMAX
        q = lax.div(i0 + 128, 128) - 1
        block = pltpu.roll(er[q + 1], lax.rem(256 - (i0 - 128 * q), 128), 1)
        for w in range(unroll):
            j = it * unroll + w
            own = jnp.broadcast_to(block[:, w : w + 1], (CH, 128))
            owns[j] = own
            for n, s in enumerate((-2, -1, 0, 1, 2)):
                v = own + win[j + 2 * DMAX + s * d, :, 0:128]
                if s == 0:
                    x0[j] = v
                s0[j, CH * n : CH * n + CH, :] = jnp.minimum(jnp.maximum(v, 0), caps[2 * n])
        return 0

    lax.fori_loop(0, H2 // unroll, body, 0)


def phase_rim_x0(d, rwin, owns, caps, rx0, rs0, unroll=13):
    def body(it, _):
        for w in range(unroll):
            j = it * unroll + w
            own = four_groups([owns[36 * q + j] for q in range(4)])
            for n, s in enumerate((-2, -1, 0, 1, 2)):
                v = own + rwin[j + 2 * DMAX + s * d]
                if s == 0:
                    rx0[j] = v
                rs0[j, CH * n : CH * n + CH, :] = jnp.minimum(jnp.maximum(v, 0), caps[2 * n + 1])
        return 0

    lax.fori_loop(0, 52 // unroll, body, 0)


def phase_rim_x1(row0, band0, d, wf, bias, rx0, rs0, rx1, unroll=36):
    bias = jnp.broadcast_to(bias, (CH, 128))
    k = band0 + rim_lane()
    across = (k >= 0) & (k < KBAND)

    def body(it, _):
        for w in range(0, unroll, 2):
            j = it * unroll + w
            x = jnp.concatenate([taps(rs0, j + DMAX, d, 0, 128), taps(rs0, j + DMAX + 1, d, 0, 128)], axis=1)
            conv = jnp.dot(wf, x, preferred_element_type=f32)
            for z in range(2):
                row = row0 + 36 * lax.div(lanes(), 32) + (j + z - DMAX)
                v = rx0[j + z + DMAX].astype(f32) + conv[:, 128 * z : 128 * z + 128] + bias
                live = across & (row >= 0) & (k < NBINS - row)
                rx1[j + z] = jnp.where(live, jnp.maximum(v, 0.0), 0.0).astype(bf16)
        return 0

    lax.fori_loop(0, 36 // unroll, body, 0)


def phase_x1(row0, band0, d, dn, wf, bias, x0, s0, rx1, x1, s1):
    insides = inside_masks(dn)
    bias = jnp.broadcast_to(bias, (CH, 128))
    lane = lanes()

    def body(it, _):
        for w in range(0, 36, 2):
            j = it * 36 + w
            jj = j + DMAX
            x = jnp.concatenate([taps(s0, jj, d, 0, 128), taps(s0, jj + 1, d, 0, 128)], axis=1)
            conv = jnp.dot(wf, x, preferred_element_type=f32)
            for z in range(2):
                row = row0 + j + z - DMAX
                live = (row >= 0) & (band0 + lane < NBINS - row)
                a = x0[jj + z].astype(f32) + conv[:, 128 * z : 128 * z + 128] + bias
                a = jnp.where(live, a, 0.0).astype(bf16)
                x1[j + z] = a
                a = jnp.maximum(a, 0)
                s1[j + z, block_of(2), :] = a
                rim = rx1[w + z]
                for n, (m, s) in enumerate(SHIFTS):
                    side = pltpu.roll(rim, lax.rem(384 + 112 - 32 * it - s * dn, 128), 1)
                    s1[j + z, block_of(m), :] = jnp.where(insides[n], rolled(a, s, dn), side)
        return 0

    lax.fori_loop(0, 4, body, 0)


def phase_x2(row0, band0, d, wf, bias, x1, s1, out, unroll=16):
    bias = jnp.broadcast_to(bias, (CH, 128))

    def body(it, _):
        rows = []
        for w in range(0, unroll, 2):
            i = it * unroll + w
            j = i + DMAX
            x = jnp.concatenate([taps(s1, j, d, 0, 128), taps(s1, j + 1, d, 0, 128)], axis=1)
            conv = jnp.dot(wf, x, preferred_element_type=f32)
            for z in range(2):
                ma, _mb = row_masks(row0, band0, i + z)
                a = x1[j + z].astype(f32) + conv[:, 128 * z : 128 * z + 128] + bias
                rows.append(jnp.where(ma, a, 0.0).astype(bf16))
        out[:, pl.ds(pl.multiple_of(it * unroll, unroll), unroll), :] = jnp.swapaxes(jnp.stack(rows), 0, 1)
        return 0

    lax.fori_loop(0, TI // unroll, body, 0)


def phase_gw(h, s, soff, d, gw, gb, unroll=64):
    def body(it, carry):
        acc, accb = carry
        for w in range(0, unroll, 2):
            i = it * unroll + w
            x = jnp.concatenate(
                [taps(s, i + soff, d, 0, 128), taps(s, i + 1 + soff, d, 0, 128)], axis=1
            )
            ha, hb = h(i), h(i + 1)
            hh = jnp.concatenate([ha, hb], axis=1)
            acc = acc + lax.dot_general(hh, x, NT, preferred_element_type=f32)
            accb = accb + (ha.astype(f32) + hb.astype(f32))
        return acc, accb

    acc, accb = lax.fori_loop(
        0, TI // unroll, body, (jnp.zeros((CH, 9 * CH), f32), jnp.zeros((CH, 128), f32))
    )
    gw[...] = acc
    gb[...] = accb


def packed(rows):
    lane = lanes()
    left, right = rows[0], rows[7]
    for w in range(1, 8):
        left = jnp.where(lane < 16 * w, left, pltpu.roll(rows[w], 16 * w, 1))
    for w in range(6, -1, -1):
        right = jnp.where(lane >= 16 * (w + 1), right, pltpu.roll(rows[w], 16 * w + 16, 1))
    return left, right


SHIFTS = ((0, -2), (1, -1), (3, 1), (4, 2))


def block_of(n):
    return slice(CH * n, CH * n + CH)


def rolled(x, s, d):
    return pltpu.roll(x, lax.rem(256 - s * d, 128), 1)


def halo_sides(row0, band0, depth, group, rl, rr):
    lane = lanes()
    row = row0 + group * 8 - depth + lax.div(lane, 16)
    kr = band0 + 128 + lax.rem(lane, 16)
    kl = band0 - 16 + lax.rem(lane, 16)
    right = jnp.where((row >= 0) & (kr < KBAND) & (kr < NBINS - row), rl[group], 0)
    left = jnp.where((row >= 0) & (kl >= 0) & (kl < NBINS - row), rr[group], 0)
    return right, left


def side_of(right, left, w, s, d):
    if s > 0:
        return pltpu.roll(right, lax.rem(256 - 16 * w - s * d, 128), 1)
    return pltpu.roll(left, lax.rem(256 + 16 * (7 - w) - s * d, 128), 1)


def put_row(row0, band0, d, depth, j, a, dst):
    row = row0 + j - depth
    live = (row >= 0) & (band0 + lanes() < NBINS - row)
    a = jnp.where(live, a, 0)
    dst[j, block_of(2), :] = a
    for m, s in SHIFTS:
        dst[j, block_of(m), :] = rolled(a, s, d)


def patch_group(row0, band0, d, depth, group, insides, rl, rr, dst):
    right, left = halo_sides(row0, band0, depth, group, rl, rr)
    for w in range(8):
        j = group * 8 + w
        for n, (m, s) in enumerate(SHIFTS):
            dst[j, block_of(m), :] = jnp.where(
                insides[n], dst[j, block_of(m), :], side_of(right, left, w, s, d)
            )


def inside_masks(d):
    return [in_range(s, d) for _m, s in SHIFTS]


def phase_patch(row0, band0, d, depth, groups, rl, rr, dst, unroll):
    insides = inside_masks(d)

    def body(it, _):
        for g in range(unroll):
            patch_group(row0, band0, d, depth, it * unroll + g, insides, rl, rr, dst)
        return 0

    lax.fori_loop(0, groups // unroll, body, 0)


def phase_own_shifts(row0, band0, d, a, dst, unroll=32):
    def body(it, _):
        for w in range(unroll):
            j = 2 * DMAX + it * unroll + w
            put_row(row0, band0, d, 2 * DMAX, j, a[j], dst)
        return 0

    lax.fori_loop(0, TI // unroll, body, 0)


def phase_rim_shifts(row0, band0, d, a, dst):
    def body(it, _):
        for w in range(16):
            j = it * 144 + w
            put_row(row0, band0, d, 2 * DMAX, j, a[j], dst)
        return 0

    lax.fori_loop(0, 2, body, 0)


def phase_g1(d, dn, wb, x1, t1, t0, gpl, gpr, send_chunk, unroll=48):
    def body(it, _):
        rows = []
        for w in range(0, unroll, 2):
            j = it * unroll + w
            x = jnp.concatenate([taps(t1, j + DMAX, d, 0, 128), taps(t1, j + DMAX + 1, d, 0, 128)], axis=1)
            q = jnp.dot(wb, x, preferred_element_type=f32)
            for z in range(2):
                h = t1[j + DMAX + z, 64:96, :].astype(f32)
                gate = x1[j + z].astype(f32) > 0
                g = (h + jnp.where(gate, q[:, 128 * z : 128 * z + 128], 0.0)).astype(bf16)
                rows.append(g)
        for n in range(unroll // 8):
            left, right = packed(rows[8 * n : 8 * n + 8])
            gpl[it * (unroll // 8) + n] = left
            gpr[it * (unroll // 8) + n] = right
        send_chunk(it)
        for w, g in enumerate(rows):
            j = it * unroll + w
            t0[j, block_of(2), :] = g
            for m, s in SHIFTS:
                t0[j, block_of(m), :] = rolled(g, s, dn)
        return 0

    lax.fori_loop(0, H1 // unroll, body, 0)


def phase_g0(d, wb, s0, t0, begin, end, carry, unroll=32):
    lane = lanes()
    ones = jnp.ones((128, 128), bf16)

    def body(it, carry):
        rsum, lo, hi = carry
        rows = []
        for w in range(0, unroll, 2):
            i = it * unroll + w
            j = i + DMAX
            x = jnp.concatenate([taps(t0, j, d, 0, 128), taps(t0, j + 1, d, 0, 128)], axis=1)
            q = jnp.dot(wb, x, preferred_element_type=f32)
            for z in range(2):
                g1 = t0[j + z, 64:96, 0:128].astype(f32)
                gate = s0[j + z + DMAX, 64:96, 0:128].astype(f32) > 0
                gp = (g1 + jnp.where(gate, q[:, 128 * z : 128 * z + 128], 0.0)).astype(bf16)
                rows.append(gp)
                moved = pltpu.roll(gp, i + z, 1).astype(f32)
                low = jnp.where(lane >= i + z, moved, 0.0)
                lo = lo + low
                hi = hi + (moved - low)
        sums = jnp.dot(jnp.concatenate(rows, axis=0), ones, preferred_element_type=f32)
        for w in range(unroll):
            rsum = jnp.where(lane == it * unroll + w, sums[CH * w : CH * w + CH], rsum)
        return rsum, lo, hi

    return lax.fori_loop(begin // unroll, end // unroll, body, carry)
MESH = pl.DeviceIdType.MESH
NR, NO = 32, 8


def place_weights(w, wf, wb):
    row = lax.broadcasted_iota(jnp.int32, (CH, 9 * CH), 0)
    col = lax.broadcasted_iota(jnp.int32, (CH, 9 * CH), 1)
    for layer in range(2):
        fwd = jnp.zeros((CH, 9 * CH), f32)
        bwd = jnp.zeros((CH, 9 * CH), f32)
        for t in range(9):
            spot = jnp.where(col == row + CH * t, 1.0, 0.0).astype(bf16)
            fwd = fwd + jnp.dot(w[layer, t], spot, preferred_element_type=f32)
            bwd = bwd + lax.dot_general(
                w[layer, 8 - t], spot, (((0,), (0,)), ((), ())), preferred_element_type=f32
            )
        wf[layer] = fwd.astype(bf16)
        wb[layer] = bwd.astype(bf16)


def pack_grads(layer, gw, gb, pay):
    third = jnp.concatenate([gw[:, 256:288], jnp.sum(gb[...], axis=1, keepdims=True), jnp.zeros((CH, 95), f32)], axis=1)
    for og in range(4):
        rows = slice(8 * og, 8 * og + 8)
        for lt in range(2):
            pay[layer * 8 + og * 2 + lt, 0] = gw[rows, 128 * lt : 128 * lt + 128]
    return third


def unpack_grads(res, gw_out, gb_out):
    eye = lax.broadcasted_iota(jnp.int32, (CH, CH), 0) == lax.broadcasted_iota(jnp.int32, (CH, CH), 1)
    third = jnp.concatenate([res[og, 1] for og in range(4)], axis=0)
    for layer in range(2):
        for lt in range(2):
            tile = jnp.concatenate([res[layer * 8 + og * 2 + lt, 0] for og in range(4)], axis=0)
            for n in range(4):
                gw_out[layer, 4 * lt + n] = tile[:, CH * n : CH * n + CH]
        gw_out[layer, 8] = third[:, 64 * layer : 64 * layer + CH]
        column = third[:, 64 * layer + CH : 64 * layer + CH + 1]
        gb_out[layer : layer + 1, :] = jnp.sum(jnp.where(eye, column, 0.0), axis=0, keepdims=True)


def remote(src, dst, send, recv, target):
    return pltpu.make_async_remote_copy(
        src_ref=src, dst_ref=dst, send_sem=send, recv_sem=recv, device_id=target, device_id_type=MESH
    )


def wrap(r, o):
    return (lax.rem(r + 2 * NR, NR), lax.rem(o + NO, NO))


def halo_copies(r, o, a, pl_, pr_, rl, rr, send, recv):
    jobs = [
        (pl_, rl.at[2:18], 0, -1),
        (pr_, rr.at[2:18], 0, 1),
        (a.at[128:144], a.at[0:16], 1, 0),
        (a.at[16:32], a.at[144:160], -1, 0),
        (pl_.at[14:16], rl.at[0:2], 1, -1),
        (pl_.at[0:2], rl.at[18:20], -1, -1),
        (pr_.at[14:16], rr.at[0:2], 1, 1),
        (pr_.at[0:2], rr.at[18:20], -1, 1),
    ]
    return [
        remote(src, dst, send.at[n], recv.at[n], wrap(r + dr, o + do))
        for n, (src, dst, dr, do) in enumerate(jobs)
    ]


def embed_copies(r, o, emb, ec, er, send, recv):
    other = o + 1 - 2 * lax.rem(o, 2)
    copies = [
        remote(emb, ec.at[n], send.at[n - 1], recv.at[n - 1], wrap(r - other - (n - 2), other))
        for n in range(1, 5)
    ]
    copies.append(remote(emb, er.at[0], send.at[4], recv.at[4], wrap(r + 1, o)))
    copies.append(remote(emb, er.at[2], send.at[5], recv.at[5], wrap(r - 1, o)))
    return copies


def greet_exchange(r, o, barrier):
    other = o + 1 - 2 * lax.rem(o, 2)
    targets = [wrap(r + o + n - 2, other) for n in range(1, 5)]
    targets += [wrap(r + dr, o + do) for dr in (-1, 0, 1) for do in (-1, 0, 1) if (dr, do) != (0, 0)]
    for target in targets:
        pl.semaphore_signal(barrier, inc=1, device_id=target, device_id_type=MESH)
    return len(targets)


def lay_rows(cot, a, pl_, pr_):
    def body(it, _):
        block = jnp.swapaxes(cot[:, pl.ds(pl.multiple_of(it * 16, 16), 16), :], 0, 1)
        a[pl.ds(2 * DMAX + it * 16, 16)] = block
        for n in range(2):
            left, right = packed([block[8 * n + w] for w in range(8)])
            pl_[it * 2 + n] = left
            pr_[it * 2 + n] = right
        return 0

    lax.fori_loop(0, 8, body, 0)


def kernel(
    dil, emb_hbm, w_hbm, bias_hbm, cot_hbm, out_hbm, res_hbm, ge_hbm,
    res, ge,    emb, w, bias, cot, out, ec, er, a, rl, rr, pl_, pr_, grl, grr, gpl, gpr, x0, x1, s0, t1, s1, t0, wf, wb, gw, gb,
    pay, terms, wr1, w2, wr2, inbox, shares, win, caps, rwin, owns, rx0, rs0, rx1,
    io, esend, erecv, hsend, hrecv, gsend, grecv, sa, ra, sb, rb, sc, rc, st, rt, su, ru, local_sem,
):
    r, o = lax.axis_index("diag"), lax.axis_index("off")
    core, b = lax.rem(r, 2), lax.div(r, 2)
    me = o * 2 + core
    row0, band0 = r * TI, o * TK
    fetches = [
        pltpu.make_async_copy(src, dst, io.at[n])
        for n, (src, dst) in enumerate(((emb_hbm, emb), (w_hbm, w), (bias_hbm, bias), (cot_hbm, cot)))
    ]
    for c in fetches:
        c.start()

    def peer_a(n):
        other = lax.rem(me + n, 16)
        return other, (2 * b + lax.rem(other, 2), lax.div(other, 2))

    def peer_b(n):
        other = lax.rem(b + n, 16)
        return other, (2 * other + core, o)

    barrier = pltpu.get_barrier_semaphore()

    def greet(target):
        pl.semaphore_signal(barrier, inc=1, device_id=target, device_id_type=MESH)

    count = greet_exchange(r, o, barrier)
    for n in range(1, 16):
        greet(peer_a(n)[1])
        greet(peer_b(n)[1])
    greet(wrap(r - o - 1, o))

    @pl.when(o > 0)
    def _():
        greet(wrap(r - o, o))

    count = count + 30 + 1 + jnp.minimum(o, 1)
    ec[0] = jnp.zeros((CH, 128), bf16)
    ec[5] = jnp.zeros((CH, 128), bf16)
    d0, d1 = dil[0], dil[1]
    lane_caps(band0, d0, caps)
    for c in fetches:
        c.wait()
    er[1] = emb[...]
    place_weights(w, wf, wb)
    lay_rows(cot, a, pl_, pr_)
    pl.semaphore_wait(barrier, count)
    ecopies = embed_copies(r, o, emb, ec, er, esend, erecv)
    hcopies = halo_copies(r, o, a, pl_, pr_, rl, rr, hsend, hrecv)
    for c in ecopies + hcopies:
        c.start()

    eye = lax.broadcasted_iota(jnp.int32, (CH, CH), 0) == lax.broadcasted_iota(jnp.int32, (CH, CH), 1)

    def column(layer):
        return jnp.sum(jnp.where(eye, bias[layer : layer + 1, :], 0.0), axis=1, keepdims=True)

    phase_own_shifts(row0, band0, d1, a, t1)
    for c in ecopies:
        c.wait_recv()
    bounded_blocks(r, o, ec, er)
    phase_windows(ec, win)
    phase_rim_windows(win, rwin)
    phase_x0(d0, er, win, caps, x0, s0, owns)
    phase_rim_x0(d0, rwin, owns, caps, rx0, rs0)
    phase_rim_x1(row0, band0, d0, wf[0], column(0), rx0, rs0, rx1)
    phase_x1(row0, band0, d0, d1, wf[0], column(0), x0, s0, rx1, x1, s1)
    for c in hcopies:
        c.wait_recv()
    phase_rim_shifts(row0, band0, d1, a, t1)
    phase_patch(row0, band0, d1, 2 * DMAX, H2 // 8, rl, rr, t1, 5)

    def edge_copies(it):
        part = pl.ds(it * 6, 6)
        return (
            remote(gpl.at[part], grl.at[part], gsend.at[it], grecv.at[it], wrap(r, o - 1)),
            remote(gpr.at[part], grr.at[part], gsend.at[3 + it], grecv.at[3 + it], wrap(r, o + 1)),
        )

    def send_chunk(it):
        for c in edge_copies(it):
            c.start()

    phase_g1(d1, d0, wb[1], x1, t1, t0, gpl, gpr, send_chunk)
    gcopies = [c for n in range(3) for c in edge_copies(n)]
    phase_gw(lambda i: t1[i + 2 * DMAX, 64:96, :], s1, DMAX, d1, gw, gb)
    third1 = pack_grads(1, gw, gb, pay)
    phase_gw(lambda i: t0[i + DMAX, 64:96, :], s0, 2 * DMAX, d0, gw, gb)
    third0 = pack_grads(0, gw, gb, pay)
    rest = third0 + pltpu.roll(third1, 64, 1)
    for n in range(16):
        pay[n, 1] = rest[8 * n : 8 * n + 8] if n < 4 else jnp.zeros((8, 128), f32)

    first = [remote(pay.at[other], wr1.at[me], sa.at[n], ra.at[me], target)
             for n in range(1, 16) for other, target in [peer_a(n)]]
    for c in first:
        c.start()

    for c in gcopies:
        c.wait_recv()
    phase_patch(row0, band0, d0, DMAX, H1 // 8, grl, grr, t0, 6)

    def arrived(dst, sem):
        pltpu.make_async_copy(dst, dst, sem).wait()

    def total(buf):
        acc = buf[0]
        for n in range(1, 16):
            acc = acc + buf[n]
        return acc

    zero = jnp.zeros((CH, TI), f32)
    sums = phase_g0(d0, wb[0], s0, t0, 0, 64, (zero, zero, zero))
    wr1[me] = pay[me]
    for n in range(1, 16):
        other, _t = peer_a(n)
        arrived(wr1.at[other], ra.at[other])
    w2[...] = total(wr1)
    second = [remote(w2, wr2.at[b], sb.at[n], rb.at[b], target)
              for n in range(1, 16) for other, target in [peer_b(n)]]
    for c in second:
        c.start()

    rsum, lo, hi = phase_g0(d0, wb[0], s0, t0, 64, 128, sums)
    terms[0] = lo
    terms[1] = hi
    low = remote(terms.at[0], inbox.at[0], st.at[0], rt.at[0], wrap(r + o, o))
    high = remote(terms.at[1], inbox.at[1], st.at[1], rt.at[1], wrap(r + o + 1, o))
    high.start()
    local = pltpu.make_async_copy(terms.at[0], inbox.at[0], local_sem)

    @pl.when(o > 0)
    def _():
        low.start()

    @pl.when(o == 0)
    def _():
        local.start()

    phase_x2(row0, band0, d1, wf[1], column(1), x1, s1, out, 64)
    write = pltpu.make_async_copy(out, out_hbm, io.at[4])
    write.start()

    @pl.when(o > 0)
    def _():
        low.wait_recv()

    @pl.when(o == 0)
    def _():
        local.wait()

    high.wait_recv()
    shares[o] = rsum + inbox[0] + inbox[1]
    eall = [remote(shares.at[o], shares.at[o], su.at[n], ru.at[o], wrap(r, o + n)) for n in range(1, 8)]
    for c in eall:
        c.start()

    wr2[b] = w2[...]
    for n in range(1, 16):
        other, _t = peer_b(n)
        arrived(wr2.at[other], rb.at[other])
    res[me] = total(wr2)
    third = [remote(res.at[me], res.at[me], sc.at[n], rc.at[me], target)
             for n in range(1, 16) for other, target in [peer_a(n)]]
    for c in third:
        c.start()
    for n in range(1, 8):
        oo = lax.rem(o + n, 8)
        arrived(shares.at[oo], ru.at[oo])
    acc = shares[0]
    for n in range(1, 8):
        acc = acc + shares[n]
    ge[...] = acc
    write_ge = pltpu.make_async_copy(ge, ge_hbm, io.at[5])
    write_ge.start()
    for n in range(1, 16):
        other, _t = peer_a(n)
        arrived(res.at[other], rc.at[other])
    write_res = pltpu.make_async_copy(res, res_hbm, io.at[6])
    write_res.start()
    for c in first + second + third + [high] + eall + ecopies + hcopies + gcopies:
        c.wait_send()

    @pl.when(o > 0)
    def _():
        low.wait_send()

    for c in (write, write_ge, write_res):
        c.wait()


def finish(section, res, ge, out, gw_out, gb_out, ge_out, held, rv, gv, gwv, gbv, come, go):
    size = CH // 4
    parts = [slice(n * size, n * size + size) for n in range(4)]
    ins = [pltpu.make_async_copy(section.at[p], held.at[p], come.at[n]) for n, p in enumerate(parts)]
    outs = [pltpu.make_async_copy(held.at[p], out.at[p], go.at[n]) for n, p in enumerate(parts)]
    res_in = pltpu.make_async_copy(res, rv, come.at[4])
    ge_in = pltpu.make_async_copy(ge, gv, come.at[5])
    for c in [res_in, ge_in] + ins:
        c.start()
    small = [
        pltpu.make_async_copy(src, dst, go.at[4 + n])
        for n, (src, dst) in enumerate(((gwv, gw_out), (gbv, gb_out), (gv, ge_out)))
    ]
    res_in.wait()
    unpack_grads(rv, gwv, gbv)
    ge_in.wait()
    for c in small:
        c.start()
    for n in range(4):
        ins[n].wait()
        outs[n].start()
    for c in outs + small:
        c.wait()


def per_device(bin_embed, weights, biases, dilations, cotangent):
    vmem = pl.BlockSpec(memory_space=pltpu.VMEM)
    smem = pl.BlockSpec(memory_space=pltpu.SMEM)
    hbm = pl.BlockSpec(memory_space=pl.ANY)
    shape = jax.ShapeDtypeStruct
    dma = pltpu.SemaphoreType.DMA
    mem = pltpu.VMEM
    halo = [mem((H2, CH, 128), bf16), mem((20, CH, 128), bf16), mem((20, CH, 128), bf16),
            mem((16, CH, 128), bf16), mem((16, CH, 128), bf16)]
    edge = [mem((18, CH, 128), bf16)] * 4
    section, res, ge = pl.pallas_call(
        kernel,
        out_shape=[shape((CH, TI, TK), bf16), shape((16, 2, 8, 128), f32), shape((CH, TI), f32)],
        in_specs=[smem, hbm, hbm, hbm, hbm],
        out_specs=[hbm, hbm, hbm],
        scratch_shapes=[
            mem((16, 2, 8, 128), f32), mem((CH, TI), f32),
            mem((CH, TI), bf16), mem((2, 9, CH, CH), bf16), mem((2, CH), f32),
            mem((CH, TI, TK), bf16), mem((CH, TI, TK), bf16),
            mem((6, CH, 128), bf16), mem((3, CH, 128), bf16), *halo, *edge,
            mem((H2, CH, 128), bf16), mem((H1, CH, 128), bf16),
            mem((H2, 5 * CH, 128), bf16), mem((H2, 5 * CH, 128), bf16),
            mem((H1, 5 * CH, 128), bf16), mem((H1, 5 * CH, 128), bf16),
            mem((2, CH, 9 * CH), bf16), mem((2, CH, 9 * CH), bf16),
            mem((CH, 9 * CH), f32), mem((CH, 128), f32),
            mem((16, 2, 8, 128), f32), mem((2, CH, TI), f32),
            mem((16, 2, 8, 128), f32), mem((2, 8, 128), f32),
            mem((16, 2, 8, 128), f32), mem((2, CH, TI), f32), mem((8, CH, TI), f32),
            mem((H2 + 4 * DMAX, CH, 256), bf16), mem((10, CH, 128), bf16),
            mem((84, CH, 128), bf16), mem((H2, CH, 128), bf16), mem((52, CH, 128), bf16),
            mem((52, 5 * CH, 128), bf16), mem((36, CH, 128), bf16),
            dma((7,)), dma((6,)), dma((6,)), dma((8,)), dma((8,)), dma((6,)), dma((6,)),
            dma((16,)), dma((16,)), dma((16,)), dma((16,)), dma((16,)), dma((16,)),
            dma((2,)), dma((2,)), dma((8,)), dma((8,)), dma,
        ],
        compiler_params=pltpu.CompilerParams(collective_id=0, has_side_effects=True, vmem_limit_bytes=60 << 20),
        name="section",
    )(dilations, bin_embed, weights, biases, cotangent)
    out, gw, gb, ge_out = pl.pallas_call(
        finish,
        out_shape=[shape((CH, TI, TK), bf16), shape((2, 9, CH, CH), f32), shape((2, CH), f32), shape((CH, TI), f32)],
        in_specs=[hbm] * 3,
        out_specs=[hbm] * 4,
        scratch_shapes=[mem((CH, TI, TK), bf16), mem((16, 2, 8, 128), f32), mem((CH, TI), f32),
                        mem((2, 9, CH, CH), f32), mem((2, CH), f32), dma((6,)), dma((7,))],
        name="finish",
    )(section, res, ge)
    return out, gw, gb, ge_out


def solution(mesh):
    placed = (P(None, "diag"), P(), P(), P(), P(None, "diag", "off"))
    return jax.shard_map(
        per_device,
        mesh=mesh,
        in_specs=placed,
        out_specs=(P(None, "diag", "off"), P(), P(), P(None, "diag")),
        check_vma=False,
    )
```

```python
import jax
import jax.numpy as jnp
from jax import lax
from jax.experimental import pallas as pl
from jax.experimental.pallas import tpu as pltpu
from jax.sharding import PartitionSpec as P

DMAX = 8
CH = 32
TI = 128
TK = 128
H1 = TI + 2 * DMAX
H2 = TI + 4 * DMAX
NBINS = 4096
KBAND = 1024
bf16 = jnp.bfloat16
f32 = jnp.float32
NT = (((1,), (1,)), ((), ()))


def lanes(n=1):
    return lax.broadcasted_iota(jnp.int32, (CH, 128), 1)


def level(value):
    return jnp.full((CH, 128), value.astype(f32)).astype(bf16)


def in_range(s, d):
    p = lanes().astype(bf16)
    return p < level(128 - s * d) if s > 0 else p >= level(-s * d)


def turned(x, amount):
    return pltpu.roll(x, lax.rem(256 - amount, 128), 1)


def shift_pair(a, b, amount, inside, both=True):
    ra, rb = turned(a, amount), turned(b, amount)
    out_a = jnp.where(inside, ra, rb)
    if not both:
        return out_a
    return out_a, jnp.where(inside, rb, ra)


def row_masks(row0, band0, i):
    p = lanes()
    row = row0 + i
    ka = band0 + p
    kb = band0 + jnp.where(p < 64, p + 128, p - 128)
    live = (row >= 0)
    ma = (ka < NBINS - row) & live
    mb = (kb < NBINS - row) & (kb >= 0) & (kb < KBAND) & live
    return ma, mb


def store_shifts(dst, i, a, b, amounts, insides, both=True):
    for n, s in enumerate((-2, -1, 0, 1, 2)):
        rows = slice(CH * n, CH * (n + 1))
        if s == 0:
            dst[i, rows, 0:128] = a
            if both:
                dst[i, rows, 128:256] = b
        elif both:
            sa, sb = shift_pair(a, b, amounts[n], insides[n])
            dst[i, rows, 0:128] = sa
            dst[i, rows, 128:256] = sb
        else:
            dst[i, rows, 0:128] = shift_pair(a, b, amounts[n], insides[n], False)


def taps(src, i, d, lo=0, hi=256):
    return jnp.concatenate(
        [src[i - d, 64:160, lo:hi], src[i, 32:128, lo:hi], src[i + d, 0:96, lo:hi]], axis=0
    )


def shift_tables(d):
    amounts = [s * d for s in (-2, -1, 0, 1, 2)]
    return amounts, [in_range(s, d) for s in (-2, -1, 0, 1, 2)]


LOW = -1e38


def bounded_blocks(r, o, ec, er):
    for n in range(1, 5):
        ec[n] = jnp.where(r + o + n - 2 < NBINS // TI, ec[n], LOW)
    for n in (0, 2):
        ec_row = r + n - 1
        er[n] = jnp.where((ec_row >= 0) & (ec_row < NBINS // TI), er[n], LOW)


def rim_lane():
    t = lax.rem(lanes(), 32)
    return jnp.where(t < 16, t - 16, t + 112)


def lane_caps(band0, d, caps):
    for n, s in enumerate((-2, -1, 0, 1, 2)):
        for rim in range(2):
            k = band0 + s * d + (rim_lane() if rim else lanes())
            caps[2 * n + rim] = jnp.where((k >= 0) & (k < KBAND), 3e38, 0.0).astype(bf16)


def phase_windows(ec, win, unroll=32):
    u = lanes()
    ub = u.astype(bf16)

    def body(it, _):
        m0 = it * unroll - 4 * DMAX
        q = lax.div(m0 + 128, 128) - 1
        t0 = m0 - 128 * q
        prev, here, after, later = (ec[q + 1 + n] for n in range(4))
        high = jnp.where((u >= 64) & (t0 < 32), prev, after)
        low = jnp.where((u < 64) & (t0 >= 96), later, here)
        for w in range(unroll):
            t = t0 + w
            beyond = ub >= level(t)
            back = lax.rem(128 - t, 128)
            win[it * unroll + w, :, 0:128] = pltpu.roll(jnp.where(beyond, here, after), back, 1)
            win[it * unroll + w, :, 128:256] = pltpu.roll(jnp.where(beyond, high, low), back, 1)
        return 0

    lax.fori_loop(0, (H2 + 4 * DMAX) // unroll, body, 0)


def four_groups(rows):
    p = lanes()
    low = jnp.where(p < 32, rows[0], rows[1])
    high = jnp.where(p < 96, rows[2], rows[3])
    return jnp.where(p < 64, low, high)


def phase_rim_windows(win, rwin, unroll=12):
    def body(it, _):
        for w in range(unroll):
            n = it * unroll + w
            rwin[n] = four_groups(
                [pltpu.roll(win[36 * q + n, :, 128:256], (32 * q + 16) % 128, 1) for q in range(4)]
            )
        return 0

    lax.fori_loop(0, 84 // unroll, body, 0)


def phase_x0(d, er, win, caps, x0, s0, owns, unroll=16):
    def body(it, _):
        i0 = it * unroll - 2 * DMAX
        q = lax.div(i0 + 128, 128) - 1
        block = pltpu.roll(er[q + 1], lax.rem(256 - (i0 - 128 * q), 128), 1)
        for w in range(unroll):
            j = it * unroll + w
            own = jnp.broadcast_to(block[:, w : w + 1], (CH, 128))
            owns[j] = own
            for n, s in enumerate((-2, -1, 0, 1, 2)):
                v = own + win[j + 2 * DMAX + s * d, :, 0:128]
                if s == 0:
                    x0[j] = v
                s0[j, CH * n : CH * n + CH, :] = jnp.minimum(jnp.maximum(v, 0), caps[2 * n])
        return 0

    lax.fori_loop(0, H2 // unroll, body, 0)


def phase_rim_x0(d, rwin, owns, caps, rx0, rs0, unroll=13):
    def body(it, _):
        for w in range(unroll):
            j = it * unroll + w
            own = four_groups([owns[36 * q + j] for q in range(4)])
            for n, s in enumerate((-2, -1, 0, 1, 2)):
                v = own + rwin[j + 2 * DMAX + s * d]
                if s == 0:
                    rx0[j] = v
                rs0[j, CH * n : CH * n + CH, :] = jnp.minimum(jnp.maximum(v, 0), caps[2 * n + 1])
        return 0

    lax.fori_loop(0, 52 // unroll, body, 0)


def phase_rim_x1(row0, band0, d, wf, bias, rx0, rs0, rx1, unroll=36):
    bias = jnp.broadcast_to(bias, (CH, 128))
    k = band0 + rim_lane()
    across = (k >= 0) & (k < KBAND)

    def body(it, _):
        for w in range(0, unroll, 2):
            j = it * unroll + w
            x = jnp.concatenate([taps(rs0, j + DMAX, d, 0, 128), taps(rs0, j + DMAX + 1, d, 0, 128)], axis=1)
            conv = jnp.dot(wf, x, preferred_element_type=f32)
            for z in range(2):
                row = row0 + 36 * lax.div(lanes(), 32) + (j + z - DMAX)
                v = rx0[j + z + DMAX].astype(f32) + conv[:, 128 * z : 128 * z + 128] + bias
                live = across & (row >= 0) & (k < NBINS - row)
                rx1[j + z] = jnp.where(live, jnp.maximum(v, 0.0), 0.0).astype(bf16)
        return 0

    lax.fori_loop(0, 36 // unroll, body, 0)


def phase_x1(row0, band0, d, dn, wf, bias, x0, s0, rx1, x1, s1):
    insides = inside_masks(dn)
    bias = jnp.broadcast_to(bias, (CH, 128))
    lane = lanes()

    def body(it, _):
        for w in range(0, 36, 2):
            j = it * 36 + w
            jj = j + DMAX
            x = jnp.concatenate([taps(s0, jj, d, 0, 128), taps(s0, jj + 1, d, 0, 128)], axis=1)
            conv = jnp.dot(wf, x, preferred_element_type=f32)
            for z in range(2):
                row = row0 + j + z - DMAX
                live = (row >= 0) & (band0 + lane < NBINS - row)
                a = x0[jj + z].astype(f32) + conv[:, 128 * z : 128 * z + 128] + bias
                a = jnp.where(live, a, 0.0).astype(bf16)
                x1[j + z] = a
                a = jnp.maximum(a, 0)
                s1[j + z, block_of(2), :] = a
                rim = rx1[w + z]
                for n, (m, s) in enumerate(SHIFTS):
                    side = pltpu.roll(rim, lax.rem(384 + 112 - 32 * it - s * dn, 128), 1)
                    s1[j + z, block_of(m), :] = jnp.where(insides[n], rolled(a, s, dn), side)
        return 0

    lax.fori_loop(0, 4, body, 0)


def phase_x2(row0, band0, d, wf, bias, x1, s1, out, unroll=16):
    bias = jnp.broadcast_to(bias, (CH, 128))

    def body(it, _):
        rows = []
        for w in range(0, unroll, 2):
            i = it * unroll + w
            j = i + DMAX
            x = jnp.concatenate([taps(s1, j, d, 0, 128), taps(s1, j + 1, d, 0, 128)], axis=1)
            conv = jnp.dot(wf, x, preferred_element_type=f32)
            for z in range(2):
                ma, _mb = row_masks(row0, band0, i + z)
                a = x1[j + z].astype(f32) + conv[:, 128 * z : 128 * z + 128] + bias
                rows.append(jnp.where(ma, a, 0.0).astype(bf16))
        out[:, pl.ds(pl.multiple_of(it * unroll, unroll), unroll), :] = jnp.swapaxes(jnp.stack(rows), 0, 1)
        return 0

    lax.fori_loop(0, TI // unroll, body, 0)


def phase_gw(h, s, soff, d, gw, gb, unroll=64):
    def body(it, carry):
        acc, accb = carry
        for w in range(0, unroll, 2):
            i = it * unroll + w
            x = jnp.concatenate(
                [taps(s, i + soff, d, 0, 128), taps(s, i + 1 + soff, d, 0, 128)], axis=1
            )
            ha, hb = h(i), h(i + 1)
            hh = jnp.concatenate([ha, hb], axis=1)
            acc = acc + lax.dot_general(hh, x, NT, preferred_element_type=f32)
            accb = accb + (ha.astype(f32) + hb.astype(f32))
        return acc, accb

    acc, accb = lax.fori_loop(
        0, TI // unroll, body, (jnp.zeros((CH, 9 * CH), f32), jnp.zeros((CH, 128), f32))
    )
    gw[...] = acc
    gb[...] = accb


def packed(rows):
    lane = lanes()
    left, right = rows[0], rows[7]
    for w in range(1, 8):
        left = jnp.where(lane < 16 * w, left, pltpu.roll(rows[w], 16 * w, 1))
    for w in range(6, -1, -1):
        right = jnp.where(lane >= 16 * (w + 1), right, pltpu.roll(rows[w], 16 * w + 16, 1))
    return left, right


SHIFTS = ((0, -2), (1, -1), (3, 1), (4, 2))


def block_of(n):
    return slice(CH * n, CH * n + CH)


def rolled(x, s, d):
    return pltpu.roll(x, lax.rem(256 - s * d, 128), 1)


def halo_sides(row0, band0, depth, group, rl, rr):
    lane = lanes()
    row = row0 + group * 8 - depth + lax.div(lane, 16)
    kr = band0 + 128 + lax.rem(lane, 16)
    kl = band0 - 16 + lax.rem(lane, 16)
    right = jnp.where((row >= 0) & (kr < KBAND) & (kr < NBINS - row), rl[group], 0)
    left = jnp.where((row >= 0) & (kl >= 0) & (kl < NBINS - row), rr[group], 0)
    return right, left


def side_of(right, left, w, s, d):
    if s > 0:
        return pltpu.roll(right, lax.rem(256 - 16 * w - s * d, 128), 1)
    return pltpu.roll(left, lax.rem(256 + 16 * (7 - w) - s * d, 128), 1)


def put_row(row0, band0, d, depth, j, a, dst):
    row = row0 + j - depth
    live = (row >= 0) & (band0 + lanes() < NBINS - row)
    a = jnp.where(live, a, 0)
    dst[j, block_of(2), :] = a
    for m, s in SHIFTS:
        dst[j, block_of(m), :] = rolled(a, s, d)


def patch_group(row0, band0, d, depth, group, insides, rl, rr, dst):
    right, left = halo_sides(row0, band0, depth, group, rl, rr)
    for w in range(8):
        j = group * 8 + w
        for n, (m, s) in enumerate(SHIFTS):
            dst[j, block_of(m), :] = jnp.where(
                insides[n], dst[j, block_of(m), :], side_of(right, left, w, s, d)
            )


def inside_masks(d):
    return [in_range(s, d) for _m, s in SHIFTS]


def phase_patch(row0, band0, d, depth, groups, rl, rr, dst, unroll):
    insides = inside_masks(d)

    def body(it, _):
        for g in range(unroll):
            patch_group(row0, band0, d, depth, it * unroll + g, insides, rl, rr, dst)
        return 0

    lax.fori_loop(0, groups // unroll, body, 0)


def phase_own_shifts(row0, band0, d, a, dst, unroll=32):
    def body(it, _):
        for w in range(unroll):
            j = 2 * DMAX + it * unroll + w
            put_row(row0, band0, d, 2 * DMAX, j, a[j], dst)
        return 0

    lax.fori_loop(0, TI // unroll, body, 0)


def phase_rim_shifts(row0, band0, d, a, dst):
    def body(it, _):
        for w in range(16):
            j = it * 144 + w
            put_row(row0, band0, d, 2 * DMAX, j, a[j], dst)
        return 0

    lax.fori_loop(0, 2, body, 0)


def phase_g1(d, dn, wb, x1, t1, t0, gpl, gpr, send_chunk, unroll=48):
    def body(it, _):
        rows = []
        for w in range(0, unroll, 2):
            j = it * unroll + w
            x = jnp.concatenate([taps(t1, j + DMAX, d, 0, 128), taps(t1, j + DMAX + 1, d, 0, 128)], axis=1)
            q = jnp.dot(wb, x, preferred_element_type=f32)
            for z in range(2):
                h = t1[j + DMAX + z, 64:96, :].astype(f32)
                gate = x1[j + z].astype(f32) > 0
                g = (h + jnp.where(gate, q[:, 128 * z : 128 * z + 128], 0.0)).astype(bf16)
                rows.append(g)
        for n in range(unroll // 8):
            left, right = packed(rows[8 * n : 8 * n + 8])
            gpl[it * (unroll // 8) + n] = left
            gpr[it * (unroll // 8) + n] = right
        send_chunk(it)
        for w, g in enumerate(rows):
            j = it * unroll + w
            t0[j, block_of(2), :] = g
            for m, s in SHIFTS:
                t0[j, block_of(m), :] = rolled(g, s, dn)
        return 0

    lax.fori_loop(0, H1 // unroll, body, 0)


def phase_g0(d, wb, s0, t0, begin, end, carry, unroll=32):
    lane = lanes()
    ones = jnp.ones((128, 128), bf16)

    def body(it, carry):
        rsum, lo, hi = carry
        rows = []
        for w in range(0, unroll, 2):
            i = it * unroll + w
            j = i + DMAX
            x = jnp.concatenate([taps(t0, j, d, 0, 128), taps(t0, j + 1, d, 0, 128)], axis=1)
            q = jnp.dot(wb, x, preferred_element_type=f32)
            for z in range(2):
                g1 = t0[j + z, 64:96, 0:128].astype(f32)
                gate = s0[j + z + DMAX, 64:96, 0:128].astype(f32) > 0
                gp = (g1 + jnp.where(gate, q[:, 128 * z : 128 * z + 128], 0.0)).astype(bf16)
                rows.append(gp)
                moved = pltpu.roll(gp, i + z, 1).astype(f32)
                low = jnp.where(lane >= i + z, moved, 0.0)
                lo = lo + low
                hi = hi + (moved - low)
        sums = jnp.dot(jnp.concatenate(rows, axis=0), ones, preferred_element_type=f32)
        for w in range(unroll):
            rsum = jnp.where(lane == it * unroll + w, sums[CH * w : CH * w + CH], rsum)
        return rsum, lo, hi

    return lax.fori_loop(begin // unroll, end // unroll, body, carry)
MESH = pl.DeviceIdType.MESH
NR, NO = 32, 8


def place_weights(w, wf, wb):
    row = lax.broadcasted_iota(jnp.int32, (CH, 9 * CH), 0)
    col = lax.broadcasted_iota(jnp.int32, (CH, 9 * CH), 1)
    for layer in range(2):
        fwd = jnp.zeros((CH, 9 * CH), f32)
        bwd = jnp.zeros((CH, 9 * CH), f32)
        for t in range(9):
            spot = jnp.where(col == row + CH * t, 1.0, 0.0).astype(bf16)
            fwd = fwd + jnp.dot(w[layer, t], spot, preferred_element_type=f32)
            bwd = bwd + lax.dot_general(
                w[layer, 8 - t], spot, (((0,), (0,)), ((), ())), preferred_element_type=f32
            )
        wf[layer] = fwd.astype(bf16)
        wb[layer] = bwd.astype(bf16)


def pack_grads(layer, gw, gb, pay):
    third = jnp.concatenate([gw[:, 256:288], jnp.sum(gb[...], axis=1, keepdims=True), jnp.zeros((CH, 95), f32)], axis=1)
    for og in range(4):
        rows = slice(8 * og, 8 * og + 8)
        for lt in range(2):
            pay[layer * 8 + og * 2 + lt, 0] = gw[rows, 128 * lt : 128 * lt + 128]
    return third


def unpack_grads(res, gw_out, gb_out):
    eye = lax.broadcasted_iota(jnp.int32, (CH, CH), 0) == lax.broadcasted_iota(jnp.int32, (CH, CH), 1)
    third = jnp.concatenate([res[og, 1] for og in range(4)], axis=0)
    for layer in range(2):
        for lt in range(2):
            tile = jnp.concatenate([res[layer * 8 + og * 2 + lt, 0] for og in range(4)], axis=0)
            for n in range(4):
                gw_out[layer, 4 * lt + n] = tile[:, CH * n : CH * n + CH]
        gw_out[layer, 8] = third[:, 64 * layer : 64 * layer + CH]
        column = third[:, 64 * layer + CH : 64 * layer + CH + 1]
        gb_out[layer : layer + 1, :] = jnp.sum(jnp.where(eye, column, 0.0), axis=0, keepdims=True)


def remote(src, dst, send, recv, target):
    return pltpu.make_async_remote_copy(
        src_ref=src, dst_ref=dst, send_sem=send, recv_sem=recv, device_id=target, device_id_type=MESH
    )


def wrap(r, o):
    return (lax.rem(r + 2 * NR, NR), lax.rem(o + NO, NO))


def halo_copies(r, o, a, pl_, pr_, rl, rr, send, recv):
    jobs = [
        (pl_, rl.at[2:18], 0, -1),
        (pr_, rr.at[2:18], 0, 1),
        (a.at[128:144], a.at[0:16], 1, 0),
        (a.at[16:32], a.at[144:160], -1, 0),
        (pl_.at[14:16], rl.at[0:2], 1, -1),
        (pl_.at[0:2], rl.at[18:20], -1, -1),
        (pr_.at[14:16], rr.at[0:2], 1, 1),
        (pr_.at[0:2], rr.at[18:20], -1, 1),
    ]
    return [
        remote(src, dst, send.at[n], recv.at[n], wrap(r + dr, o + do))
        for n, (src, dst, dr, do) in enumerate(jobs)
    ]


def embed_copies(r, o, emb, ec, er, send, recv):
    other = o + 1 - 2 * lax.rem(o, 2)
    copies = [
        remote(emb, ec.at[n], send.at[n - 1], recv.at[n - 1], wrap(r - other - (n - 2), other))
        for n in range(1, 5)
    ]
    copies.append(remote(emb, er.at[0], send.at[4], recv.at[4], wrap(r + 1, o)))
    copies.append(remote(emb, er.at[2], send.at[5], recv.at[5], wrap(r - 1, o)))
    return copies


def greet_exchange(r, o, barrier):
    other = o + 1 - 2 * lax.rem(o, 2)
    targets = [wrap(r + o + n - 2, other) for n in range(1, 5)]
    targets += [wrap(r + dr, o + do) for dr in (-1, 0, 1) for do in (-1, 0, 1) if (dr, do) != (0, 0)]
    for target in targets:
        pl.semaphore_signal(barrier, inc=1, device_id=target, device_id_type=MESH)
    return len(targets)


def lay_rows(cot, a, pl_, pr_):
    def body(it, _):
        block = jnp.swapaxes(cot[:, pl.ds(pl.multiple_of(it * 16, 16), 16), :], 0, 1)
        a[pl.ds(2 * DMAX + it * 16, 16)] = block
        for n in range(2):
            left, right = packed([block[8 * n + w] for w in range(8)])
            pl_[it * 2 + n] = left
            pr_[it * 2 + n] = right
        return 0

    lax.fori_loop(0, 8, body, 0)


def kernel(
    dil, emb_hbm, w_hbm, bias_hbm, cot_hbm, out_hbm, res_hbm, ge_hbm,
    res, ge,    emb, w, bias, cot, out, ec, er, a, rl, rr, pl_, pr_, grl, grr, gpl, gpr, x0, x1, s0, t1, s1, t0, wf, wb, gw, gb,
    pay, terms, wr1, w2, wr2, inbox, shares, win, caps, rwin, owns, rx0, rs0, rx1,
    io, esend, erecv, hsend, hrecv, gsend, grecv, sa, ra, sb, rb, sc, rc, st, rt, su, ru, local_sem,
):
    r, o = lax.axis_index("diag"), lax.axis_index("off")
    core, b = lax.rem(r, 2), lax.div(r, 2)
    me = o * 2 + core
    row0, band0 = r * TI, o * TK
    fetches = [
        pltpu.make_async_copy(src, dst, io.at[n])
        for n, (src, dst) in enumerate(((emb_hbm, emb), (w_hbm, w), (bias_hbm, bias), (cot_hbm, cot)))
    ]
    for c in fetches:
        c.start()

    def peer_a(n):
        other = lax.rem(me + n, 16)
        return other, (2 * b + lax.rem(other, 2), lax.div(other, 2))

    def peer_b(n):
        other = lax.rem(b + n, 16)
        return other, (2 * other + core, o)

    barrier = pltpu.get_barrier_semaphore()

    def greet(target):
        pl.semaphore_signal(barrier, inc=1, device_id=target, device_id_type=MESH)

    count = greet_exchange(r, o, barrier)
    for n in range(1, 16):
        greet(peer_a(n)[1])
        greet(peer_b(n)[1])
    greet(wrap(r - o - 1, o))

    @pl.when(o > 0)
    def _():
        greet(wrap(r - o, o))

    count = count + 30 + 1 + jnp.minimum(o, 1)
    ec[0] = jnp.zeros((CH, 128), bf16)
    ec[5] = jnp.zeros((CH, 128), bf16)
    d0, d1 = dil[0], dil[1]
    lane_caps(band0, d0, caps)
    for c in fetches:
        c.wait()
    er[1] = emb[...]
    place_weights(w, wf, wb)
    lay_rows(cot, a, pl_, pr_)
    pl.semaphore_wait(barrier, count)
    ecopies = embed_copies(r, o, emb, ec, er, esend, erecv)
    hcopies = halo_copies(r, o, a, pl_, pr_, rl, rr, hsend, hrecv)
    for c in ecopies + hcopies:
        c.start()

    eye = lax.broadcasted_iota(jnp.int32, (CH, CH), 0) == lax.broadcasted_iota(jnp.int32, (CH, CH), 1)

    def column(layer):
        return jnp.sum(jnp.where(eye, bias[layer : layer + 1, :], 0.0), axis=1, keepdims=True)

    phase_own_shifts(row0, band0, d1, a, t1)
    for c in ecopies:
        c.wait_recv()
    bounded_blocks(r, o, ec, er)
    phase_windows(ec, win)
    phase_rim_windows(win, rwin)
    phase_x0(d0, er, win, caps, x0, s0, owns)
    phase_rim_x0(d0, rwin, owns, caps, rx0, rs0)
    phase_rim_x1(row0, band0, d0, wf[0], column(0), rx0, rs0, rx1)
    phase_x1(row0, band0, d0, d1, wf[0], column(0), x0, s0, rx1, x1, s1)
    phase_gw(lambda i: t1[i + 2 * DMAX, 64:96, :], s1, DMAX, d1, gw, gb)
    third1 = pack_grads(1, gw, gb, pay)
    for c in hcopies[2:4]:
        c.wait_recv()
    phase_rim_shifts(row0, band0, d1, a, t1)
    for c in hcopies[:2] + hcopies[4:]:
        c.wait_recv()
    phase_patch(row0, band0, d1, 2 * DMAX, H2 // 8, rl, rr, t1, 5)

    def edge_copies(it):
        part = pl.ds(it * 6, 6)
        return (
            remote(gpl.at[part], grl.at[part], gsend.at[it], grecv.at[it], wrap(r, o - 1)),
            remote(gpr.at[part], grr.at[part], gsend.at[3 + it], grecv.at[3 + it], wrap(r, o + 1)),
        )

    def send_chunk(it):
        for c in edge_copies(it):
            c.start()

    phase_g1(d1, d0, wb[1], x1, t1, t0, gpl, gpr, send_chunk)
    gcopies = [c for n in range(3) for c in edge_copies(n)]
    phase_gw(lambda i: t0[i + DMAX, 64:96, :], s0, 2 * DMAX, d0, gw, gb)
    third0 = pack_grads(0, gw, gb, pay)
    rest = third0 + pltpu.roll(third1, 64, 1)
    for n in range(16):
        pay[n, 1] = rest[8 * n : 8 * n + 8] if n < 4 else jnp.zeros((8, 128), f32)

    first = [remote(pay.at[other], wr1.at[me], sa.at[n], ra.at[me], target)
             for n in range(1, 16) for other, target in [peer_a(n)]]
    for c in first:
        c.start()

    phase_x2(row0, band0, d1, wf[1], column(1), x1, s1, out, 64)
    write = pltpu.make_async_copy(out, out_hbm, io.at[4])
    write.start()

    for c in gcopies:
        c.wait_recv()
    phase_patch(row0, band0, d0, DMAX, H1 // 8, grl, grr, t0, 6)

    def arrived(dst, sem):
        pltpu.make_async_copy(dst, dst, sem).wait()

    def total(buf):
        acc = buf[0]
        for n in range(1, 16):
            acc = acc + buf[n]
        return acc

    zero = jnp.zeros((CH, TI), f32)
    sums = phase_g0(d0, wb[0], s0, t0, 0, 64, (zero, zero, zero))
    wr1[me] = pay[me]
    for n in range(1, 16):
        other, _t = peer_a(n)
        arrived(wr1.at[other], ra.at[other])
    w2[...] = total(wr1)
    second = [remote(w2, wr2.at[b], sb.at[n], rb.at[b], target)
              for n in range(1, 16) for other, target in [peer_b(n)]]
    for c in second:
        c.start()

    rsum, lo, hi = phase_g0(d0, wb[0], s0, t0, 64, 128, sums)
    terms[0] = lo
    terms[1] = hi
    low = remote(terms.at[0], inbox.at[0], st.at[0], rt.at[0], wrap(r + o, o))
    high = remote(terms.at[1], inbox.at[1], st.at[1], rt.at[1], wrap(r + o + 1, o))
    high.start()
    local = pltpu.make_async_copy(terms.at[0], inbox.at[0], local_sem)

    @pl.when(o > 0)
    def _():
        low.start()

    @pl.when(o == 0)
    def _():
        local.start()


    @pl.when(o > 0)
    def _():
        low.wait_recv()

    @pl.when(o == 0)
    def _():
        local.wait()

    high.wait_recv()
    shares[o] = rsum + inbox[0] + inbox[1]
    eall = [remote(shares.at[o], shares.at[o], su.at[n], ru.at[o], wrap(r, o + n)) for n in range(1, 8)]
    for c in eall:
        c.start()

    wr2[b] = w2[...]
    for n in range(1, 16):
        other, _t = peer_b(n)
        arrived(wr2.at[other], rb.at[other])
    res[me] = total(wr2)
    third = [remote(res.at[me], res.at[me], sc.at[n], rc.at[me], target)
             for n in range(1, 16) for other, target in [peer_a(n)]]
    for c in third:
        c.start()
    for n in range(1, 8):
        oo = lax.rem(o + n, 8)
        arrived(shares.at[oo], ru.at[oo])
    acc = shares[0]
    for n in range(1, 8):
        acc = acc + shares[n]
    ge[...] = acc
    write_ge = pltpu.make_async_copy(ge, ge_hbm, io.at[5])
    write_ge.start()
    for n in range(1, 16):
        other, _t = peer_a(n)
        arrived(res.at[other], rc.at[other])
    write_res = pltpu.make_async_copy(res, res_hbm, io.at[6])
    write_res.start()
    for c in first + second + third + [high] + eall + ecopies + hcopies + gcopies:
        c.wait_send()

    @pl.when(o > 0)
    def _():
        low.wait_send()

    for c in (write, write_ge, write_res):
        c.wait()


def finish(section, res, ge, out, gw_out, gb_out, ge_out, held, rv, gv, gwv, gbv, come, go):
    size = CH // 4
    parts = [slice(n * size, n * size + size) for n in range(4)]
    ins = [pltpu.make_async_copy(section.at[p], held.at[p], come.at[n]) for n, p in enumerate(parts)]
    outs = [pltpu.make_async_copy(held.at[p], out.at[p], go.at[n]) for n, p in enumerate(parts)]
    res_in = pltpu.make_async_copy(res, rv, come.at[4])
    ge_in = pltpu.make_async_copy(ge, gv, come.at[5])
    for c in [res_in, ge_in] + ins:
        c.start()
    small = [
        pltpu.make_async_copy(src, dst, go.at[4 + n])
        for n, (src, dst) in enumerate(((gwv, gw_out), (gbv, gb_out), (gv, ge_out)))
    ]
    res_in.wait()
    unpack_grads(rv, gwv, gbv)
    ge_in.wait()
    for c in small:
        c.start()
    for n in range(4):
        ins[n].wait()
        outs[n].start()
    for c in outs + small:
        c.wait()


def per_device(bin_embed, weights, biases, dilations, cotangent):
    vmem = pl.BlockSpec(memory_space=pltpu.VMEM)
    smem = pl.BlockSpec(memory_space=pltpu.SMEM)
    hbm = pl.BlockSpec(memory_space=pl.ANY)
    shape = jax.ShapeDtypeStruct
    dma = pltpu.SemaphoreType.DMA
    mem = pltpu.VMEM
    halo = [mem((H2, CH, 128), bf16), mem((20, CH, 128), bf16), mem((20, CH, 128), bf16),
            mem((16, CH, 128), bf16), mem((16, CH, 128), bf16)]
    edge = [mem((18, CH, 128), bf16)] * 4
    section, res, ge = pl.pallas_call(
        kernel,
        out_shape=[shape((CH, TI, TK), bf16), shape((16, 2, 8, 128), f32), shape((CH, TI), f32)],
        in_specs=[smem, hbm, hbm, hbm, hbm],
        out_specs=[hbm, hbm, hbm],
        scratch_shapes=[
            mem((16, 2, 8, 128), f32), mem((CH, TI), f32),
            mem((CH, TI), bf16), mem((2, 9, CH, CH), bf16), mem((2, CH), f32),
            mem((CH, TI, TK), bf16), mem((CH, TI, TK), bf16),
            mem((6, CH, 128), bf16), mem((3, CH, 128), bf16), *halo, *edge,
            mem((H2, CH, 128), bf16), mem((H1, CH, 128), bf16),
            mem((H2, 5 * CH, 128), bf16), mem((H2, 5 * CH, 128), bf16),
            mem((H1, 5 * CH, 128), bf16), mem((H1, 5 * CH, 128), bf16),
            mem((2, CH, 9 * CH), bf16), mem((2, CH, 9 * CH), bf16),
            mem((CH, 9 * CH), f32), mem((CH, 128), f32),
            mem((16, 2, 8, 128), f32), mem((2, CH, TI), f32),
            mem((16, 2, 8, 128), f32), mem((2, 8, 128), f32),
            mem((16, 2, 8, 128), f32), mem((2, CH, TI), f32), mem((8, CH, TI), f32),
            mem((H2 + 4 * DMAX, CH, 256), bf16), mem((10, CH, 128), bf16),
            mem((84, CH, 128), bf16), mem((H2, CH, 128), bf16), mem((52, CH, 128), bf16),
            mem((52, 5 * CH, 128), bf16), mem((36, CH, 128), bf16),
            dma((7,)), dma((6,)), dma((6,)), dma((8,)), dma((8,)), dma((6,)), dma((6,)),
            dma((16,)), dma((16,)), dma((16,)), dma((16,)), dma((16,)), dma((16,)),
            dma((2,)), dma((2,)), dma((8,)), dma((8,)), dma,
        ],
        compiler_params=pltpu.CompilerParams(collective_id=0, has_side_effects=True, vmem_limit_bytes=60 << 20),
        name="section",
    )(dilations, bin_embed, weights, biases, cotangent)
    out, gw, gb, ge_out = pl.pallas_call(
        finish,
        out_shape=[shape((CH, TI, TK), bf16), shape((2, 9, CH, CH), f32), shape((2, CH), f32), shape((CH, TI), f32)],
        in_specs=[hbm] * 3,
        out_specs=[hbm] * 4,
        scratch_shapes=[mem((CH, TI, TK), bf16), mem((16, 2, 8, 128), f32), mem((CH, TI), f32),
                        mem((2, 9, CH, CH), f32), mem((2, CH), f32), dma((6,)), dma((7,))],
        name="finish",
    )(section, res, ge)
    return out, gw, gb, ge_out


def solution(mesh):
    placed = (P(None, "diag"), P(), P(), P(), P(None, "diag", "off"))
    return jax.shard_map(
        per_device,
        mesh=mesh,
        in_specs=placed,
        out_specs=(P(None, "diag", "off"), P(), P(), P(None, "diag")),
        check_vma=False,
    )
```

```python
import jax
import jax.numpy as jnp
from jax import lax
from jax.experimental import pallas as pl
from jax.experimental.pallas import tpu as pltpu
from jax.sharding import PartitionSpec as P

DMAX = 8
CH = 32
TI = 128
TK = 128
H1 = TI + 2 * DMAX
H2 = TI + 4 * DMAX
NBINS = 4096
KBAND = 1024
bf16 = jnp.bfloat16
f32 = jnp.float32
NT = (((1,), (1,)), ((), ()))


def lanes(n=1):
    return lax.broadcasted_iota(jnp.int32, (CH, 128), 1)


def level(value):
    return jnp.full((CH, 128), value.astype(f32)).astype(bf16)


def in_range(s, d):
    p = lanes().astype(bf16)
    return p < level(128 - s * d) if s > 0 else p >= level(-s * d)


def turned(x, amount):
    return pltpu.roll(x, lax.rem(256 - amount, 128), 1)


def shift_pair(a, b, amount, inside, both=True):
    ra, rb = turned(a, amount), turned(b, amount)
    out_a = jnp.where(inside, ra, rb)
    if not both:
        return out_a
    return out_a, jnp.where(inside, rb, ra)


def row_masks(row0, band0, i):
    p = lanes()
    row = row0 + i
    ka = band0 + p
    kb = band0 + jnp.where(p < 64, p + 128, p - 128)
    live = (row >= 0)
    ma = (ka < NBINS - row) & live
    mb = (kb < NBINS - row) & (kb >= 0) & (kb < KBAND) & live
    return ma, mb


def store_shifts(dst, i, a, b, amounts, insides, both=True):
    for n, s in enumerate((-2, -1, 0, 1, 2)):
        rows = slice(CH * n, CH * (n + 1))
        if s == 0:
            dst[i, rows, 0:128] = a
            if both:
                dst[i, rows, 128:256] = b
        elif both:
            sa, sb = shift_pair(a, b, amounts[n], insides[n])
            dst[i, rows, 0:128] = sa
            dst[i, rows, 128:256] = sb
        else:
            dst[i, rows, 0:128] = shift_pair(a, b, amounts[n], insides[n], False)


def taps(src, i, d, lo=0, hi=256):
    return jnp.concatenate(
        [src[i - d, 64:160, lo:hi], src[i, 32:128, lo:hi], src[i + d, 0:96, lo:hi]], axis=0
    )


def shift_tables(d):
    amounts = [s * d for s in (-2, -1, 0, 1, 2)]
    return amounts, [in_range(s, d) for s in (-2, -1, 0, 1, 2)]


LOW = -1e38


def bounded_blocks(r, o, ec, er):
    for n in range(1, 5):
        ec[n] = jnp.where(r + o + n - 2 < NBINS // TI, ec[n], LOW)
    for n in (0, 2):
        ec_row = r + n - 1
        er[n] = jnp.where((ec_row >= 0) & (ec_row < NBINS // TI), er[n], LOW)


def rim_lane():
    t = lax.rem(lanes(), 32)
    return jnp.where(t < 16, t - 16, t + 112)


def lane_caps(band0, d, caps):
    for n, s in enumerate((-2, -1, 0, 1, 2)):
        for rim in range(2):
            k = band0 + s * d + (rim_lane() if rim else lanes())
            caps[2 * n + rim] = jnp.where((k >= 0) & (k < KBAND), 3e38, 0.0).astype(bf16)


def phase_windows(ec, win, unroll=32):
    u = lanes()
    ub = u.astype(bf16)

    def body(it, _):
        m0 = it * unroll - 4 * DMAX
        q = lax.div(m0 + 128, 128) - 1
        t0 = m0 - 128 * q
        prev, here, after, later = (ec[q + 1 + n] for n in range(4))
        high = jnp.where((u >= 64) & (t0 < 32), prev, after)
        low = jnp.where((u < 64) & (t0 >= 96), later, here)
        for w in range(unroll):
            t = t0 + w
            beyond = ub >= level(t)
            back = lax.rem(128 - t, 128)
            win[it * unroll + w, :, 0:128] = pltpu.roll(jnp.where(beyond, here, after), back, 1)
            win[it * unroll + w, :, 128:256] = pltpu.roll(jnp.where(beyond, high, low), back, 1)
        return 0

    lax.fori_loop(0, (H2 + 4 * DMAX) // unroll, body, 0)


def four_groups(rows):
    p = lanes()
    low = jnp.where(p < 32, rows[0], rows[1])
    high = jnp.where(p < 96, rows[2], rows[3])
    return jnp.where(p < 64, low, high)


def phase_rim_windows(win, rwin, unroll=12):
    def body(it, _):
        for w in range(unroll):
            n = it * unroll + w
            rwin[n] = four_groups(
                [pltpu.roll(win[36 * q + n, :, 128:256], (32 * q + 16) % 128, 1) for q in range(4)]
            )
        return 0

    lax.fori_loop(0, 84 // unroll, body, 0)


def phase_x0(d, er, win, caps, x0, s0, owns, unroll=16):
    def body(it, _):
        i0 = it * unroll - 2 * DMAX
        q = lax.div(i0 + 128, 128) - 1
        block = pltpu.roll(er[q + 1], lax.rem(256 - (i0 - 128 * q), 128), 1)
        for w in range(unroll):
            j = it * unroll + w
            own = jnp.broadcast_to(block[:, w : w + 1], (CH, 128))
            owns[j] = own
            for n, s in enumerate((-2, -1, 0, 1, 2)):
                v = own + win[j + 2 * DMAX + s * d, :, 0:128]
                if s == 0:
                    x0[j] = v
                s0[j, CH * n : CH * n + CH, :] = jnp.minimum(jnp.maximum(v, 0), caps[2 * n])
        return 0

    lax.fori_loop(0, H2 // unroll, body, 0)


def phase_rim_x0(d, rwin, owns, caps, rx0, rs0, unroll=13):
    def body(it, _):
        for w in range(unroll):
            j = it * unroll + w
            own = four_groups([owns[36 * q + j] for q in range(4)])
            for n, s in enumerate((-2, -1, 0, 1, 2)):
                v = own + rwin[j + 2 * DMAX + s * d]
                if s == 0:
                    rx0[j] = v
                rs0[j, CH * n : CH * n + CH, :] = jnp.minimum(jnp.maximum(v, 0), caps[2 * n + 1])
        return 0

    lax.fori_loop(0, 52 // unroll, body, 0)


def phase_rim_x1(row0, band0, d, wf, bias, rx0, rs0, rx1, unroll=36):
    bias = jnp.broadcast_to(bias, (CH, 128))
    k = band0 + rim_lane()
    across = (k >= 0) & (k < KBAND)

    def body(it, _):
        for w in range(0, unroll, 2):
            j = it * unroll + w
            x = jnp.concatenate([taps(rs0, j + DMAX, d, 0, 128), taps(rs0, j + DMAX + 1, d, 0, 128)], axis=1)
            conv = jnp.dot(wf, x, preferred_element_type=f32)
            for z in range(2):
                row = row0 + 36 * lax.div(lanes(), 32) + (j + z - DMAX)
                v = rx0[j + z + DMAX].astype(f32) + conv[:, 128 * z : 128 * z + 128] + bias
                live = across & (row >= 0) & (k < NBINS - row)
                rx1[j + z] = jnp.where(live, jnp.maximum(v, 0.0), 0.0).astype(bf16)
        return 0

    lax.fori_loop(0, 36 // unroll, body, 0)


def phase_x1(row0, band0, d, dn, wf, bias, x0, s0, rx1, x1, s1):
    insides = inside_masks(dn)
    bias = jnp.broadcast_to(bias, (CH, 128))
    lane = lanes()

    def body(it, _):
        for w in range(0, 36, 2):
            j = it * 36 + w
            jj = j + DMAX
            x = jnp.concatenate([taps(s0, jj, d, 0, 128), taps(s0, jj + 1, d, 0, 128)], axis=1)
            conv = jnp.dot(wf, x, preferred_element_type=f32)
            for z in range(2):
                row = row0 + j + z - DMAX
                live = (row >= 0) & (band0 + lane < NBINS - row)
                a = x0[jj + z].astype(f32) + conv[:, 128 * z : 128 * z + 128] + bias
                a = jnp.where(live, a, 0.0).astype(bf16)
                x1[j + z] = a
                a = jnp.maximum(a, 0)
                s1[j + z, block_of(2), :] = a
                rim = rx1[w + z]
                for n, (m, s) in enumerate(SHIFTS):
                    side = pltpu.roll(rim, lax.rem(384 + 112 - 32 * it - s * dn, 128), 1)
                    s1[j + z, block_of(m), :] = jnp.where(insides[n], rolled(a, s, dn), side)
        return 0

    lax.fori_loop(0, 4, body, 0)


def phase_x2(row0, band0, d, wf, bias, x1, s1, out, unroll=16):
    bias = jnp.broadcast_to(bias, (CH, 128))

    def body(it, _):
        rows = []
        for w in range(0, unroll, 2):
            i = it * unroll + w
            j = i + DMAX
            x = jnp.concatenate([taps(s1, j, d, 0, 128), taps(s1, j + 1, d, 0, 128)], axis=1)
            conv = jnp.dot(wf, x, preferred_element_type=f32)
            for z in range(2):
                ma, _mb = row_masks(row0, band0, i + z)
                a = x1[j + z].astype(f32) + conv[:, 128 * z : 128 * z + 128] + bias
                rows.append(jnp.where(ma, a, 0.0).astype(bf16))
        out[:, pl.ds(pl.multiple_of(it * unroll, unroll), unroll), :] = jnp.swapaxes(jnp.stack(rows), 0, 1)
        return 0

    lax.fori_loop(0, TI // unroll, body, 0)


def phase_gw(h, s, soff, d, gw, gb, unroll=64):
    def body(it, carry):
        acc, accb = carry
        for w in range(0, unroll, 2):
            i = it * unroll + w
            x = jnp.concatenate(
                [taps(s, i + soff, d, 0, 128), taps(s, i + 1 + soff, d, 0, 128)], axis=1
            )
            ha, hb = h(i), h(i + 1)
            hh = jnp.concatenate([ha, hb], axis=1)
            acc = acc + lax.dot_general(hh, x, NT, preferred_element_type=f32)
            accb = accb + (ha.astype(f32) + hb.astype(f32))
        return acc, accb

    acc, accb = lax.fori_loop(
        0, TI // unroll, body, (jnp.zeros((CH, 9 * CH), f32), jnp.zeros((CH, 128), f32))
    )
    gw[...] = acc
    gb[...] = accb


def packed(rows):
    lane = lanes()
    left, right = rows[0], rows[7]
    for w in range(1, 8):
        left = jnp.where(lane < 16 * w, left, pltpu.roll(rows[w], 16 * w, 1))
    for w in range(6, -1, -1):
        right = jnp.where(lane >= 16 * (w + 1), right, pltpu.roll(rows[w], 16 * w + 16, 1))
    return left, right


SHIFTS = ((0, -2), (1, -1), (3, 1), (4, 2))


def block_of(n):
    return slice(CH * n, CH * n + CH)


def rolled(x, s, d):
    return pltpu.roll(x, lax.rem(256 - s * d, 128), 1)


def halo_sides(row0, band0, depth, group, rl, rr):
    lane = lanes()
    row = row0 + group * 8 - depth + lax.div(lane, 16)
    kr = band0 + 128 + lax.rem(lane, 16)
    kl = band0 - 16 + lax.rem(lane, 16)
    right = jnp.where((row >= 0) & (kr < KBAND) & (kr < NBINS - row), rl[group], 0)
    left = jnp.where((row >= 0) & (kl >= 0) & (kl < NBINS - row), rr[group], 0)
    return right, left


def side_of(right, left, w, s, d):
    if s > 0:
        return pltpu.roll(right, lax.rem(256 - 16 * w - s * d, 128), 1)
    return pltpu.roll(left, lax.rem(256 + 16 * (7 - w) - s * d, 128), 1)


def put_row(row0, band0, d, depth, j, a, dst):
    row = row0 + j - depth
    live = (row >= 0) & (band0 + lanes() < NBINS - row)
    a = jnp.where(live, a, 0)
    dst[j, block_of(2), :] = a
    for m, s in SHIFTS:
        dst[j, block_of(m), :] = rolled(a, s, d)


def patch_group(row0, band0, d, depth, group, insides, rl, rr, dst):
    right, left = halo_sides(row0, band0, depth, group, rl, rr)
    for w in range(8):
        j = group * 8 + w
        for n, (m, s) in enumerate(SHIFTS):
            dst[j, block_of(m), :] = jnp.where(
                insides[n], dst[j, block_of(m), :], side_of(right, left, w, s, d)
            )


def inside_masks(d):
    return [in_range(s, d) for _m, s in SHIFTS]


def phase_patch(row0, band0, d, depth, groups, rl, rr, dst, unroll):
    insides = inside_masks(d)

    def body(it, _):
        for g in range(unroll):
            patch_group(row0, band0, d, depth, it * unroll + g, insides, rl, rr, dst)
        return 0

    lax.fori_loop(0, groups // unroll, body, 0)


def phase_own_shifts(row0, band0, d, a, dst, unroll=32):
    def body(it, _):
        for w in range(unroll):
            j = 2 * DMAX + it * unroll + w
            put_row(row0, band0, d, 2 * DMAX, j, a[j], dst)
        return 0

    lax.fori_loop(0, TI // unroll, body, 0)


def phase_rim_shifts(row0, band0, d, a, dst):
    def body(it, _):
        for w in range(16):
            j = it * 144 + w
            put_row(row0, band0, d, 2 * DMAX, j, a[j], dst)
        return 0

    lax.fori_loop(0, 2, body, 0)


def phase_g1(d, dn, wb, x1, t1, t0, gpl, gpr, send_chunk, unroll=48):
    def body(it, _):
        rows = []
        for w in range(0, unroll, 2):
            j = it * unroll + w
            x = jnp.concatenate([taps(t1, j + DMAX, d, 0, 128), taps(t1, j + DMAX + 1, d, 0, 128)], axis=1)
            q = jnp.dot(wb, x, preferred_element_type=f32)
            for z in range(2):
                h = t1[j + DMAX + z, 64:96, :].astype(f32)
                gate = x1[j + z].astype(f32) > 0
                g = (h + jnp.where(gate, q[:, 128 * z : 128 * z + 128], 0.0)).astype(bf16)
                rows.append(g)
        for n in range(unroll // 8):
            left, right = packed(rows[8 * n : 8 * n + 8])
            gpl[it * (unroll // 8) + n] = left
            gpr[it * (unroll // 8) + n] = right
        send_chunk(it)
        for w, g in enumerate(rows):
            j = it * unroll + w
            t0[j, block_of(2), :] = g
            for m, s in SHIFTS:
                t0[j, block_of(m), :] = rolled(g, s, dn)
        return 0

    lax.fori_loop(0, H1 // unroll, body, 0)


def phase_g0(d, wb, s0, t0, begin, end, carry, unroll=32):
    lane = lanes()
    ones = jnp.ones((128, 128), bf16)

    def body(it, carry):
        rsum, lo, hi = carry
        rows = []
        for w in range(0, unroll, 2):
            i = it * unroll + w
            j = i + DMAX
            x = jnp.concatenate([taps(t0, j, d, 0, 128), taps(t0, j + 1, d, 0, 128)], axis=1)
            q = jnp.dot(wb, x, preferred_element_type=f32)
            for z in range(2):
                g1 = t0[j + z, 64:96, 0:128].astype(f32)
                gate = s0[j + z + DMAX, 64:96, 0:128].astype(f32) > 0
                gp = (g1 + jnp.where(gate, q[:, 128 * z : 128 * z + 128], 0.0)).astype(bf16)
                rows.append(gp)
                moved = pltpu.roll(gp, i + z, 1).astype(f32)
                low = jnp.where(lane >= i + z, moved, 0.0)
                lo = lo + low
                hi = hi + (moved - low)
        sums = jnp.dot(jnp.concatenate(rows, axis=0), ones, preferred_element_type=f32)
        for w in range(unroll):
            rsum = jnp.where(lane == it * unroll + w, sums[CH * w : CH * w + CH], rsum)
        return rsum, lo, hi

    return lax.fori_loop(begin // unroll, end // unroll, body, carry)
MESH = pl.DeviceIdType.MESH
NR, NO = 32, 8


def place_weights(w, wf, wb):
    row = lax.broadcasted_iota(jnp.int32, (CH, 9 * CH), 0)
    col = lax.broadcasted_iota(jnp.int32, (CH, 9 * CH), 1)
    for layer in range(2):
        fwd = jnp.zeros((CH, 9 * CH), f32)
        bwd = jnp.zeros((CH, 9 * CH), f32)
        for t in range(9):
            spot = jnp.where(col == row + CH * t, 1.0, 0.0).astype(bf16)
            fwd = fwd + jnp.dot(w[layer, t], spot, preferred_element_type=f32)
            bwd = bwd + lax.dot_general(
                w[layer, 8 - t], spot, (((0,), (0,)), ((), ())), preferred_element_type=f32
            )
        wf[layer] = fwd.astype(bf16)
        wb[layer] = bwd.astype(bf16)


def pack_grads(layer, gw, gb, pay):
    third = jnp.concatenate([gw[:, 256:288], jnp.sum(gb[...], axis=1, keepdims=True), jnp.zeros((CH, 95), f32)], axis=1)
    for og in range(4):
        rows = slice(8 * og, 8 * og + 8)
        for lt in range(2):
            pay[layer * 8 + og * 2 + lt, 0] = gw[rows, 128 * lt : 128 * lt + 128]
    return third


def unpack_grads(res, gw_out, gb_out):
    eye = lax.broadcasted_iota(jnp.int32, (CH, CH), 0) == lax.broadcasted_iota(jnp.int32, (CH, CH), 1)
    third = jnp.concatenate([res[og, 1] for og in range(4)], axis=0)
    for layer in range(2):
        for lt in range(2):
            tile = jnp.concatenate([res[layer * 8 + og * 2 + lt, 0] for og in range(4)], axis=0)
            for n in range(4):
                gw_out[layer, 4 * lt + n] = tile[:, CH * n : CH * n + CH]
        gw_out[layer, 8] = third[:, 64 * layer : 64 * layer + CH]
        column = third[:, 64 * layer + CH : 64 * layer + CH + 1]
        gb_out[layer : layer + 1, :] = jnp.sum(jnp.where(eye, column, 0.0), axis=0, keepdims=True)


def remote(src, dst, send, recv, target):
    return pltpu.make_async_remote_copy(
        src_ref=src, dst_ref=dst, send_sem=send, recv_sem=recv, device_id=target, device_id_type=MESH
    )


def wrap(r, o):
    return (lax.rem(r + 2 * NR, NR), lax.rem(o + NO, NO))


def halo_copies(r, o, a, pl_, pr_, rl, rr, send, recv):
    jobs = [
        (pl_, rl.at[2:18], 0, -1),
        (pr_, rr.at[2:18], 0, 1),
        (a.at[128:144], a.at[0:16], 1, 0),
        (a.at[16:32], a.at[144:160], -1, 0),
        (pl_.at[14:16], rl.at[0:2], 1, -1),
        (pl_.at[0:2], rl.at[18:20], -1, -1),
        (pr_.at[14:16], rr.at[0:2], 1, 1),
        (pr_.at[0:2], rr.at[18:20], -1, 1),
    ]
    return [
        remote(src, dst, send.at[n], recv.at[n], wrap(r + dr, o + do))
        for n, (src, dst, dr, do) in enumerate(jobs)
    ]


def embed_copies(r, o, emb, ec, er, send, recv):
    other = o + 1 - 2 * lax.rem(o, 2)
    copies = [
        remote(emb, ec.at[n], send.at[n - 1], recv.at[n - 1], wrap(r - other - (n - 2), other))
        for n in range(1, 5)
    ]
    copies.append(remote(emb, er.at[0], send.at[4], recv.at[4], wrap(r + 1, o)))
    copies.append(remote(emb, er.at[2], send.at[5], recv.at[5], wrap(r - 1, o)))
    return copies


def greet_exchange(r, o, barrier):
    other = o + 1 - 2 * lax.rem(o, 2)
    targets = [wrap(r + o + n - 2, other) for n in range(1, 5)]
    targets += [wrap(r + dr, o + do) for dr in (-1, 0, 1) for do in (-1, 0, 1) if (dr, do) != (0, 0)]
    for target in targets:
        pl.semaphore_signal(barrier, inc=1, device_id=target, device_id_type=MESH)
    return len(targets)


def lay_rows(cot, a, pl_, pr_):
    def body(it, _):
        block = jnp.swapaxes(cot[:, pl.ds(pl.multiple_of(it * 16, 16), 16), :], 0, 1)
        a[pl.ds(2 * DMAX + it * 16, 16)] = block
        for n in range(2):
            left, right = packed([block[8 * n + w] for w in range(8)])
            pl_[it * 2 + n] = left
            pr_[it * 2 + n] = right
        return 0

    lax.fori_loop(0, 8, body, 0)


def kernel(
    dil, emb_hbm, w_hbm, bias_hbm, cot_hbm, out_hbm, res_hbm, ge_hbm,
    res, ge,    emb, w, bias, cot, out, ec, er, a, rl, rr, pl_, pr_, grl, grr, gpl, gpr, x0, x1, s0, t1, s1, t0, wf, wb, gw, gb,
    pay, terms, wr1, w2, wr2, inbox, shares, win, caps, rwin, owns, rx0, rs0, rx1,
    io, esend, erecv, hsend, hrecv, gsend, grecv, sa, ra, sb, rb, sc, rc, st, rt, su, ru, local_sem,
):
    r, o = lax.axis_index("diag"), lax.axis_index("off")
    core, b = lax.rem(r, 2), lax.div(r, 2)
    me = o * 2 + core
    row0, band0 = r * TI, o * TK
    fetches = [
        pltpu.make_async_copy(src, dst, io.at[n])
        for n, (src, dst) in enumerate(((emb_hbm, emb), (w_hbm, w), (bias_hbm, bias), (cot_hbm, cot)))
    ]
    for c in fetches:
        c.start()

    def peer_a(n):
        other = lax.rem(me + n, 16)
        return other, (2 * b + lax.rem(other, 2), lax.div(other, 2))

    def peer_b(n):
        other = lax.rem(b + n, 16)
        return other, (2 * other + core, o)

    barrier = pltpu.get_barrier_semaphore()

    def greet(target):
        pl.semaphore_signal(barrier, inc=1, device_id=target, device_id_type=MESH)

    count = greet_exchange(r, o, barrier)
    for n in range(1, 16):
        greet(peer_a(n)[1])
        greet(peer_b(n)[1])
    greet(wrap(r - o - 1, o))

    @pl.when(o > 0)
    def _():
        greet(wrap(r - o, o))

    count = count + 30 + 1 + jnp.minimum(o, 1)
    ec[0] = jnp.zeros((CH, 128), bf16)
    ec[5] = jnp.zeros((CH, 128), bf16)
    d0, d1 = dil[0], dil[1]
    lane_caps(band0, d0, caps)
    for c in fetches:
        c.wait()
    er[1] = emb[...]
    place_weights(w, wf, wb)
    lay_rows(cot, a, pl_, pr_)
    pl.semaphore_wait(barrier, count)
    ecopies = embed_copies(r, o, emb, ec, er, esend, erecv)
    hcopies = halo_copies(r, o, a, pl_, pr_, rl, rr, hsend, hrecv)
    for c in ecopies + hcopies:
        c.start()

    eye = lax.broadcasted_iota(jnp.int32, (CH, CH), 0) == lax.broadcasted_iota(jnp.int32, (CH, CH), 1)

    def column(layer):
        return jnp.sum(jnp.where(eye, bias[layer : layer + 1, :], 0.0), axis=1, keepdims=True)

    phase_own_shifts(row0, band0, d1, a, t1)
    for c in ecopies:
        c.wait_recv()
    bounded_blocks(r, o, ec, er)
    phase_windows(ec, win)
    phase_rim_windows(win, rwin)
    phase_x0(d0, er, win, caps, x0, s0, owns)
    phase_rim_x0(d0, rwin, owns, caps, rx0, rs0)
    phase_rim_x1(row0, band0, d0, wf[0], column(0), rx0, rs0, rx1)
    phase_x1(row0, band0, d0, d1, wf[0], column(0), x0, s0, rx1, x1, s1)
    for c in hcopies[2:4]:
        c.wait_recv()
    phase_rim_shifts(row0, band0, d1, a, t1)
    for c in hcopies[:2] + hcopies[4:]:
        c.wait_recv()
    phase_patch(row0, band0, d1, 2 * DMAX, H2 // 8, rl, rr, t1, 5)

    def edge_copies(it):
        part = pl.ds(it * 6, 6)
        return (
            remote(gpl.at[part], grl.at[part], gsend.at[it], grecv.at[it], wrap(r, o - 1)),
            remote(gpr.at[part], grr.at[part], gsend.at[3 + it], grecv.at[3 + it], wrap(r, o + 1)),
        )

    def send_chunk(it):
        for c in edge_copies(it):
            c.start()

    phase_g1(d1, d0, wb[1], x1, t1, t0, gpl, gpr, send_chunk)
    gcopies = [c for n in range(3) for c in edge_copies(n)]
    phase_gw(lambda i: t1[i + 2 * DMAX, 64:96, :], s1, DMAX, d1, gw, gb)
    third1 = pack_grads(1, gw, gb, pay)
    phase_gw(lambda i: t0[i + DMAX, 64:96, :], s0, 2 * DMAX, d0, gw, gb)
    third0 = pack_grads(0, gw, gb, pay)
    rest = third0 + pltpu.roll(third1, 64, 1)
    for n in range(16):
        pay[n, 1] = rest[8 * n : 8 * n + 8] if n < 4 else jnp.zeros((8, 128), f32)

    first = [remote(pay.at[other], wr1.at[me], sa.at[n], ra.at[me], target)
             for n in range(1, 16) for other, target in [peer_a(n)]]
    for c in first:
        c.start()

    for c in gcopies:
        c.wait_recv()
    phase_patch(row0, band0, d0, DMAX, H1 // 8, grl, grr, t0, 6)

    def arrived(dst, sem):
        pltpu.make_async_copy(dst, dst, sem).wait()

    def total(buf):
        acc = buf[0]
        for n in range(1, 16):
            acc = acc + buf[n]
        return acc

    zero = jnp.zeros((CH, TI), f32)
    sums = phase_g0(d0, wb[0], s0, t0, 0, 64, (zero, zero, zero))
    wr1[me] = pay[me]
    for n in range(1, 16):
        other, _t = peer_a(n)
        arrived(wr1.at[other], ra.at[other])
    w2[...] = total(wr1)
    second = [remote(w2, wr2.at[b], sb.at[n], rb.at[b], target)
              for n in range(1, 16) for other, target in [peer_b(n)]]
    for c in second:
        c.start()

    rsum, lo, hi = phase_g0(d0, wb[0], s0, t0, 64, 128, sums)
    terms[0] = lo
    terms[1] = hi
    low = remote(terms.at[0], inbox.at[0], st.at[0], rt.at[0], wrap(r + o, o))
    high = remote(terms.at[1], inbox.at[1], st.at[1], rt.at[1], wrap(r + o + 1, o))
    high.start()
    local = pltpu.make_async_copy(terms.at[0], inbox.at[0], local_sem)

    @pl.when(o > 0)
    def _():
        low.start()

    @pl.when(o == 0)
    def _():
        local.start()

    phase_x2(row0, band0, d1, wf[1], column(1), x1, s1, out, 64)
    write = pltpu.make_async_copy(out, out_hbm, io.at[4])
    write.start()

    @pl.when(o > 0)
    def _():
        low.wait_recv()

    @pl.when(o == 0)
    def _():
        local.wait()

    high.wait_recv()
    shares[o] = rsum + inbox[0] + inbox[1]
    eall = [remote(shares.at[o], shares.at[o], su.at[n], ru.at[o], wrap(r, o + n)) for n in range(1, 8)]
    for c in eall:
        c.start()

    wr2[b] = w2[...]
    for n in range(1, 16):
        other, _t = peer_b(n)
        arrived(wr2.at[other], rb.at[other])
    res[me] = total(wr2)
    third = [remote(res.at[me], res.at[me], sc.at[n], rc.at[me], target)
             for n in range(1, 16) for other, target in [peer_a(n)]]
    for c in third:
        c.start()
    for c in ecopies + hcopies + gcopies + first + second + [high]:
        c.wait_send()

    @pl.when(o > 0)
    def _():
        low.wait_send()

    for n in range(1, 8):
        oo = lax.rem(o + n, 8)
        arrived(shares.at[oo], ru.at[oo])
    acc = shares[0]
    for n in range(1, 8):
        acc = acc + shares[n]
    ge[...] = acc
    write_ge = pltpu.make_async_copy(ge, ge_hbm, io.at[5])
    write_ge.start()
    for n in range(1, 16):
        other, _t = peer_a(n)
        arrived(res.at[other], rc.at[other])
    write_res = pltpu.make_async_copy(res, res_hbm, io.at[6])
    write_res.start()
    for c in third + eall:
        c.wait_send()

    for c in (write, write_ge, write_res):
        c.wait()


def finish(section, res, ge, out, gw_out, gb_out, ge_out, held, rv, gv, gwv, gbv, come, go):
    size = CH // 4
    parts = [slice(n * size, n * size + size) for n in range(4)]
    ins = [pltpu.make_async_copy(section.at[p], held.at[p], come.at[n]) for n, p in enumerate(parts)]
    outs = [pltpu.make_async_copy(held.at[p], out.at[p], go.at[n]) for n, p in enumerate(parts)]
    res_in = pltpu.make_async_copy(res, rv, come.at[4])
    ge_in = pltpu.make_async_copy(ge, gv, come.at[5])
    for c in [res_in, ge_in] + ins:
        c.start()
    small = [
        pltpu.make_async_copy(src, dst, go.at[4 + n])
        for n, (src, dst) in enumerate(((gwv, gw_out), (gbv, gb_out), (gv, ge_out)))
    ]
    res_in.wait()
    unpack_grads(rv, gwv, gbv)
    ge_in.wait()
    for c in small:
        c.start()
    for n in range(4):
        ins[n].wait()
        outs[n].start()
    for c in outs + small:
        c.wait()


def per_device(bin_embed, weights, biases, dilations, cotangent):
    vmem = pl.BlockSpec(memory_space=pltpu.VMEM)
    smem = pl.BlockSpec(memory_space=pltpu.SMEM)
    hbm = pl.BlockSpec(memory_space=pl.ANY)
    shape = jax.ShapeDtypeStruct
    dma = pltpu.SemaphoreType.DMA
    mem = pltpu.VMEM
    halo = [mem((H2, CH, 128), bf16), mem((20, CH, 128), bf16), mem((20, CH, 128), bf16),
            mem((16, CH, 128), bf16), mem((16, CH, 128), bf16)]
    edge = [mem((18, CH, 128), bf16)] * 4
    section, res, ge = pl.pallas_call(
        kernel,
        out_shape=[shape((CH, TI, TK), bf16), shape((16, 2, 8, 128), f32), shape((CH, TI), f32)],
        in_specs=[smem, hbm, hbm, hbm, hbm],
        out_specs=[hbm, hbm, hbm],
        scratch_shapes=[
            mem((16, 2, 8, 128), f32), mem((CH, TI), f32),
            mem((CH, TI), bf16), mem((2, 9, CH, CH), bf16), mem((2, CH), f32),
            mem((CH, TI, TK), bf16), mem((CH, TI, TK), bf16),
            mem((6, CH, 128), bf16), mem((3, CH, 128), bf16), *halo, *edge,
            mem((H2, CH, 128), bf16), mem((H1, CH, 128), bf16),
            mem((H2, 5 * CH, 128), bf16), mem((H2, 5 * CH, 128), bf16),
            mem((H1, 5 * CH, 128), bf16), mem((H1, 5 * CH, 128), bf16),
            mem((2, CH, 9 * CH), bf16), mem((2, CH, 9 * CH), bf16),
            mem((CH, 9 * CH), f32), mem((CH, 128), f32),
            mem((16, 2, 8, 128), f32), mem((2, CH, TI), f32),
            mem((16, 2, 8, 128), f32), mem((2, 8, 128), f32),
            mem((16, 2, 8, 128), f32), mem((2, CH, TI), f32), mem((8, CH, TI), f32),
            mem((H2 + 4 * DMAX, CH, 256), bf16), mem((10, CH, 128), bf16),
            mem((84, CH, 128), bf16), mem((H2, CH, 128), bf16), mem((52, CH, 128), bf16),
            mem((52, 5 * CH, 128), bf16), mem((36, CH, 128), bf16),
            dma((7,)), dma((6,)), dma((6,)), dma((8,)), dma((8,)), dma((6,)), dma((6,)),
            dma((16,)), dma((16,)), dma((16,)), dma((16,)), dma((16,)), dma((16,)),
            dma((2,)), dma((2,)), dma((8,)), dma((8,)), dma,
        ],
        compiler_params=pltpu.CompilerParams(collective_id=0, has_side_effects=True, vmem_limit_bytes=60 << 20),
        name="section",
    )(dilations, bin_embed, weights, biases, cotangent)
    out, gw, gb, ge_out = pl.pallas_call(
        finish,
        out_shape=[shape((CH, TI, TK), bf16), shape((2, 9, CH, CH), f32), shape((2, CH), f32), shape((CH, TI), f32)],
        in_specs=[hbm] * 3,
        out_specs=[hbm] * 4,
        scratch_shapes=[mem((CH, TI, TK), bf16), mem((16, 2, 8, 128), f32), mem((CH, TI), f32),
                        mem((2, 9, CH, CH), f32), mem((2, CH), f32), dma((6,)), dma((7,))],
        name="finish",
    )(section, res, ge)
    return out, gw, gb, ge_out


def solution(mesh):
    placed = (P(None, "diag"), P(), P(), P(), P(None, "diag", "off"))
    return jax.shard_map(
        per_device,
        mesh=mesh,
        in_specs=placed,
        out_specs=(P(None, "diag", "off"), P(), P(), P(None, "diag")),
        check_vma=False,
    )
```
